32 devices in a mesh: dp: 4 (over z), head: 2 (over x), seq: 4 (over y, core).
Axes of the slice: x: 2, y: 2, z: 4, core: 2. Of those that a mesh axis runs over, the one named last changes fastest.
Arguments:
- tokens: int32 [12288], P(('dp', 'head', 'seq')), may hold values from 0 to 8191
- segments: int32 [12288], P(('dp', 'head', 'seq')), may hold values from 0 to 24, as said below
- live_lengths: int32 [4, 25], P('dp'), may hold values from 1 to 3072, as said below
- timesteps: int32 [4, 25], P('dp'), may hold values from 0 to 1999
- table: bfloat16 [8192, 128], P('seq')
- input_weight: bfloat16 [128, 768], replicated, may hold values from -6 to 6
- time_first: bfloat16 [128, 768], replicated, may hold values from -0.5 to 0.5
- time_second: bfloat16 [768, 768], replicated, may hold values from -0.21875 to 0.21875
- first_gain: float32 [768], replicated, may hold values from 0.25 to 1.75
- first_shift: float32 [768], replicated, may hold values from -1.75 to 1.75
- query_weight: bfloat16 [768, 768], replicated, may hold values from -0.21875 to 0.21875
- key_weight: bfloat16 [768, 768], replicated, may hold values from -0.21875 to 0.21875
- value_weight: bfloat16 [768, 768], replicated, may hold values from -0.21875 to 0.21875
- output_weight: bfloat16 [768, 768], replicated, may hold values from -4 to 4
- second_gain: float32 [768], replicated, may hold values from 0.25 to 1.75
- second_shift: float32 [768], replicated, may hold values from -1.75 to 1.75
- up_weight: bfloat16 [768, 3072], replicated, may hold values from -0.21875 to 0.21875
- down_weight: bfloat16 [3072, 768], replicated, may hold values from -0.109375 to 0.109375
- upstream: bfloat16 [12288, 768], P(('dp', 'head', 'seq')), may hold values from -6 to 6
Outputs:
- activation: bfloat16 [12288, 768], P(('dp', 'head', 'seq'))
- embed_grad: float32 [12288, 128], P(('dp', 'head', 'seq'))
- table_grad: float32 [8192, 128], P('seq')
- input_grad: float32 [128, 768], P('dp')
- time_first_grad: float32 [128, 768], P('dp')
- time_second_grad: float32 [768, 768], P('dp')
- first_gain_grad: float32 [768], replicated
- first_shift_grad: float32 [768], replicated
- query_grad: float32 [768, 768], P('dp')
- key_grad: float32 [768, 768], P('dp')
- value_grad: float32 [768, 768], P('dp')
- output_grad: float32 [768, 768], P('dp')
- second_gain_grad: float32 [768], replicated
- second_shift_grad: float32 [768], replicated
- up_grad: float32 [768, 3072], P('dp')
- down_grad: float32 [3072, 768], P('dp')
The draws below stay inside these ranges and needn't reach their ends.
Inputs may be any that keep to these rules, and one draw needn't show every extreme that they name: Within each group of 3072 tokens (one index of dp) segments start at 0 and never fall; every slot with tokens holds 64 tokens except one that holds 1536 tokens or more, up to the whole group; slots of a group may be left without tokens. `live_lengths`: the live tokens of each slot are its first ones; the rest are padding. The slot holding the long item is live in full.
All inputs are finite; a program needn't handle non-finite values.
Results may differ from the reference program's by a relative error of at most 0.019.
Values may be sent and summed in bfloat16 or wider, within the bound.
A program may use at most 192 MiB of HBM per device.

```python
import math
import jax
import jax.numpy as jnp
import numpy as np
from jax import lax

D = 768
HEADS = 12
HEAD_DIM = 64
FF = 3072
EMB = 128
TFEAT = 128
VOCAB = 8192
SHORT = 64
GROUP = 3072
GROUPS = 4
TOKENS = 12288
SEGS = 25


def plan_layout(key):
    count_key, pick_key, place_key = jax.random.split(key, 3)
    most = SEGS - 1
    shorts = jax.random.randint(count_key, (GROUPS,), 0, most + 1)
    chosen = jax.random.randint(pick_key, (), 0, GROUPS)
    unsplit = (chosen + 1) % GROUPS
    group_index = jnp.arange(GROUPS)
    shorts = jnp.where(group_index == chosen, most, shorts)
    shorts = jnp.where(group_index == unsplit, 0, shorts)
    place = jax.random.randint(place_key, (GROUPS,), 0, shorts + 1)
    long_len = GROUP - shorts * SHORT
    return (place, long_len)


def draw_segments(key, part):
    place, long_len = plan_layout(key)
    index = jnp.arange(GROUP, dtype=jnp.int32)[None, :]
    begin = (place * SHORT)[:, None]
    finish = begin + long_len[:, None]
    after = place[:, None] + 1 + (index - finish) // SHORT
    slots = jnp.where(index < begin, index // SHORT, jnp.where(index < finish, place[:, None], after))
    return slots.reshape(-1).astype(jnp.int32)


def draw_live_lengths(key, part):
    place, long_len = plan_layout(key)
    key = jax.random.fold_in(key, 7)
    slot = jnp.arange(SEGS, dtype=jnp.int32)[None, :]
    is_long = slot == place[:, None]
    sizes = jnp.where(is_long, long_len[:, None], SHORT)
    cuts = jax.random.randint(key, (GROUPS, SEGS), 0, SHORT // 4 + 1)
    cuts = jnp.where(is_long, 0, cuts)
    return (sizes - cuts).astype(jnp.int32)


def draw_table(key, part):
    key = jax.random.fold_in(key, 11)
    base_key, row_key, column_key = jax.random.split(key, 3)
    place = jnp.arange(VOCAB, dtype=jnp.float32) / (VOCAB - 1)
    base = jax.random.normal(base_key, (VOCAB, EMB), jnp.float32)
    trend = 1.0 + 2.0 * place
    row_scale = jnp.exp(jax.random.uniform(row_key, (VOCAB,), jnp.float32, 0.0, math.log(10.0)))
    column_scale = jnp.exp(jax.random.uniform(column_key, (EMB,), jnp.float32, 0.0, math.log(10.0)))
    return (0.1 * base * (trend * row_scale)[:, None] * column_scale[None, :]).astype(jnp.bfloat16)


def plant(values, stream_key, least, largest):
    extent = values.shape
    index_at = [jax.random.randint(jax.random.fold_in(stream_key, axis), (), 0, extent[axis]) for axis in range(len(extent))]
    values = values.at[tuple(index_at)].set(least)
    longest = extent.index(max(extent))
    index_at[longest] = (index_at[longest] + 1) % extent[longest]
    return values.at[tuple(index_at)].set(largest)


def level_of(rng, shape, pieces, smallest, largest):
    loudness = 1.0
    for position, blocks in pieces:
        draws = jax.random.uniform(jax.random.fold_in(jax.random.fold_in(rng, 6), position), (blocks,), jnp.float32, smallest / len(pieces), largest / len(pieces))
        loudness = loudness * jnp.repeat(jnp.exp(draws), shape[position] // blocks).reshape((-1,) + (1,) * (len(shape) - 1 - position))
    return loudness


def rank_bounds(number_of, lean):
    portions = [(1 << 20) // math.isqrt(rank ** lean) + 1 for rank in range(1, number_of + 1)]
    deviation = 1 + sum(portions) // (1 << 30)
    return np.cumsum(np.array([max(1, weight // deviation) for weight in portions]))


def ranked_ids(key, dims, count, lean):
    grid = rank_bounds(count, lean)
    pick = jax.random.randint(jax.random.fold_in(key, 1), dims, 0, int(grid[count - 1]))
    rank = jnp.searchsorted(jnp.asarray(grid, jnp.int32), pick, side="right")
    return jax.random.permutation(jax.random.fold_in(key, 2), count)[rank].astype(jnp.int32)


def normal_values(key, extent, deviation, most, cuts=(), held_as=jnp.bfloat16):
    entries = jax.random.normal(key, extent, jnp.float32) * deviation
    if len(cuts) > 0:
        entries = level_of(key, extent, cuts, -0.22, 0.18) * entries
    return jnp.clip(entries, min=-most, max=most).astype(held_as)


def setup_inputs(seed: int = 0) -> dict:
    streams_of = jax.random.split(jax.random.key(seed), 20)
    return {
        "tokens": plant(ranked_ids(streams_of[0], (TOKENS,), VOCAB, 2), jax.random.fold_in(streams_of[0], 3), 0, VOCAB - 1).astype(jnp.int32),
        "segments": draw_segments(jax.random.fold_in(streams_of[19], 71), 0),
        "live_lengths": draw_live_lengths(jax.random.fold_in(streams_of[19], 71), 0),
        "timesteps": plant(jax.random.randint(streams_of[3], (GROUPS, SEGS), 0, 2000), jax.random.fold_in(streams_of[3], 1), 0, 1999).astype(jnp.int32),
        "table": draw_table(jax.random.fold_in(streams_of[19], 71), 0),
        "input_weight": normal_values(streams_of[5], (EMB, D), 1 ** -0.5, 6.0),
        "time_first": normal_values(streams_of[6], (TFEAT, D), TFEAT ** -0.5, 0.5),
        "time_second": normal_values(streams_of[7], (D, D), D ** -0.5, 0.21875),
        "first_gain": jnp.clip(1.0 + 0.15 * jax.random.normal(streams_of[8], (D,), jnp.float32), 0.25, 1.75),
        "first_shift": normal_values(streams_of[9], (D,), 0.3, 1.75, (), jnp.float32),
        "query_weight": normal_values(streams_of[10], (D, D), D ** -0.5, 0.21875),
        "key_weight": normal_values(streams_of[11], (D, D), D ** -0.5, 0.21875),
        "value_weight": normal_values(streams_of[12], (D, D), D ** -0.5, 0.21875),
        "output_weight": normal_values(streams_of[13], (D, D), 2 ** -0.5, 4.0),
        "second_gain": jnp.clip(1.0 + 0.15 * jax.random.normal(streams_of[14], (D,), jnp.float32), 0.25, 1.75),
        "second_shift": normal_values(streams_of[15], (D,), 0.3, 1.75, (), jnp.float32),
        "up_weight": normal_values(streams_of[16], (D, FF), D ** -0.5, 0.21875),
        "down_weight": normal_values(streams_of[17], (FF, D), FF ** -0.5, 0.109375),
        "upstream": normal_values(streams_of[18], (TOKENS, D), 1.0, 6.0, ((0, 32),)),
    }


@jax.custom_vjp
def low(v):
    return lax.optimization_barrier(v.astype(jnp.bfloat16)).astype(jnp.float32)

@jax.custom_vjp
def low_back(v):
    return v

def low_keep(v):
    return (low(v), None)

def low_pass(kept, grad):
    return (grad,)

def back_keep(v):
    return (v, None)

def back_low(kept, grad):
    return (low(grad),)
low.defvjp(low_keep, low_pass)
low_back.defvjp(back_keep, back_low)
EPSILON = 1e-05
MASKED = -1e+30
HIGHEST = lax.Precision.HIGHEST

def layer_norm(values, gain, shift):
    centre = values - lax.optimization_barrier(jnp.mean(values, axis=-1, keepdims=True))
    spread = lax.optimization_barrier(jnp.mean(centre * centre, axis=-1, keepdims=True))
    return centre * lax.rsqrt(spread + EPSILON) * gain + shift

def product(left, right):
    return jnp.dot(left, right, precision=HIGHEST)

def time_features(steps, width):
    half = width // 2
    freqs = jnp.exp(-math.log(10000.0) * jnp.arange(half, dtype=jnp.float32) / half)
    angles = steps.astype(jnp.float32)[..., None] * freqs
    return jnp.concatenate([jnp.cos(angles), jnp.sin(angles)], axis=-1)

def group_mask(slot_ids, lengths_row):
    hits = slot_ids[:, None] == jnp.arange(SEGS, dtype=jnp.int32)[None, :]
    counts = lax.optimization_barrier(jnp.sum(hits.astype(jnp.int32), axis=0)).astype(jnp.int32)
    starts = (jnp.cumsum(counts) - counts).astype(jnp.int32)
    first = lax.optimization_barrier(jnp.sum(jnp.where(hits, starts[None, :], 0), axis=1)).astype(jnp.int32)
    limit = lax.optimization_barrier(jnp.sum(jnp.where(hits, lengths_row[None, :], 0), axis=1)).astype(jnp.int32)
    live = jnp.arange(GROUP, dtype=jnp.int32) - first < limit
    return (slot_ids[:, None] == slot_ids[None, :]) & live[None, :]

def reference(tokens, segments, live_lengths, timesteps, table, input_weight, time_first, time_second, first_gain, first_shift, query_weight, key_weight, value_weight, output_weight, second_gain, second_shift, up_weight, down_weight, upstream):
    scale = HEAD_DIM ** (-0.5)
    group_of = (jnp.arange(TOKENS, dtype=jnp.int32) // GROUP).astype(jnp.int32)
    features = time_features(timesteps, TFEAT)
    slot_groups = segments.reshape(GROUPS, GROUP)

    def forward(table_f, input_f, first_f, second_f, gain_one, shift_one, query_f, key_f, value_f, output_f, gain_two, shift_two, up_f, down_f, probe):
        norms = jnp.sqrt(lax.optimization_barrier(jnp.sum(table_f * table_f, axis=1)))
        mean_norm = jnp.mean(norms)
        embedded = jnp.take(table_f, tokens, axis=0) / mean_norm + probe
        time_hidden = jnp.einsum('gsf,fd->gsd', features, first_f, precision=HIGHEST)
        time_out = jnp.einsum('gsf,fd->gsd', jax.nn.silu(time_hidden), second_f, precision=HIGHEST)
        slot_rows = (group_of * SEGS + segments).astype(jnp.int32)
        time_vec = jnp.take(time_out.reshape(GROUPS * SEGS, D), slot_rows, axis=0)
        stream = low_back(product(low(embedded), input_f)) + time_vec

        def block(carry, part):
            stream_part, slot_ids, lengths_row = part
            keep = group_mask(slot_ids, lengths_row)
            normed = low(layer_norm(stream_part, gain_one, shift_one))
            query = low(low_back(product(normed, query_f)))
            keys = low(low_back(product(normed, key_f)))
            values = low(low_back(product(normed, value_f)))

            def one_head(trio):
                query_head, key_head, value_head = trio
                raw = low_back(product(query_head, key_head.T) * scale)
                probs = jax.nn.softmax(jnp.where(keep, raw, MASKED), axis=-1)
                return product(low(probs), value_head)
            split = lambda arr: arr.reshape(GROUP, HEADS, HEAD_DIM).transpose(1, 0, 2)
            heads_out = lax.map(jax.checkpoint(one_head), (split(query), split(keys), split(values)))
            attended = heads_out.transpose(1, 0, 2).reshape(GROUP, D)
            mixed = low(low_back(attended))
            middle = stream_part + low_back(product(mixed, output_f))
            normed_two = low(layer_norm(middle, gain_two, shift_two))
            hidden = low(jax.nn.gelu(low_back(product(normed_two, up_f)), approximate=False))
            return (carry, middle + low_back(product(hidden, down_f)))
        _, outputs = lax.scan(jax.checkpoint(block), jnp.zeros((), jnp.float32), (stream.reshape(GROUPS, GROUP, D), slot_groups, live_lengths))
        return outputs.reshape(TOKENS, D)
    result, pullback = jax.vjp(forward, table.astype(jnp.float32), input_weight.astype(jnp.float32), time_first.astype(jnp.float32), time_second.astype(jnp.float32), first_gain, first_shift, query_weight.astype(jnp.float32), key_weight.astype(jnp.float32), value_weight.astype(jnp.float32), output_weight.astype(jnp.float32), second_gain, second_shift, up_weight.astype(jnp.float32), down_weight.astype(jnp.float32), jnp.zeros((TOKENS, EMB), jnp.float32))
    grads = pullback(upstream.astype(jnp.float32))
    return (result.astype(jnp.bfloat16), grads[14], grads[0], grads[1], grads[2], grads[3], grads[4], grads[5], grads[6], grads[7], grads[8], grads[9], grads[10], grads[11], grads[12], grads[13])
```

```python
import functools
import math

import jax
import jax.numpy as jnp
from jax import lax
from jax.experimental import pallas as pl
from jax.experimental.pallas import tpu as pltpu
from jax.sharding import PartitionSpec as P

HEADS = 12
HEAD_DIM = 64
VOCAB = 8192
EPSILON = 1e-05
MASKED = -1e30
LOG2E = math.log2(math.e)
LN2 = math.log(2.0)
KEY_BLOCK = 512
SLOTS = 32
DEAD = 25
ONES = 32
VMEM_LIMIT = 60 * 2**20

F32 = jnp.float32
BF16 = jnp.bfloat16


def dot(left, right, left_dim=1, right_dim=0):
    return lax.dot_general(
        left, right, (((left_dim,), (right_dim,)), ((), ())), preferred_element_type=F32
    )


def contract_exact(left, right):
    return lax.dot_general(left, right, (((0,), (0,)), ((), ())), precision=lax.Precision.HIGHEST)


def whole(shape):
    return pl.BlockSpec(shape, lambda *_: (0,) * len(shape))


def params(**more):
    return pltpu.CompilerParams(vmem_limit_bytes=VMEM_LIMIT, **more)


def norm_parts(values):
    centre = values - jnp.mean(values, axis=-1, keepdims=True)
    spread = jnp.mean(centre * centre, axis=-1, keepdims=True)
    scale = lax.rsqrt(spread + EPSILON)
    return centre * scale, scale


def norm_back(incoming, gain, unit, scale):
    scaled = incoming * gain
    inner = scaled - jnp.mean(scaled, axis=-1, keepdims=True)
    return scale * (inner - unit * jnp.mean(scaled * unit, axis=-1, keepdims=True))


def embed_kernel(
    own,
    tokens,
    slots,
    all_slots,
    lengths,
    mean_norm,
    table,
    entry,
    gain,
    shift,
    query_weight,
    key_weight,
    value_weight,
    normed_out,
    key_out,
    value_out,
    mark_out,
    stream_out,
    query_out,
    low_out,
    picked,
    limits,
):
    step = pl.program_id(0)
    blocks = pl.num_programs(0)
    rows = picked.shape[0]
    block = lax.rem(own[0] + step, blocks)
    base = block * rows

    @pl.when(step == 0)
    def _():
        lanes = lax.broadcasted_iota(jnp.int32, (all_slots.shape[0], 128), 1)
        below = jnp.where(all_slots[...] < lanes, 1.0, 0.0)
        limits[...] = jnp.sum(below, axis=0, keepdims=True) + lengths[...]

    def pick(index, carry):
        for inner in range(8):
            row = index * 8 + inner
            picked[pl.ds(row, 1), :] = table[pl.ds(tokens[base + row], 1), :]
        return carry

    lax.fori_loop(0, rows // 8, pick, 0)
    low = (picked[...] / mean_norm[0]).astype(BF16)
    lanes = lax.broadcasted_iota(jnp.int32, (rows, 128), 1)
    slot = slots[...]
    same = jnp.where((lanes & (SLOTS - 1)) == slot, 1.0, 0.0)
    spread = jnp.where(lanes < 3 * SLOTS, same, 0.0).astype(BF16)
    stream = dot(jnp.concatenate([low, spread], axis=1), entry[...])
    unit, _ = norm_parts(stream)
    normed = (unit * gain[...] + shift[...]).astype(BF16)
    normed_out[...] = normed
    key_out[...] = dot(normed, key_weight[...]).astype(BF16)
    value_out[...] = dot(normed, value_weight[...]).astype(BF16)
    first = jnp.where(lanes < SLOTS, same, 0.0)
    limit = jnp.sum(first * limits[...], axis=1, keepdims=True)
    index = (base + lax.broadcasted_iota(jnp.int32, (rows, 1), 0)).astype(F32)
    dead = jnp.where(index < limit, 0.0, 1.0)
    marks = jnp.where(lanes == DEAD, dead, first)
    marks = jnp.where((lanes >= ONES) & (lanes < ONES + 2), 1.0, marks)
    mark_out[...] = marks.astype(BF16)

    @pl.when(step == 0)
    def _():
        stream_out[...] = stream
        low_out[...] = low
        query = dot(query_weight[...], normed, 0, 1) * (LOG2E / math.sqrt(HEAD_DIM))
        query_out[...] = query.astype(BF16)


def embed(own, tokens, slots, lengths, mean_norm, table, entry, gain, shift, wq, wk, wv, blocks):
    group = tokens.shape[0]
    rows = group // blocks
    width = wq.shape[0]
    turn = lambda step, own, tokens: (lax.rem(own[0] + step, blocks), 0)
    return pl.pallas_call(
        embed_kernel,
        grid_spec=pltpu.PrefetchScalarGridSpec(
            num_scalar_prefetch=2,
            grid=(blocks,),
            in_specs=[
                pl.BlockSpec((rows, 1), turn),
                whole((group, 1)),
                whole((1, 128)),
                pl.BlockSpec(memory_space=pltpu.SMEM),
                whole(table.shape),
                whole(entry.shape),
                whole((1, width)),
                whole((1, width)),
                whole((width, width)),
                whole((width, width)),
                whole((width, width)),
            ],
            out_specs=[
                pl.BlockSpec((rows, width), turn),
                pl.BlockSpec((rows, width), turn),
                pl.BlockSpec((rows, width), turn),
                pl.BlockSpec((rows, 128), turn),
                whole((rows, width)),
                whole((width, rows)),
                whole((rows, 128)),
            ],
            scratch_shapes=[pltpu.VMEM((rows, 128), F32), pltpu.VMEM((1, 128), F32)],
        ),
        out_shape=[
            jax.ShapeDtypeStruct((group, width), BF16),
            jax.ShapeDtypeStruct((group, width), BF16),
            jax.ShapeDtypeStruct((group, width), BF16),
            jax.ShapeDtypeStruct((group, 128), BF16),
            jax.ShapeDtypeStruct((rows, width), F32),
            jax.ShapeDtypeStruct((width, rows), BF16),
            jax.ShapeDtypeStruct((rows, 128), BF16),
        ],
        compiler_params=params(),
        name="embed",
    )(own, tokens, slots, slots, lengths, mean_norm, table, entry, gain, shift, wq, wk, wv)


def pair_columns(target, pair, rows):
    target[0:HEAD_DIM, 0:rows] = pair[0:HEAD_DIM]
    target[0:HEAD_DIM, rows : 2 * rows] = jnp.zeros((HEAD_DIM, rows), BF16)
    target[HEAD_DIM : 2 * HEAD_DIM, 0:rows] = jnp.zeros((HEAD_DIM, rows), BF16)
    target[HEAD_DIM : 2 * HEAD_DIM, rows : 2 * rows] = pair[HEAD_DIM : 2 * HEAD_DIM]


def forward_kernel(query, keys, values, marks, slots, probs_out, mixed_out, inverse_out, right, scores):
    rows = query.shape[1]
    group = keys.shape[0]
    blocks = group // KEY_BLOCK
    pair_columns(right, query, rows)
    kinds = lax.broadcasted_iota(jnp.int32, (128, rows), 0)
    away = jnp.where((kinds < DEAD) & (kinds != slots[...]), MASKED, 0.0)
    away = jnp.where(kinds == DEAD, MASKED, away).astype(BF16)
    right[128:256, 0:rows] = away
    right[128:256, rows : 2 * rows] = away

    def score(index, top):
        part = pl.ds(pl.multiple_of(index * KEY_BLOCK, KEY_BLOCK), KEY_BLOCK)
        left = jnp.concatenate([keys[part, :], marks[part, :]], axis=1)
        current = dot(left, right[...])
        scores[part, :] = current
        return jnp.maximum(top, jnp.max(current.reshape(KEY_BLOCK // 8, 8, 2 * rows), axis=0))

    top = lax.fori_loop(0, blocks, score, jnp.full((8, 2 * rows), MASKED, F32))
    top = jnp.max(top, axis=0, keepdims=True)
    ones = jnp.ones((16, KEY_BLOCK), BF16)

    def weigh(index, total):
        part = pl.ds(pl.multiple_of(index * KEY_BLOCK, KEY_BLOCK), KEY_BLOCK)
        probs = jnp.exp2(scores[part, :] - top).astype(BF16)
        probs_out[part, :] = probs
        left = jnp.concatenate([values[part, :].T, ones], axis=0)
        return total + dot(left, probs)

    total = lax.fori_loop(0, blocks, weigh, jnp.zeros((144, 2 * rows), F32))
    inverse = 1.0 / total[128:129]
    mixed_out[0:HEAD_DIM] = total[0:HEAD_DIM, 0:rows] * inverse[:, 0:rows]
    mixed_out[HEAD_DIM:128] = total[HEAD_DIM:128, rows : 2 * rows] * inverse[:, rows : 2 * rows]
    inverse_out[0, 0:1] = inverse[:, 0:rows]
    inverse_out[0, 1:2] = inverse[:, rows : 2 * rows]


def attend(query, keys, values, marks, slots):
    width, rows = query.shape
    group = keys.shape[0]
    pairs = width // 128
    column = pl.BlockSpec((group, 128), lambda pair: (0, pair))
    return pl.pallas_call(
        forward_kernel,
        grid=(pairs,),
        in_specs=[
            pl.BlockSpec((128, rows), lambda pair: (pair, 0)),
            column,
            column,
            whole((group, 128)),
            whole((1, rows)),
        ],
        out_specs=[
            pl.BlockSpec((group, 2 * rows), lambda pair: (0, pair)),
            pl.BlockSpec((128, rows), lambda pair: (pair, 0)),
            pl.BlockSpec((1, 2, rows), lambda pair: (pair, 0, 0)),
        ],
        out_shape=[
            jax.ShapeDtypeStruct((group, pairs * 2 * rows), BF16),
            jax.ShapeDtypeStruct((width, rows), F32),
            jax.ShapeDtypeStruct((pairs, 2, rows), F32),
        ],
        scratch_shapes=[pltpu.VMEM((256, 2 * rows), BF16), pltpu.VMEM((group, 2 * rows), F32)],
        compiler_params=params(),
        name="attend",
    )(query, keys, values, marks, slots)


def feed_kernel(
    mixed_wide,
    inverse,
    stream,
    upstream,
    gain,
    shift,
    output_hbm,
    up_hbm,
    down_hbm,
    activation_out,
    middle_grad_out,
    norm_out,
    mixed_grad_out,
    row_out,
    output_grad_hbm,
    up_grad_hbm,
    down_grad_hbm,
    output_weight,
    up_weight,
    down_weight,
    output_grad,
    up_grad,
    down_grad,
    loads,
    stores,
):
    rows, width = stream.shape
    hidden_width = up_weight.shape[1]
    chunk = 512
    chunks = hidden_width // chunk
    load_output = pltpu.make_async_copy(output_hbm, output_weight, loads.at[0])
    load_up = pltpu.make_async_copy(up_hbm, up_weight, loads.at[1])
    load_down = pltpu.make_async_copy(down_hbm, down_weight, loads.at[2])
    load_output.start()
    load_up.start()
    load_down.start()
    mixed = mixed_wide[...].astype(BF16)
    load_output.wait()
    middle = stream[...] + dot(mixed, output_weight[...], 0, 0)
    unit, scale = norm_parts(middle)
    normed = (unit * gain[...] + shift[...]).astype(BF16)
    normed_t = normed.T
    load_up.wait()
    load_down.wait()
    incoming = upstream[...]
    activation = middle
    normed_grad = jnp.zeros((rows, width), F32)
    for index in range(chunks):
        part = slice(index * chunk, (index + 1) * chunk)
        pre = dot(normed, up_weight[:, part])
        cdf = 0.5 * (1.0 + lax.erf(pre * math.sqrt(0.5)))
        slope = cdf + pre * jnp.exp(-0.5 * pre * pre) * (1.0 / math.sqrt(2.0 * math.pi))
        hidden = (pre * cdf).astype(BF16)
        back = dot(incoming, down_weight[part, :], 1, 1)
        pre_grad = (back * slope).astype(BF16)
        activation = activation + dot(hidden, down_weight[part, :])
        down_grad[part, :] = dot(hidden, incoming, 0, 0).astype(BF16)
        up_grad[:, part] = dot(normed_t, pre_grad).astype(BF16)
        normed_grad = normed_grad + dot(pre_grad, up_weight[:, part], 1, 1)
    store_up = pltpu.make_async_copy(up_grad, up_grad_hbm, stores.at[1])
    store_down = pltpu.make_async_copy(down_grad, down_grad_hbm, stores.at[2])
    store_up.start()
    store_down.start()
    activation_out[...] = activation.astype(BF16)
    norm_out[0:1] = jnp.sum(normed_grad * unit, axis=0, keepdims=True)
    norm_out[1:2] = jnp.sum(normed_grad, axis=0, keepdims=True)
    middle_grad = incoming.astype(F32) + norm_back(normed_grad, gain[...], unit, scale)
    middle_grad_out[...] = middle_grad
    middle_low = middle_grad.astype(BF16)
    output_grad[...] = dot(mixed, middle_low).astype(BF16)
    store_output = pltpu.make_async_copy(output_grad, output_grad_hbm, stores.at[0])
    store_output.start()
    mixed_grad = dot(output_weight[...], middle_low, 1, 1).astype(BF16).astype(F32)
    for head in range(HEADS):
        part = slice(head * HEAD_DIM, (head + 1) * HEAD_DIM)
        factor = inverse[head : head + 1]
        mixed_grad_out[part, :] = (mixed_grad[part] * factor).astype(BF16)
        row_out[head : head + 1] = factor * jnp.sum(
            mixed_grad[part] * mixed_wide[part, :], axis=0, keepdims=True
        )
    store_up.wait()
    store_down.wait()
    store_output.wait()


def feed(mixed, inverse, stream, upstream, gain, shift, output_weight, up_weight, down_weight):
    rows, width = stream.shape
    hidden_width = up_weight.shape[1]
    vmem = pl.BlockSpec(memory_space=pltpu.VMEM)
    hbm = pl.BlockSpec(memory_space=pltpu.HBM)
    return pl.pallas_call(
        feed_kernel,
        in_specs=[vmem] * 6 + [hbm] * 3,
        out_specs=[vmem] * 5 + [hbm] * 3,
        out_shape=[
            jax.ShapeDtypeStruct((rows, width), BF16),
            jax.ShapeDtypeStruct((rows, width), F32),
            jax.ShapeDtypeStruct((2, width), F32),
            jax.ShapeDtypeStruct((width, rows), BF16),
            jax.ShapeDtypeStruct((HEADS, rows), F32),
            jax.ShapeDtypeStruct((width, width), BF16),
            jax.ShapeDtypeStruct((width, hidden_width), BF16),
            jax.ShapeDtypeStruct((hidden_width, width), BF16),
        ],
        scratch_shapes=[
            pltpu.VMEM((width, width), BF16),
            pltpu.VMEM((width, hidden_width), BF16),
            pltpu.VMEM((hidden_width, width), BF16),
            pltpu.VMEM((width, width), BF16),
            pltpu.VMEM((width, hidden_width), BF16),
            pltpu.VMEM((hidden_width, width), BF16),
            pltpu.SemaphoreType.DMA((3,)),
            pltpu.SemaphoreType.DMA((3,)),
        ],
        compiler_params=params(),
        name="feed",
    )(mixed, inverse, stream, upstream, gain, shift, output_weight, up_weight, down_weight)


def back_kernel(query, keys, values, marks, probs, mixed_grad, row_sums, query_out, key_out, value_out, left, right):
    rows = query.shape[1]
    group = keys.shape[0]
    blocks = group // KEY_BLOCK
    pair_columns(left, query, rows)
    pair_columns(right, mixed_grad, rows)
    kinds = lax.broadcasted_iota(jnp.int32, (128, rows), 0)
    for half in range(2):
        total = -row_sums[0, half : half + 1]
        high = total.astype(BF16)
        rest = (total - high.astype(F32)).astype(BF16)
        shape = (128, rows)
        fill = jnp.where(kinds == ONES, jnp.broadcast_to(high.astype(F32), shape), 0.0)
        fill = jnp.where(kinds == ONES + 1, jnp.broadcast_to(rest.astype(F32), shape), fill)
        right[128:256, half * rows : (half + 1) * rows] = fill.astype(BF16)

    def step(index, total):
        part = pl.ds(pl.multiple_of(index * KEY_BLOCK, KEY_BLOCK), KEY_BLOCK)
        weights = probs[part, :]
        inner = dot(jnp.concatenate([values[part, :], marks[part, :]], axis=1), right[...])
        score_grad = (weights.astype(F32) * inner).astype(BF16)
        key_out[part, :] = (dot(score_grad, left[...], 1, 1) * LN2).astype(BF16)
        value_out[part, :] = dot(weights, right[0:128, :], 1, 1).astype(BF16)
        return total + dot(keys[part, :].T, score_grad)

    total = lax.fori_loop(0, blocks, step, jnp.zeros((128, 2 * rows), F32))
    scale = HEAD_DIM**-0.5
    query_out[0:HEAD_DIM] = (total[0:HEAD_DIM, 0:rows] * scale).astype(BF16)
    query_out[HEAD_DIM:128] = (total[HEAD_DIM:128, rows : 2 * rows] * scale).astype(BF16)


def attend_back(query, keys, values, marks, probs, mixed_grad, row_sums):
    width, rows = query.shape
    group = keys.shape[0]
    pairs = width // 128
    column = pl.BlockSpec((group, 128), lambda pair: (0, pair))
    row = pl.BlockSpec((128, rows), lambda pair: (pair, 0))
    return pl.pallas_call(
        back_kernel,
        grid=(pairs,),
        in_specs=[
            row,
            column,
            column,
            whole((group, 128)),
            pl.BlockSpec((group, 2 * rows), lambda pair: (0, pair)),
            row,
            pl.BlockSpec((1, 2, rows), lambda pair: (pair, 0, 0)),
        ],
        out_specs=[row, column, column],
        out_shape=[
            jax.ShapeDtypeStruct((width, rows), BF16),
            jax.ShapeDtypeStruct((group, width), BF16),
            jax.ShapeDtypeStruct((group, width), BF16),
        ],
        scratch_shapes=[pltpu.VMEM((128, 2 * rows), BF16), pltpu.VMEM((256, 2 * rows), BF16)],
        compiler_params=params(),
        name="attend_back",
    )(query, keys, values, marks, probs, mixed_grad, row_sums)


def time_features(steps, width):
    half = width // 2
    freqs = jnp.exp(-math.log(10000.0) * jnp.arange(half, dtype=F32) / half)
    angles = steps.astype(F32)[:, None] * freqs[None, :]
    return jnp.concatenate([jnp.cos(angles), jnp.sin(angles)], axis=1)


def split_three(values):
    high = values.astype(BF16)
    rest = values - high.astype(F32)
    middle = rest.astype(BF16)
    return high, middle, (rest - middle.astype(F32)).astype(BF16)


def body(
    tokens,
    segments,
    live_lengths,
    timesteps,
    table,
    input_weight,
    time_first,
    time_second,
    first_gain,
    first_shift,
    query_weight,
    key_weight,
    value_weight,
    output_weight,
    second_gain,
    second_shift,
    up_weight,
    down_weight,
    upstream,
):
    head_count = lax.axis_size("head")
    seq_count = lax.axis_size("seq")
    blocks = head_count * seq_count
    rows = tokens.shape[0]
    width = query_weight.shape[0]
    shard_rows = table.shape[0]
    slot_count = live_lengths.shape[1]
    highest = lax.Precision.HIGHEST
    seq_index = lax.axis_index("seq")
    own = lax.axis_index("head") * seq_count + seq_index

    all_tokens, all_slots = (
        lax.all_gather(tokens, ("head", "seq"), axis=0, tiled=True),
        lax.all_gather(segments, ("head", "seq"), axis=0, tiled=True),
    )
    full_table = lax.all_gather(table, "seq", axis=0, tiled=True).astype(F32)
    mean_norm = jnp.sum(jnp.sqrt(jnp.sum(full_table * full_table, axis=1))) / VOCAB
    features = time_features(timesteps[0], time_first.shape[0])
    second_wide = time_second.astype(F32)
    time_hidden = jnp.dot(features, time_first.astype(F32), precision=highest)
    time_act = jax.nn.silu(time_hidden)
    time_out = jnp.dot(time_act, second_wide, precision=highest)
    time_rows = jnp.pad(time_out, ((0, SLOTS - slot_count), (0, 0)))
    entry = jnp.concatenate(
        [input_weight, *split_three(time_rows), jnp.zeros((SLOTS, width), BF16)], axis=0
    )
    lengths = jnp.pad(live_lengths.astype(F32), ((0, 0), (0, 128 - slot_count)))
    normed, keys, values, marks, stream, query, embed_low = embed(
        own[None],
        all_tokens,
        all_slots[:, None],
        lengths,
        mean_norm[None],
        full_table,
        entry,
        first_gain[None],
        first_shift[None],
        query_weight,
        key_weight,
        value_weight,
        blocks,
    )
    probs, mixed, inverse = attend(query, keys, values, marks, segments[None])
    activation, middle_grad, second_norm, mixed_grad, row_sums, output_grad, up_grad, down_grad = feed(
        mixed,
        inverse.reshape(HEADS, rows),
        stream,
        upstream,
        second_gain[None],
        second_shift[None],
        output_weight,
        up_weight,
        down_weight,
    )
    query_back, key_back, value_back = attend_back(
        query, keys, values, marks, probs, mixed_grad, row_sums.reshape(HEADS // 2, 2, rows)
    )
    own_normed = lax.dynamic_slice_in_dim(normed, own * rows, rows)
    query_grad = dot(own_normed, query_back, 0, 1)
    key_grad = dot(normed, key_back, 0, 0)
    value_grad = dot(normed, value_back, 0, 0)
    partial = dot(key_back, key_weight, 1, 1) + dot(value_back, value_weight, 1, 1)
    normed_grad = lax.psum_scatter(
        partial.astype(BF16), ("head", "seq"), scatter_dimension=0, tiled=True
    ).astype(F32) + dot(query_back, query_weight, 0, 1)

    def one_norm(values, gain, shift):
        unit, _ = norm_parts(values)
        return unit * gain + shift

    _, first_back = jax.vjp(one_norm, stream, first_gain, first_shift)
    stream_part, first_gain_grad, first_shift_grad = first_back(normed_grad)
    stream_grad = middle_grad + stream_part
    stream_low = stream_grad.astype(BF16)
    input_grad = dot(embed_low, stream_low, 0, 0)
    embed_grad = dot(stream_low, input_weight, 1, 1)
    picker = (segments[:, None] == jnp.arange(slot_count, dtype=jnp.int32)[None, :]).astype(F32)
    time_out_grad = contract_exact(picker, stream_grad)
    time_second_grad = contract_exact(time_act, time_out_grad)
    act_grad = lax.dot_general(
        time_out_grad, second_wide, (((1,), (1,)), ((), ())), precision=highest
    )
    _, silu_back = jax.vjp(jax.nn.silu, time_hidden)
    time_hidden_grad = silu_back(act_grad)[0]
    time_first_grad = contract_exact(features, time_hidden_grad)

    def reduce(value):
        part = lax.psum_scatter(value.astype(BF16), "dp", scatter_dimension=0, tiled=True)
        return lax.psum(part, ("head", "seq")).astype(F32)

    shards = [
        reduce(value)
        for value in (
            input_grad,
            time_first_grad,
            time_second_grad,
            query_grad,
            key_grad,
            value_grad,
            output_grad,
            up_grad,
            down_grad,
        )
    ]
    found = jnp.take(full_table, tokens, axis=0)
    mean_part = -jnp.sum(embed_grad * found) / (mean_norm * mean_norm)
    scaled_grad = embed_grad / mean_norm
    table_sum = jax.ops.segment_sum(scaled_grad, tokens, num_segments=VOCAB)
    small = lax.psum(
        (first_gain_grad, first_shift_grad, second_norm[0], second_norm[1], mean_part, table_sum),
        ("dp", "head", "seq"),
    )
    table_rows = lax.dynamic_slice_in_dim(small[5], seq_index * shard_rows, shard_rows)
    table_wide = table.astype(F32)
    row_norms = jnp.sqrt(jnp.sum(table_wide * table_wide, axis=1))
    table_grad = table_rows + small[4] / VOCAB * table_wide / row_norms[:, None]
    return (
        activation,
        embed_grad,
        table_grad,
        shards[0],
        shards[1],
        shards[2],
        small[0],
        small[1],
        shards[3],
        shards[4],
        shards[5],
        shards[6],
        small[2],
        small[3],
        shards[7],
        shards[8],
    )


def solution(mesh):
    tokens = P(("dp", "head", "seq"))
    wide = P(("dp", "head", "seq"), None)
    group = P("dp", None)
    return jax.shard_map(
        body,
        mesh=mesh,
        in_specs=(tokens, tokens, group, group, P("seq", None)) + (P(),) * 13 + (wide,),
        out_specs=(wide, wide, P("seq", None), group, group, group, P(), P())
        + (group,) * 4
        + (P(), P(), group, group),
        check_vma=False,
    )
```

```python
import functools
import math

import jax
import jax.numpy as jnp
from jax import lax
from jax.experimental import pallas as pl
from jax.experimental.pallas import tpu as pltpu
from jax.sharding import PartitionSpec as P

HEADS = 12
HEAD_DIM = 64
VOCAB = 8192
EPSILON = 1e-05
MASKED = -1e30
LOG2E = math.log2(math.e)
LN2 = math.log(2.0)
KEY_BLOCK = 512
SLOTS = 32
DEAD = 25
ONES = 32
VMEM_LIMIT = 60 * 2**20
PIECE = 96
UNIT = (2, 2, 2, 4, PIECE, 768)
MESH = pl.DeviceIdType.MESH

F32 = jnp.float32
BF16 = jnp.bfloat16


def dot(left, right, left_dim=1, right_dim=0):
    return lax.dot_general(
        left, right, (((left_dim,), (right_dim,)), ((), ())), preferred_element_type=F32
    )


def contract_exact(left, right):
    return lax.dot_general(left, right, (((0,), (0,)), ((), ())), precision=lax.Precision.HIGHEST)


def whole(shape):
    return pl.BlockSpec(shape, lambda *_: (0,) * len(shape))


def params(**more):
    return pltpu.CompilerParams(vmem_limit_bytes=VMEM_LIMIT, **more)


def norm_parts(values):
    centre = values - jnp.mean(values, axis=-1, keepdims=True)
    spread = jnp.mean(centre * centre, axis=-1, keepdims=True)
    scale = lax.rsqrt(spread + EPSILON)
    return centre * scale, scale


def norm_back(incoming, gain, unit, scale):
    scaled = incoming * gain
    inner = scaled - jnp.mean(scaled, axis=-1, keepdims=True)
    return scale * (inner - unit * jnp.mean(scaled * unit, axis=-1, keepdims=True))


def place():
    seq = lax.axis_index("seq")
    return lax.axis_index("dp"), lax.axis_index("head"), lax.div(seq, 2), lax.rem(seq, 2)


def device(z, x, y, c):
    return (z, x, y * 2 + c)


def neighbours():
    z, x, y, c = place()
    planes = lax.axis_size("dp")
    near = [device(z, x, y, 1 - c), device(z, 1 - x, y, c), device(z, x, 1 - y, c)]
    return near, [device(lax.rem(z + step, planes), x, y, c) for step in range(1, planes)]


def greet(devices):
    barrier = pltpu.get_barrier_semaphore()
    for other in devices:
        pl.semaphore_signal(barrier, inc=1, device_id=other, device_id_type=MESH)
    pl.semaphore_wait(barrier, len(devices))


def send(source, target, sems, slot, other):
    return pltpu.make_async_remote_copy(
        src_ref=source,
        dst_ref=target,
        send_sem=sems[0].at[slot],
        recv_sem=sems[1].at[slot],
        device_id=other,
        device_id_type=MESH,
    )


def gather_kernel(table, notes, full, notes_all, steps_all, mean_out, sums, local, *sems):
    z, x, y, c = place()
    seq = y * 2 + c
    own = x * 4 + seq
    near, planes = neighbours()
    others = []
    for flip in range(1, 8):
        xx, yy, cc = flip // 4, (flip // 2) % 2, flip % 2
        others.append(device(z, x + xx - 2 * xx * x, y + yy - 2 * yy * y, c + cc - 2 * cc * c))
    greet(others + planes)
    keep = pltpu.make_async_copy(table, full.at[seq], local.at[0])
    keep.start()
    tables = [
        send(table, full.at[seq], sems, 0, near[2]),
        send(table, full.at[seq], sems, 1, near[0]),
    ]
    for copy in tables:
        copy.start()
    notes_all[own] = notes[...]
    steps_all[z] = notes[...]
    copies = [
        send(notes, notes_all.at[own], sems, 3 + index, other) for index, other in enumerate(others)
    ]
    copies += [
        send(notes, steps_all.at[z], sems, 13 + index, other) for index, other in enumerate(planes)
    ]
    for copy in copies:
        copy.start()
    wide = table[...].astype(F32)
    norms = jnp.sqrt(jnp.sum(wide * wide, axis=1, keepdims=True))
    total = jnp.sum(norms, axis=0, keepdims=True)
    sums[seq] = jnp.broadcast_to(total, (8, 128))
    partials = [
        send(sums.at[seq], sums.at[seq], sems, 10 + index, other)
        for index, other in enumerate((near[0], near[2], device(z, x, 1 - y, 1 - c)))
    ]
    for copy in partials:
        copy.start()
    tables[0].wait_recv()
    away = (1 - y) * 2 + c
    forward = send(full.at[away], full.at[away], sems, 2, near[0])
    forward.start()
    keep.wait()
    for copy in copies + partials:
        copy.wait()
    mean_out[...] = jnp.sum(sums[...], axis=0) * (1.0 / VOCAB)
    tables[1].wait_recv()
    forward.wait()
    for copy in tables:
        copy.wait_send()


def gather(table, notes):
    rows, width = table.shape
    planes = lax.axis_size("dp")
    vmem = pl.BlockSpec(memory_space=pltpu.VMEM)
    hbm = pl.BlockSpec(memory_space=pltpu.HBM)
    slots = 13 + planes - 1
    return pl.pallas_call(
        gather_kernel,
        in_specs=[vmem, vmem],
        out_specs=[hbm, vmem, vmem, vmem],
        out_shape=[
            jax.ShapeDtypeStruct((4, rows, width), BF16),
            jax.ShapeDtypeStruct((8, 8, 128), jnp.int32),
            jax.ShapeDtypeStruct((planes, 8, 128), jnp.int32),
            jax.ShapeDtypeStruct((8, 128), F32),
        ],
        scratch_shapes=[
            pltpu.VMEM((4, 8, 128), F32),
            pltpu.SemaphoreType.DMA((1,)),
            pltpu.SemaphoreType.DMA((slots,)),
            pltpu.SemaphoreType.DMA((slots,)),
        ],
        compiler_params=params(collective_id=0, has_side_effects=True),
        name="gather",
    )(table, notes)


def column_of(row):
    size = row.shape[1]
    shape = (size, size)
    same = lax.broadcasted_iota(jnp.int32, shape, 0) == lax.broadcasted_iota(jnp.int32, shape, 1)
    return jnp.sum(jnp.where(same, jnp.broadcast_to(row, shape), 0.0), axis=1, keepdims=True)


def embed_kernel(
    own,
    tokens,
    notes,
    lengths,
    mean_norm,
    table_low,
    entry,
    gain,
    shift,
    query_weight,
    key_weight,
    value_weight,
    normed_out,
    key_out,
    value_out,
    mark_out,
    stream_out,
    query_out,
    low_out,
    found_out,
    picked,
    limits,
    table,
):
    step = pl.program_id(0)
    blocks = pl.num_programs(0)
    rows = picked.shape[0]
    width = stream_out.shape[1]
    block = lax.rem(own[0] + step, blocks)
    base = block * rows

    @pl.when(step == 0)
    def _():
        kinds = lax.broadcasted_iota(jnp.int32, (128, 128), 0)
        below = jnp.zeros((128, 128), F32)
        for part in range(blocks if isinstance(blocks, int) else 8):
            for line in range(3, 6):
                below = below + jnp.where(notes[part, line : line + 1, :] < kinds, 1.0, 0.0)
        starts = jnp.sum(below, axis=1, keepdims=True)
        shape = (128, 128)
        same = lax.broadcasted_iota(jnp.int32, shape, 0) == lax.broadcasted_iota(jnp.int32, shape, 1)
        starts = jnp.sum(jnp.where(same, jnp.broadcast_to(starts, shape), 0.0), axis=0, keepdims=True)
        limits[...] = starts + lengths[...]
        for part in range(4):
            table[part * 2048 : (part + 1) * 2048, :] = table_low[part].astype(F32)

    for line in range(3):

        def pick(index, carry):
            for inner in range(8):
                row = index * 8 + inner
                picked[pl.ds(line * 128 + row, 1), :] = table[pl.ds(tokens[block, line, row], 1), :]
            return carry

        lax.fori_loop(0, 16, pick, 0)
    low = (picked[...] / mean_norm[0:1]).astype(BF16)
    lanes = lax.broadcasted_iota(jnp.int32, (rows, 128), 1)
    slot = jnp.concatenate(
        [column_of(notes[block, line : line + 1, :].astype(F32)) for line in range(3, 6)], axis=0
    )
    same = jnp.where((lanes & (SLOTS - 1)).astype(F32) == slot, 1.0, 0.0)
    spread = jnp.where(lanes < 3 * SLOTS, same, 0.0).astype(BF16)
    stream = dot(jnp.concatenate([low, spread], axis=1), entry[...])
    unit, _ = norm_parts(stream)
    normed = (unit * gain[...].reshape(1, width) + shift[...].reshape(1, width)).astype(BF16)
    normed_out[...] = normed.T
    key_out[...] = dot(normed, key_weight[...]).astype(BF16)
    value_out[...] = dot(normed, value_weight[...]).astype(BF16)
    first = jnp.where(lanes < SLOTS, same, 0.0)
    limit = jnp.sum(first * limits[...], axis=1, keepdims=True)
    index = (base + lax.broadcasted_iota(jnp.int32, (rows, 1), 0)).astype(F32)
    dead = jnp.where(index < limit, 0.0, 1.0)
    marks = jnp.where(lanes == DEAD, dead, first)
    marks = jnp.where((lanes >= ONES) & (lanes < ONES + 2), 1.0, marks)
    mark_out[...] = marks.astype(BF16)

    @pl.when(step == 0)
    def _():
        stream_out[...] = stream
        low_out[...] = low
        found_out[...] = picked[...].astype(BF16)
        query = dot(query_weight[...], normed, 0, 1) * (LOG2E / math.sqrt(HEAD_DIM))
        query_out[...] = query.astype(BF16)


def embed(own, notes, lengths, mean_norm, table, entry, gain, shift, wq, wk, wv, rows, blocks):
    group = rows * blocks
    width = wq.shape[0]
    turn = lambda step, own: (lax.rem(own[0] + step, blocks), 0)
    return pl.pallas_call(
        embed_kernel,
        grid_spec=pltpu.PrefetchScalarGridSpec(
            num_scalar_prefetch=1,
            grid=(blocks,),
            in_specs=[
                pl.BlockSpec(memory_space=pltpu.SMEM),
                whole(notes.shape),
                whole((1, 128)),
                whole((8, 128)),
                whole(table.shape),
                whole(entry.shape),
                whole((width,)),
                whole((width,)),
                whole((width, width)),
                whole((width, width)),
                whole((width, width)),
            ],
            out_specs=[
                pl.BlockSpec((width, rows), lambda *args: turn(*args)[::-1]),
                pl.BlockSpec((rows, width), turn),
                pl.BlockSpec((rows, width), turn),
                pl.BlockSpec((rows, 128), turn),
                whole((rows, width)),
                whole((width, rows)),
                whole((rows, 128)),
                whole((rows, 128)),
            ],
            scratch_shapes=[
                pltpu.VMEM((rows, 128), F32),
                pltpu.VMEM((1, 128), F32),
                pltpu.VMEM((VOCAB, 128), F32),
            ],
        ),
        out_shape=[
            jax.ShapeDtypeStruct((width, group), BF16),
            jax.ShapeDtypeStruct((group, width), BF16),
            jax.ShapeDtypeStruct((group, width), BF16),
            jax.ShapeDtypeStruct((group, 128), BF16),
            jax.ShapeDtypeStruct((rows, width), F32),
            jax.ShapeDtypeStruct((width, rows), BF16),
            jax.ShapeDtypeStruct((rows, 128), BF16),
            jax.ShapeDtypeStruct((rows, 128), BF16),
        ],
        compiler_params=params(),
        name="embed",
    )(own, notes, notes, lengths, mean_norm, table, entry, gain, shift, wq, wk, wv)


def pair_columns(target, pair, rows):
    target[0:HEAD_DIM, 0:rows] = pair[0:HEAD_DIM]
    target[0:HEAD_DIM, rows : 2 * rows] = jnp.zeros((HEAD_DIM, rows), BF16)
    target[HEAD_DIM : 2 * HEAD_DIM, 0:rows] = jnp.zeros((HEAD_DIM, rows), BF16)
    target[HEAD_DIM : 2 * HEAD_DIM, rows : 2 * rows] = pair[HEAD_DIM : 2 * HEAD_DIM]


def forward_kernel(query, keys, values, marks, slots, probs_out, mixed_out, inverse_out, right, scores):
    rows = query.shape[1]
    group = keys.shape[0]
    blocks = group // KEY_BLOCK
    pair_columns(right, query, rows)
    kinds = lax.broadcasted_iota(jnp.int32, (128, rows), 0)
    away = jnp.where((kinds < DEAD) & (kinds != slots[...]), MASKED, 0.0)
    away = jnp.where(kinds == DEAD, MASKED, away).astype(BF16)
    right[128:256, 0:rows] = away
    right[128:256, rows : 2 * rows] = away

    def score(index, top):
        part = pl.ds(pl.multiple_of(index * KEY_BLOCK, KEY_BLOCK), KEY_BLOCK)
        left = jnp.concatenate([keys[part, :], marks[part, :]], axis=1)
        current = dot(left, right[...])
        scores[part, :] = current
        return jnp.maximum(top, jnp.max(current.reshape(KEY_BLOCK // 8, 8, 2 * rows), axis=0))

    top = lax.fori_loop(0, blocks, score, jnp.full((8, 2 * rows), MASKED, F32))
    top = jnp.max(top, axis=0, keepdims=True)
    ones = jnp.ones((16, KEY_BLOCK), BF16)

    def weigh(index, total):
        part = pl.ds(pl.multiple_of(index * KEY_BLOCK, KEY_BLOCK), KEY_BLOCK)
        probs = jnp.exp2(scores[part, :] - top).astype(BF16)
        probs_out[part, :] = probs
        left = jnp.concatenate([values[part, :].T, ones], axis=0)
        return total + dot(left, probs)

    total = lax.fori_loop(0, blocks, weigh, jnp.zeros((144, 2 * rows), F32))
    inverse = 1.0 / total[128:129]
    mixed_out[0:HEAD_DIM] = total[0:HEAD_DIM, 0:rows] * inverse[:, 0:rows]
    mixed_out[HEAD_DIM:128] = total[HEAD_DIM:128, rows : 2 * rows] * inverse[:, rows : 2 * rows]
    inverse_out[0, 0:1] = inverse[:, 0:rows]
    inverse_out[0, 1:2] = inverse[:, rows : 2 * rows]


def attend(query, keys, values, marks, slots):
    width, rows = query.shape
    group = keys.shape[0]
    pairs = width // 128
    column = pl.BlockSpec((group, 128), lambda pair: (0, pair))
    return pl.pallas_call(
        forward_kernel,
        grid=(pairs,),
        in_specs=[
            pl.BlockSpec((128, rows), lambda pair: (pair, 0)),
            column,
            column,
            whole((group, 128)),
            whole((1, rows)),
        ],
        out_specs=[
            pl.BlockSpec((group, 2 * rows), lambda pair: (0, pair)),
            pl.BlockSpec((128, rows), lambda pair: (pair, 0)),
            pl.BlockSpec((1, 2, rows), lambda pair: (pair, 0, 0)),
        ],
        out_shape=[
            jax.ShapeDtypeStruct((group, pairs * 2 * rows), BF16),
            jax.ShapeDtypeStruct((width, rows), F32),
            jax.ShapeDtypeStruct((pairs, 2, rows), F32),
        ],
        scratch_shapes=[pltpu.VMEM((256, 2 * rows), BF16), pltpu.VMEM((group, 2 * rows), F32)],
        compiler_params=params(),
        name="attend",
    )(query, keys, values, marks, slots)


def feed_kernel(
    mixed_wide,
    inverse,
    stream,
    upstream,
    gain,
    shift,
    output_hbm,
    up_hbm,
    down_hbm,
    activation_out,
    middle_grad_out,
    norm_out,
    mixed_grad_out,
    row_out,
    output_grad_hbm,
    up_grad_hbm,
    down_grad_hbm,
    output_weight,
    up_weight,
    down_weight,
    output_grad,
    up_grad,
    down_grad,
    loads,
    stores,
):
    rows, width = stream.shape
    hidden_width = up_weight.shape[1]
    chunk = width
    chunks = hidden_width // chunk
    load_output = pltpu.make_async_copy(output_hbm, output_weight, loads.at[0])
    load_up = pltpu.make_async_copy(up_hbm, up_weight, loads.at[1])
    load_down = pltpu.make_async_copy(down_hbm, down_weight, loads.at[2])
    load_output.start()
    load_up.start()
    load_down.start()
    mixed = mixed_wide[...].astype(BF16)
    load_output.wait()
    middle = stream[...] + dot(mixed, output_weight[...], 0, 0)
    unit, scale = norm_parts(middle)
    wide_gain = gain[...].reshape(1, width)
    normed = (unit * wide_gain + shift[...].reshape(1, width)).astype(BF16)
    normed_t = normed.T
    load_up.wait()
    load_down.wait()
    incoming = upstream[...]
    activation = middle
    normed_grad = jnp.zeros((rows, width), F32)
    for index in range(chunks):
        part = slice(index * chunk, (index + 1) * chunk)
        pre = dot(normed, up_weight[:, part])
        cdf = 0.5 * (1.0 + lax.erf(pre * math.sqrt(0.5)))
        slope = cdf + pre * jnp.exp(-0.5 * pre * pre) * (1.0 / math.sqrt(2.0 * math.pi))
        hidden = (pre * cdf).astype(BF16)
        back = dot(incoming, down_weight[part, :], 1, 1)
        pre_grad = (back * slope).astype(BF16)
        activation = activation + dot(hidden, down_weight[part, :])
        down_grad[:, :, :, index] = (
            dot(hidden, incoming, 0, 0).astype(BF16).reshape(2, 2, 2, PIECE, width)
        )
        up_part = dot(normed_t, pre_grad).astype(BF16).reshape(4, 2, PIECE, width)
        for half in range(2):
            up_grad[index // 2, index % 2, half] = up_part[:, half]
        normed_grad = normed_grad + dot(pre_grad, up_weight[:, part], 1, 1)
    store_up = pltpu.make_async_copy(up_grad, up_grad_hbm, stores.at[1])
    store_down = pltpu.make_async_copy(down_grad, down_grad_hbm, stores.at[2])
    store_up.start()
    store_down.start()
    activation_out[...] = activation.astype(BF16)
    norm_out[0:1] = jnp.sum(normed_grad * unit, axis=0, keepdims=True)
    norm_out[1:2] = jnp.sum(normed_grad, axis=0, keepdims=True)
    middle_grad = incoming.astype(F32) + norm_back(normed_grad, wide_gain, unit, scale)
    middle_grad_out[...] = middle_grad
    middle_low = middle_grad.astype(BF16)
    output_part = dot(mixed, middle_low).astype(BF16).reshape(4, 2, PIECE, width)
    for half in range(2):
        output_grad[half] = output_part[:, half]
    store_output = pltpu.make_async_copy(output_grad, output_grad_hbm, stores.at[0])
    store_output.start()
    mixed_grad = dot(output_weight[...], middle_low, 1, 1).astype(BF16).astype(F32)
    for head in range(HEADS):
        part = slice(head * HEAD_DIM, (head + 1) * HEAD_DIM)
        factor = inverse[head : head + 1]
        mixed_grad_out[part, :] = (mixed_grad[part] * factor).astype(BF16)
        row_out[head : head + 1] = factor * jnp.sum(
            mixed_grad[part] * mixed_wide[part, :], axis=0, keepdims=True
        )
    store_up.wait()
    store_down.wait()
    store_output.wait()


def feed(mixed, inverse, stream, upstream, gain, shift, output_weight, up_weight, down_weight):
    rows, width = stream.shape
    hidden_width = up_weight.shape[1]
    vmem = pl.BlockSpec(memory_space=pltpu.VMEM)
    hbm = pl.BlockSpec(memory_space=pltpu.HBM)
    return pl.pallas_call(
        feed_kernel,
        in_specs=[vmem] * 6 + [hbm] * 3,
        out_specs=[vmem] * 5 + [hbm] * 3,
        out_shape=[
            jax.ShapeDtypeStruct((rows, width), BF16),
            jax.ShapeDtypeStruct((rows, width), F32),
            jax.ShapeDtypeStruct((2, width), F32),
            jax.ShapeDtypeStruct((width, rows), BF16),
            jax.ShapeDtypeStruct((HEADS, rows), F32),
            jax.ShapeDtypeStruct((2, 4, PIECE, width), BF16),
            jax.ShapeDtypeStruct(UNIT, BF16),
            jax.ShapeDtypeStruct(UNIT, BF16),
        ],
        scratch_shapes=[
            pltpu.VMEM((width, width), BF16),
            pltpu.VMEM((width, hidden_width), BF16),
            pltpu.VMEM((hidden_width, width), BF16),
            pltpu.VMEM((2, 4, PIECE, width), BF16),
            pltpu.VMEM(UNIT, BF16),
            pltpu.VMEM(UNIT, BF16),
            pltpu.SemaphoreType.DMA((3,)),
            pltpu.SemaphoreType.DMA((3,)),
        ],
        compiler_params=params(),
        name="feed",
    )(mixed, inverse, stream, upstream, gain, shift, output_weight, up_weight, down_weight)


def add_into(target, other, lead):
    for index in lead:
        total = target[index].astype(F32) + other[index].astype(F32)
        target[index] = total.astype(BF16)


class Plane:
    def __init__(self, unit, buffers, loaded, sems):
        self.unit, self.sems = unit, sems
        self.local, self.one, self.two_a, self.two_b, self.three = buffers
        self.z, self.x, self.y, self.c = place()
        (self.core, self.across, self.along), _ = neighbours()
        self.half = self.three.shape[-1] // 2
        self.load = pltpu.make_async_copy(unit.at[self.c], self.local, loaded)

    def copy(self, slot):
        x, y, half = self.x, self.y, self.half
        left, right = pl.ds(0, half), pl.ds(half, half)
        if slot == 0:
            return send(self.unit.at[1 - self.c], self.one, self.sems, 0, self.core)
        if slot == 1:
            return send(self.one.at[:, 1 - x, :, :, left], self.two_a, self.sems, 1, self.across)
        if slot == 2:
            return send(self.one.at[1 - y, :, :, :, right], self.two_b, self.sems, 2, self.along)
        if slot == 3:
            return send(
                self.two_a.at[1 - y], self.three.at[:, :, left], self.sems, 3, self.along
            )
        return send(self.two_b.at[1 - x], self.three.at[:, :, right], self.sems, 4, self.across)

    def start(self, *slots):
        for slot in slots:
            self.copy(slot).start()

    def begin(self):
        self.load.start()
        self.start(0)

    def add_one(self):
        self.load.wait()
        self.copy(0).wait_recv()
        add_into(self.one, self.local, [(y, x, z) for y in range(2) for x in range(2) for z in range(4)])

    def add_two(self):
        x, y, half = self.x, self.y, self.half
        self.copy(1).wait_recv()
        self.copy(2).wait_recv()
        for index in range(2):
            for z in range(4):
                total = self.two_a[index, z].astype(F32)
                total = total + self.one[index, x, z, :, 0:half].astype(F32)
                self.two_a[index, z] = total.astype(BF16)
                total = self.two_b[index, z].astype(F32)
                total = total + self.one[y, index, z, :, half : 2 * half].astype(F32)
                self.two_b[index, z] = total.astype(BF16)

    def add_three(self):
        x, y, half = self.x, self.y, self.half
        self.copy(3).wait_recv()
        self.copy(4).wait_recv()
        for z in range(4):
            total = self.three[z, :, 0:half].astype(F32) + self.two_a[y, z].astype(F32)
            self.three[z, :, 0:half] = total.astype(BF16)
            total = self.three[z, :, half : 2 * half].astype(F32) + self.two_b[x, z].astype(F32)
            self.three[z, :, half : 2 * half] = total.astype(BF16)

    def finish(self):
        for slot in range(5):
            self.copy(slot).wait_send()


def plane_buffers():
    _, _, _, zs, piece, width = UNIT
    return [
        pltpu.VMEM((2, 2, zs, piece, width), BF16),
        pltpu.VMEM((2, 2, zs, piece, width), BF16),
        pltpu.VMEM((2, zs, piece, width // 2), BF16),
        pltpu.VMEM((2, zs, piece, width // 2), BF16),
        pltpu.VMEM((zs, piece, width), BF16),
        pltpu.SemaphoreType.DMA,
        pltpu.SemaphoreType.DMA((5,)),
        pltpu.SemaphoreType.DMA((5,)),
    ]


def make_plane(unit, scratch):
    return Plane(unit, scratch[:5], scratch[5], scratch[6:8])


def back_kernel(
    linked,
    query,
    keys,
    values,
    marks,
    probs,
    mixed_grad,
    row_sums,
    normed_hbm,
    query_hbm,
    key_hbm,
    value_hbm,
    output_hbm,
    down_unit,
    up_unit,
    normed_unit,
    heads_unit,
    down_out,
    up_out,
    left,
    right,
    query_back,
    key_back,
    value_back,
    normed,
    query_weight,
    key_weight,
    value_weight,
    grads,
    staged,
    loads,
    stores,
    *scratch,
):
    pair = pl.program_id(0)
    pairs = pl.num_programs(0) - 1
    width, rows = query_back.shape
    group = keys.shape[0]
    blocks = group // KEY_BLOCK
    owners = group // rows
    down = make_plane(down_unit, scratch[:8]) if linked else None
    up = make_plane(up_unit, scratch[8:16]) if linked else None
    sources = [normed_hbm, query_hbm, key_hbm, value_hbm]
    targets = [normed, query_weight, key_weight, value_weight]
    copies = [
        pltpu.make_async_copy(source, target, loads.at[index])
        for index, (source, target) in enumerate(zip(sources, targets))
    ]
    output_copy = pltpu.make_async_copy(output_hbm, heads_unit.at[0, 0], loads.at[4])

    @pl.when(pair == 0)
    def _():
        for copy in copies:
            copy.start()
        output_copy.start()
        if linked:
            greet(neighbours()[0])
            down.begin()
            up.begin()

    def hook(spot):
        if not linked:
            return

        def at(when, action):
            if when % blocks == spot:
                pl.when(pair == when // blocks)(action)

        def down_one():
            down.add_one()
            down.start(1, 2)

        def up_one():
            up.add_one()
            up.start(1, 2)

        def down_two():
            down.add_two()
            down.start(3, 4)

        def up_two():
            up.add_two()
            up.start(3, 4)

        def down_three():
            down.add_three()
            pltpu.make_async_copy(down.three, down_out, stores.at[11]).start()

        at(5, down_one)
        at(16, up_one)
        at(19, down_two)
        at(29, down_three)
        at(35, up_two)

    @pl.when(pair < pairs)
    def _():
        pair_columns(left, query, rows)
        pair_columns(right, mixed_grad, rows)
        kinds = lax.broadcasted_iota(jnp.int32, (128, rows), 0)
        shape = (128, rows)
        for half in range(2):
            total = -row_sums[0, half : half + 1]
            high = total.astype(BF16).astype(F32)
            fill = jnp.where(kinds == ONES, jnp.broadcast_to(high, shape), 0.0)
            fill = jnp.where(kinds == ONES + 1, jnp.broadcast_to(total - high, shape), fill)
            right[128:256, half * rows : (half + 1) * rows] = fill.astype(BF16)

        column = pl.ds(pl.multiple_of(pair * 128, 128), 128)
        total = jnp.zeros((128, 2 * rows), F32)
        for index in range(blocks):
            part = slice(index * KEY_BLOCK, (index + 1) * KEY_BLOCK)
            weights = probs[part, :]
            inner = dot(jnp.concatenate([values[part, :], marks[part, :]], axis=1), right[...])
            score_grad = (weights.astype(F32) * inner).astype(BF16)
            key_back[part, column] = (dot(score_grad, left[...], 1, 1) * LN2).astype(BF16)
            value_back[part, column] = dot(weights, right[0:128, :], 1, 1).astype(BF16)
            total = total + dot(keys[part, :].T, score_grad)
            hook(index)
        scale = HEAD_DIM**-0.5
        base = pl.multiple_of(pair * 128, 128)
        query_back[pl.ds(base, HEAD_DIM), :] = (total[0:HEAD_DIM, 0:rows] * scale).astype(BF16)
        base = pl.multiple_of(pair * 128 + HEAD_DIM, HEAD_DIM)
        query_back[pl.ds(base, HEAD_DIM), :] = (total[HEAD_DIM:128, rows : 2 * rows] * scale).astype(BF16)

    @pl.when(pair == pairs)
    def _():
        for copy in copies:
            copy.wait()
        output_copy.wait()
        own = lax.axis_index("head") * lax.axis_size("seq") + lax.axis_index("seq")
        mine = pl.ds(pl.multiple_of(own * rows, 128), rows)
        heads_stores = []

        def keep(kind, value):
            grads[kind - 1] = value.astype(BF16).reshape(4, 2, PIECE, width)

        keep(1, dot(normed[:, mine], query_back[...], 1, 1))
        keep(2, dot(normed[...], key_back[...]))
        keep(3, dot(normed[...], value_back[...]))
        for kind in (1, 2, 3):
            for half in range(2):
                copy = pltpu.make_async_copy(
                    grads.at[kind - 1, :, half],
                    heads_unit.at[kind // 2, kind % 2, half],
                    stores.at[(kind - 1) * 2 + half],
                )
                copy.start()
                heads_stores.append(copy)

        def owner_store(owner):
            x, y, c = lax.div(owner, 4), lax.rem(lax.div(owner, 2), 2), lax.rem(owner, 2)
            slot = lax.rem(owner, 2)
            return pltpu.make_async_copy(staged.at[slot], normed_unit.at[c, y, x], stores.at[6 + slot])

        def owner_step(owner, carry):
            part = pl.ds(pl.multiple_of(owner * rows, 128), rows)
            total = dot(key_back[part, :], key_weight[...], 1, 1)
            total = total + dot(value_back[part, :], value_weight[...], 1, 1)

            @pl.when(owner >= 2)
            def _():
                owner_store(owner - 2).wait()

            staged[lax.rem(owner, 2)] = total.astype(BF16).reshape(4, PIECE, width)

            @pl.when(owner == own)
            def _():
                extra = dot(query_back[...], query_weight[...], 0, 1)
                staged[lax.rem(owner, 2)] = (total + extra).astype(BF16).reshape(4, PIECE, width)

            owner_store(owner).start()
            return carry

        lax.fori_loop(0, owners, owner_step, 0)
        for owner in (owners - 2, owners - 1):
            owner_store(owner).wait()
        for copy in heads_stores:
            copy.wait()
        if linked:
            up.add_three()
            store = pltpu.make_async_copy(up.three, up_out, stores.at[10])
            store.start()
            store.wait()
            pltpu.make_async_copy(down.three, down_out, stores.at[11]).wait()
            down.finish()
            up.finish()


def attend_back(
    linked, query, keys, values, marks, probs, mixed_grad, row_sums, normed, wq, wk, wv, output_part, down_unit, up_unit
):
    width, rows = query.shape
    group = keys.shape[0]
    pairs = width // 128
    held = lambda pair: jnp.minimum(pair, pairs - 1)
    column = pl.BlockSpec((group, 128), lambda pair: (0, held(pair)))
    row = pl.BlockSpec((128, rows), lambda pair: (held(pair), 0))
    hbm = pl.BlockSpec(memory_space=pltpu.HBM)
    third = jax.ShapeDtypeStruct(UNIT[3:], BF16)
    more = dict(collective_id=1, has_side_effects=True) if linked else {}
    return pl.pallas_call(
        functools.partial(back_kernel, linked),
        grid=(pairs + 1,),
        in_specs=[
            row,
            column,
            column,
            pl.BlockSpec((group, 128), lambda pair: (0, 0), pipeline_mode=pl.Buffered(1)),
            pl.BlockSpec((group, 2 * rows), lambda pair: (0, held(pair))),
            row,
            pl.BlockSpec((1, 2, rows), lambda pair: (held(pair), 0, 0)),
        ]
        + [hbm] * 7,
        out_specs=[hbm] * 4,
        out_shape=[
            jax.ShapeDtypeStruct(UNIT, BF16),
            jax.ShapeDtypeStruct(UNIT, BF16),
            third,
            third,
        ],
        scratch_shapes=[
            pltpu.VMEM((128, 2 * rows), BF16),
            pltpu.VMEM((256, 2 * rows), BF16),
            pltpu.VMEM((width, rows), BF16),
            pltpu.VMEM((group, width), BF16),
            pltpu.VMEM((group, width), BF16),
            pltpu.VMEM((width, group), BF16),
            pltpu.VMEM((width, width), BF16),
            pltpu.VMEM((width, width), BF16),
            pltpu.VMEM((width, width), BF16),
            pltpu.VMEM((3, 4, 2, PIECE, width), BF16),
            pltpu.VMEM((2, 4, PIECE, width), BF16),
            pltpu.SemaphoreType.DMA((5,)),
            pltpu.SemaphoreType.DMA((12,)),
        ]
        + (plane_buffers() * 2 if linked else []),
        compiler_params=params(**more),
        name="attend_back",
    )(query, keys, values, marks, probs, mixed_grad, row_sums, normed, wq, wk, wv, output_part, down_unit, up_unit)


class Line:
    def __init__(self, three, four, out, sems):
        self.three, self.four, self.out, self.sems = three, four, out, sems
        self.z, self.x, self.y, self.c = place()
        (self.core, self.across, self.along), self.planes = neighbours()
        self.half = three.shape[-1] // 2

    def copy(self, slot):
        x, y, c = self.x, self.y, self.c
        left, right = pl.ds(0, self.half), pl.ds(self.half, self.half)
        if slot < 3:
            target = lax.rem(self.z + slot + 1, 4)
            return send(self.three.at[target], self.four.at[slot], self.sems, slot, self.planes[slot])
        mine = self.out.at[c, y, x]
        if slot == 3:
            return send(mine, mine, self.sems, 3, self.across)
        if slot == 4:
            return send(mine, mine, self.sems, 4, self.along)
        if slot == 5:
            other = self.out.at[c, y, 1 - x, :, left]
            return send(other, other, self.sems, 5, self.along)
        if slot == 6:
            other = self.out.at[c, 1 - y, x, :, right]
            return send(other, other, self.sems, 6, self.across)
        return send(self.out.at[c], self.out.at[c], self.sems, 7, self.core)

    def begin(self):
        for slot in range(3):
            self.copy(slot).start()

    def add(self):
        total = self.three[self.z].astype(F32)
        for slot in range(3):
            self.copy(slot).wait_recv()
            total = total + self.four[slot].astype(F32)
        self.out[self.c, self.y, self.x] = total.astype(BF16)
        self.copy(3).start()
        self.copy(4).start()

    def forward(self):
        self.copy(3).wait_recv()
        self.copy(4).wait_recv()
        self.copy(5).start()
        self.copy(6).start()

    def share(self):
        self.copy(5).wait_recv()
        self.copy(6).wait_recv()
        self.copy(7).start()

    def finish(self):
        self.copy(7).wait_recv()
        for slot in range(8):
            self.copy(slot).wait_send()


class Rows:
    def __init__(self, given, part, landed, out, sems):
        self.given, self.part, self.landed, self.out, self.sems = given, part, landed, out, sems
        self.z, self.x, self.y, self.c = place()
        (self.core, self.across, self.along), self.planes = neighbours()

    def index(self, x, y, c):
        return x * 4 + y * 2 + c

    def copy(self, slot):
        x, y, c = self.x, self.y, self.c
        size = self.given.shape[1] // 2
        mine = self.given.at[self.index(x, y, c)]
        if slot < 3:
            return send(mine, mine, self.sems, slot, (self.core, self.across, self.along)[slot])
        if slot == 3:
            other = self.given.at[self.index(1 - x, y, c), pl.ds(0, size)]
            return send(other, other, self.sems, 3, self.along)
        if slot == 4:
            other = self.given.at[self.index(x, 1 - y, c), pl.ds(size, size)]
            return send(other, other, self.sems, 4, self.across)
        if slot < 8:
            flip_x, flip_y = ((1, 0), (0, 1), (1, 1))[slot - 5]
            other = self.given.at[
                self.index(x + flip_x - 2 * flip_x * x, y + flip_y - 2 * flip_y * y, c)
            ]
            return send(other, other, self.sems, slot, self.core)
        if slot < 11:
            step = slot - 8
            target = lax.rem(self.z + step + 1, 4)
            return send(
                self.part.at[target], self.landed.at[step], self.sems, slot, self.planes[step]
            )
        if slot < 14:
            mine = self.out.at[x, self.z]
            return send(mine, mine, self.sems, slot, self.planes[slot - 11])
        return send(self.out.at[x], self.out.at[x], self.sems, 14, self.across)

    def start(self, *slots):
        for slot in slots:
            self.copy(slot).start()

    def landed_all(self, *slots):
        for slot in slots:
            self.copy(slot).wait_recv()

    def finish(self):
        for slot in range(15):
            self.copy(slot).wait_send()


class Small:
    def __init__(self, rows, entry, half_rows, half_entry, landings, out, entry_out, sems):
        self.rows, self.entry, self.half_rows, self.half_entry = rows, entry, half_rows, half_entry
        self.landings, self.out, self.entry_out, self.sems = landings, out, entry_out, sems
        self.z, self.x, self.y, self.c = place()
        (self.core, self.across, self.along), self.planes = neighbours()
        half = rows.shape[-1] // 2
        self.mine = pl.ds(pl.multiple_of(self.c * half, 128), half)
        self.away = pl.ds(pl.multiple_of((1 - self.c) * half, 128), half)

    def copy(self, slot):
        rows_land, entry_land, last = self.landings
        stage, kind = slot // 2, slot % 2
        if stage == 0:
            source = (self.rows.at[:, self.away], self.entry.at[:, :, self.away])[kind]
        else:
            source = (self.half_rows, self.half_entry)[kind]
        if stage < 3:
            target = (rows_land, entry_land)[kind].at[stage]
            return send(source, target, self.sems, slot, (self.core, self.across, self.along)[stage])
        if stage < 6:
            step = stage - 3
            if kind == 0:
                target = self.out.at[self.z, :, self.mine]
            else:
                source = self.half_entry.at[lax.rem(self.z + step + 1, 4)]
                target = last.at[step]
            return send(source, target, self.sems, slot, self.planes[step])
        part = (self.out.at[:, :, self.mine], self.entry_out.at[:, self.mine])[kind]
        return send(part, part, self.sems, slot, self.core)

    def start(self, stage):
        self.copy(2 * stage).start()
        self.copy(2 * stage + 1).start()

    def landed(self, stage):
        self.copy(2 * stage).wait_recv()
        self.copy(2 * stage + 1).wait_recv()

    def add(self, stage):
        rows_land, entry_land, _ = self.landings
        self.landed(stage)
        if stage == 0:
            self.half_rows[...] = self.rows[:, self.mine] + rows_land[0]
            total = self.entry[:, :, self.mine].astype(F32) + entry_land[0].astype(F32)
        else:
            self.half_rows[...] = self.half_rows[...] + rows_land[stage]
            total = self.half_entry[...].astype(F32) + entry_land[stage].astype(F32)
        self.half_entry[...] = total.astype(BF16)

    def sent(self, stage):
        self.copy(2 * stage).wait_send()
        self.copy(2 * stage + 1).wait_send()

    def collect(self):
        last = self.landings[2]
        self.out[self.z, :, self.mine] = self.half_rows[...]
        total = self.half_entry[self.z].astype(F32)
        for step in range(3):
            self.landed(3 + step)
            total = total + last[step].astype(F32)
        self.entry_out[:, self.mine] = total.astype(BF16)
        self.start(6)


def late_kernel(
    slots,
    tokens,
    stream,
    middle_grad,
    gain,
    embed_low,
    found,
    input_weight,
    second_norm,
    mean_norm,
    down_three,
    up_three,
    normed_unit,
    heads_unit,
    embed_grad_out,
    table_out,
    small_out,
    entry_out,
    down_out,
    up_out,
    heads_out,
    given,
    part,
    part_landed,
    rows_own,
    entry_own,
    half_rows,
    half_entry,
    rows_land,
    entry_land,
    entry_last,
    down_four,
    up_four,
    heads_four,
    *scratch,
):
    z, x, y, c = place()
    own = x * 4 + y * 2 + c
    width = stream.shape[1]
    rows = stream.shape[0]
    near, planes = neighbours()
    normed_plane = make_plane(normed_unit, scratch[0:8])
    heads_plane = make_plane(heads_unit, scratch[8:16])
    sems = scratch[16:]
    down = Line(down_three, down_four, down_out, sems[0:2])
    up = Line(up_three, up_four, up_out, sems[2:4])
    heads = Line(heads_plane.three, heads_four, heads_out, sems[4:6])
    table = Rows(given, part, part_landed, table_out, sems[6:8])
    small = Small(
        rows_own,
        entry_own,
        half_rows,
        half_entry,
        (rows_land, entry_land, entry_last),
        small_out,
        entry_out,
        sems[8:10],
    )
    greet(near + planes)
    normed_plane.begin()
    heads_plane.begin()
    down.begin()
    up.begin()
    normed_plane.add_one()
    normed_plane.start(1, 2)
    heads_plane.add_one()
    unit, scale = norm_parts(stream[...])
    normed_plane.add_two()
    normed_plane.start(3, 4)
    normed_plane.add_three()
    heads_plane.start(1, 2)

    incoming = normed_plane.three[...].reshape(rows, width).astype(F32)
    stream_grad = middle_grad[...] + norm_back(incoming, gain[...].reshape(1, width), unit, scale)
    stream_low = stream_grad.astype(BF16)
    embed_grad = dot(stream_low, input_weight[...], 1, 1)
    given[own] = embed_grad.astype(BF16)
    table.start(0, 1, 2)
    embed_grad_out[...] = embed_grad
    entry_own[...] = dot(embed_low[...], stream_low, 0, 0).astype(BF16).reshape(4, 32, width)
    kinds = lax.broadcasted_iota(jnp.int32, (SLOTS, rows), 0)
    picker = jnp.where(kinds == slots[...], 1.0, 0.0).astype(BF16)
    rest = (stream_grad - stream_low.astype(F32)).astype(BF16)
    rows_own[0:SLOTS] = dot(picker, stream_low) + dot(picker, rest)
    rows_own[SLOTS : SLOTS + 1] = jnp.sum(incoming * unit, axis=0, keepdims=True)
    rows_own[SLOTS + 1 : SLOTS + 2] = jnp.sum(incoming, axis=0, keepdims=True)
    rows_own[SLOTS + 2 : SLOTS + 4] = second_norm[...]
    inner = jnp.sum(embed_grad * found[...].astype(F32), axis=0, keepdims=True)
    inner = jnp.sum(inner, axis=1, keepdims=True)
    rows_own[SLOTS + 4 : SLOTS + 5] = jnp.broadcast_to(inner, (1, width))
    rows_own[SLOTS + 5 : SLOTS + 8] = jnp.zeros((3, width), F32)
    small.start(0)
    down.add()
    up.add()
    table.landed_all(0, 1, 2)
    table.start(3, 4)
    small.add(0)
    small.start(1)
    table.landed_all(3, 4)
    table.start(5, 6, 7)
    down.forward()
    up.forward()
    small.sent(1)
    small.add(1)
    small.start(2)
    table.landed_all(5, 6, 7)
    seq = y * 2 + c
    all_given = given[...].reshape(8 * rows, 128)
    size = part.shape[1]
    for quarter in range(4):
        base = seq * (8 * size) + x * (4 * size) + quarter * size
        ids = lax.broadcasted_iota(jnp.int32, (size, rows), 0) + base
        hits = jnp.concatenate(
            [jnp.where(ids == tokens[owner], 1.0, 0.0).astype(BF16) for owner in range(8)], axis=1
        )
        part[quarter] = dot(hits, all_given).astype(BF16)
    table.start(8, 9, 10)
    small.sent(2)
    small.add(2)
    for stage in (3, 4, 5):
        small.start(stage)
    heads_plane.add_two()
    heads_plane.start(3, 4)
    down.share()
    up.share()
    total = part[z].astype(F32)
    for slot in (8, 9, 10):
        table.landed_all(slot)
        total = total + part_landed[slot - 8].astype(F32)
    table_out[x, z] = total.astype(BF16)
    table.start(11, 12, 13)
    small.collect()
    heads_plane.add_three()
    heads.begin()
    table.landed_all(11, 12, 13)
    table.start(14)
    heads.add()
    heads.forward()
    heads.share()
    table.landed_all(14)
    small.landed(6)
    small.sent(0)
    for stage in (3, 4, 5, 6):
        small.sent(stage)
    table.finish()
    normed_plane.finish()
    heads_plane.finish()
    down.finish()
    up.finish()
    heads.finish()


def late(slots, tokens, stream, middle_grad, gain, embed_low, found, input_weight, second_norm, mean_norm, down_three, up_three, normed_unit, heads_unit):
    rows, width = stream.shape
    quarter = VOCAB // 4 // 8
    vmem = pl.BlockSpec(memory_space=pltpu.VMEM)
    hbm = pl.BlockSpec(memory_space=pltpu.HBM)
    done = jax.ShapeDtypeStruct((2, 2, 2, PIECE, width), BF16)
    pair = lambda count: [pltpu.SemaphoreType.DMA((count,)), pltpu.SemaphoreType.DMA((count,))]
    return pl.pallas_call(
        late_kernel,
        in_specs=[vmem] * 12 + [hbm] * 2,
        out_specs=[vmem] * 7,
        out_shape=[
            jax.ShapeDtypeStruct((rows, 128), F32),
            jax.ShapeDtypeStruct((2, 4, quarter, 128), BF16),
            jax.ShapeDtypeStruct((4, 40, width), F32),
            jax.ShapeDtypeStruct((32, width), BF16),
            done,
            done,
            done,
        ],
        scratch_shapes=[
            pltpu.VMEM((8, rows, 128), BF16),
            pltpu.VMEM((4, quarter, 128), BF16),
            pltpu.VMEM((3, quarter, 128), BF16),
            pltpu.VMEM((40, width), F32),
            pltpu.VMEM((4, 32, width), BF16),
            pltpu.VMEM((40, width // 2), F32),
            pltpu.VMEM((4, 32, width // 2), BF16),
            pltpu.VMEM((3, 40, width // 2), F32),
            pltpu.VMEM((3, 4, 32, width // 2), BF16),
            pltpu.VMEM((3, 32, width // 2), BF16),
            pltpu.VMEM((3, PIECE, width), BF16),
            pltpu.VMEM((3, PIECE, width), BF16),
            pltpu.VMEM((3, PIECE, width), BF16),
        ]
        + plane_buffers() * 2
        + pair(8) * 3
        + pair(15)
        + pair(14),
        compiler_params=params(collective_id=2, has_side_effects=True),
        name="late",
    )(slots, tokens, stream, middle_grad, gain, embed_low, found, input_weight, second_norm, mean_norm, down_three, up_three, normed_unit, heads_unit)


def finish_kernel(
    embed_grad,
    table_sum,
    small,
    entry,
    down,
    up,
    heads,
    table,
    mean_norm,
    hidden,
    acts,
    features,
    second_weight,
    embed_out,
    table_out,
    entry_out,
    first_out,
    second_out,
    gain_one,
    shift_one,
    query_out,
    key_out,
    value_out,
    output_out,
    gain_two,
    shift_two,
    up_out,
    down_out,
):
    width = second_weight.shape[0]
    embed_out[...] = embed_grad[...]
    entry_out[...] = entry[...].astype(F32)
    for piece in range(8):
        c, y, x = piece // 4, (piece // 2) % 2, piece % 2
        down_out[piece * PIECE : (piece + 1) * PIECE, :] = down[c, y, x].astype(F32)
        quarter = piece // 2
        up_out[x * PIECE : (x + 1) * PIECE, quarter * width : (quarter + 1) * width] = up[c, y, x].astype(F32)
        target = (output_out, query_out, key_out, value_out)[quarter]
        target[x * PIECE : (x + 1) * PIECE, :] = heads[c, y, x].astype(F32)
    totals = small[0, SLOTS : SLOTS + 8]
    for plane in range(1, small.shape[0]):
        totals = totals + small[plane, SLOTS : SLOTS + 8]
    gain_one[...] = totals[0:1].reshape(width)
    shift_one[...] = totals[1:2].reshape(width)
    gain_two[...] = totals[2:3].reshape(width)
    shift_two[...] = totals[3:4].reshape(width)
    mean = mean_norm[0:1]
    inverse = 1.0 / mean
    mean_grad = -totals[4:5, 0:128] * inverse * inverse * (1.0 / VOCAB)
    wide = table[...].astype(F32)
    norms = jnp.sqrt(jnp.sum(wide * wide, axis=1, keepdims=True))
    sums = table_sum[...].reshape(table.shape).astype(F32)
    table_out[...] = sums * inverse + mean_grad * (wide / norms)
    tog = jnp.concatenate([small[plane, 0:SLOTS] for plane in range(small.shape[0])], axis=0)
    second_out[...] = lax.dot_general(
        acts[...], tog, (((0,), (0,)), ((), ())), precision=lax.Precision.HIGHEST, preferred_element_type=F32
    )
    high = tog.astype(BF16)
    rest = (tog - high.astype(F32)).astype(BF16)
    act_grad = dot(high, second_weight[...], 1, 1) + dot(rest, second_weight[...], 1, 1)
    value = hidden[...]
    gate = 1.0 / (1.0 + jnp.exp(-value))
    hidden_grad = act_grad * (gate * (1.0 + value * (1.0 - gate)))
    first_out[...] = lax.dot_general(
        features[...], hidden_grad, (((0,), (0,)), ((), ())), precision=lax.Precision.HIGHEST, preferred_element_type=F32
    )


def finish(embed_grad, table_sum, small, entry, down, up, heads, table, mean_norm, hidden, acts, features, second_weight):
    rows = embed_grad.shape[0]
    width = second_weight.shape[0]
    wide = lambda *shape: jax.ShapeDtypeStruct(shape, F32)
    shard = width // 4
    return pl.pallas_call(
        finish_kernel,
        out_shape=[
            wide(rows, 128),
            wide(*table.shape),
            wide(32, width),
            wide(features.shape[1], width),
            wide(acts.shape[1], width),
            wide(width),
            wide(width),
            wide(shard, width),
            wide(shard, width),
            wide(shard, width),
            wide(shard, width),
            wide(width),
            wide(width),
            wide(shard, 4 * width),
            wide(width, width),
        ],
        compiler_params=params(),
        name="finish",
    )(embed_grad, table_sum, small, entry, down, up, heads, table, mean_norm, hidden, acts, features, second_weight)


def time_features(steps, width):
    half = width // 2
    freqs = jnp.exp(-math.log(10000.0) * jnp.arange(half, dtype=F32) / half)
    angles = steps.astype(F32)[:, None] * freqs[None, :]
    return jnp.concatenate([jnp.cos(angles), jnp.sin(angles)], axis=1)


def split_three(values):
    high = values.astype(BF16)
    rest = values - high.astype(F32)
    middle = rest.astype(BF16)
    return high, middle, (rest - middle.astype(F32)).astype(BF16)


def body(
    tokens,
    segments,
    live_lengths,
    timesteps,
    table,
    input_weight,
    time_first,
    time_second,
    first_gain,
    first_shift,
    query_weight,
    key_weight,
    value_weight,
    output_weight,
    second_gain,
    second_shift,
    up_weight,
    down_weight,
    upstream,
):
    blocks = lax.axis_size("head") * lax.axis_size("seq")
    planes = lax.axis_size("dp")
    rows = tokens.shape[0]
    width = query_weight.shape[0]
    shard_rows = table.shape[0]
    slot_count = live_lengths.shape[1]
    highest = lax.Precision.HIGHEST
    plane = lax.axis_index("dp")
    seq_index = lax.axis_index("seq")
    own = lax.axis_index("head") * lax.axis_size("seq") + seq_index
    linked = planes == 4

    notes = jnp.concatenate(
        [
            tokens.reshape(3, 128),
            segments.reshape(3, 128),
            jnp.pad(timesteps, ((0, 1), (0, 128 - slot_count))),
        ],
        axis=0,
    )
    full_table, notes_all, steps_all, mean_norm = gather(table, notes)
    steps = jnp.where(jnp.arange(SLOTS)[None, :] < slot_count, steps_all[:, 6, :SLOTS], 0).reshape(-1)
    present = jnp.tile(jnp.arange(SLOTS) < slot_count, planes)
    features = jnp.where(present[:, None], time_features(steps, time_first.shape[0]), 0.0)
    second_wide = time_second.astype(F32)
    time_hidden = jnp.dot(features, time_first.astype(F32), precision=highest)
    time_act = jax.nn.silu(time_hidden)
    time_rows = jnp.dot(
        lax.dynamic_slice_in_dim(time_act, plane * SLOTS, SLOTS), second_wide, precision=highest
    )
    entry = jnp.concatenate(
        [input_weight, *split_three(time_rows), jnp.zeros((SLOTS, width), BF16)], axis=0
    )
    lengths = jnp.pad(live_lengths.astype(F32), ((0, 0), (0, 128 - slot_count)))
    normed, keys, values, marks, stream, query, embed_low, found = embed(
        own[None],
        notes_all,
        lengths,
        mean_norm,
        full_table,
        entry,
        first_gain,
        first_shift,
        query_weight,
        key_weight,
        value_weight,
        rows,
        blocks,
    )
    probs, mixed, inverse = attend(query, keys, values, marks, segments[None])
    activation, middle_grad, second_norm, mixed_grad, row_sums, output_part, up_unit, down_unit = feed(
        mixed,
        inverse.reshape(HEADS, rows),
        stream,
        upstream,
        second_gain,
        second_shift,
        output_weight,
        up_weight,
        down_weight,
    )
    normed_unit, heads_unit, down_three, up_three = attend_back(
        linked,
        query,
        keys,
        values,
        marks,
        probs,
        mixed_grad,
        row_sums.reshape(HEADS // 2, 2, rows),
        normed,
        query_weight,
        key_weight,
        value_weight,
        output_part,
        down_unit,
        up_unit,
    )
    if linked:
        shard = width // planes
        embed_grad, table_sum, small, entry_sum, down_sum, up_sum, heads_sum = late(
            segments[None],
            notes_all[:, 0:3].reshape(8, 1, rows),
            stream,
            middle_grad,
            first_gain,
            embed_low,
            found,
            input_weight,
            second_norm,
            mean_norm,
            down_three,
            up_three,
            normed_unit,
            heads_unit,
        )
        outs = finish(
            embed_grad,
            table_sum,
            small,
            entry_sum,
            down_sum,
            up_sum,
            heads_sum,
            table,
            mean_norm,
            time_hidden,
            lax.dynamic_slice_in_dim(time_act, plane * shard, shard, axis=1),
            lax.dynamic_slice_in_dim(features, plane * 32, 32, axis=1),
            time_second,
        )
        return (activation, *outs)

    heads_all = heads_unit.reshape(4, 2, 4, PIECE, width).transpose(0, 2, 1, 3, 4)
    output_grad, query_grad, key_grad, value_grad = heads_all.reshape(4, width, width)
    down_grad = down_unit.transpose(3, 0, 1, 2, 4, 5).reshape(-1, width)
    up_grad = up_unit.transpose(3, 2, 4, 0, 1, 5).reshape(width, -1)
    normed_grad = lax.psum_scatter(
        normed_unit.transpose(2, 1, 0, 3, 4, 5).reshape(-1, width),
        ("head", "seq"),
        scatter_dimension=0,
        tiled=True,
    ).astype(F32)
    mean_norm = mean_norm[0, 0]
    features = lax.dynamic_slice_in_dim(features, plane * SLOTS, slot_count)
    time_hidden = lax.dynamic_slice_in_dim(time_hidden, plane * SLOTS, slot_count)
    time_act = lax.dynamic_slice_in_dim(time_act, plane * SLOTS, slot_count)

    def one_norm(values, gain, shift):
        unit, _ = norm_parts(values)
        return unit * gain + shift

    _, first_back = jax.vjp(one_norm, stream, first_gain, first_shift)
    stream_part, first_gain_grad, first_shift_grad = first_back(normed_grad)
    stream_grad = middle_grad + stream_part
    stream_low = stream_grad.astype(BF16)
    input_grad = dot(embed_low, stream_low, 0, 0)
    embed_grad = dot(stream_low, input_weight, 1, 1)
    picker = (segments[:, None] == jnp.arange(slot_count, dtype=jnp.int32)[None, :]).astype(F32)
    time_out_grad = contract_exact(picker, stream_grad)
    time_second_grad = contract_exact(time_act, time_out_grad)
    act_grad = lax.dot_general(
        time_out_grad, second_wide, (((1,), (1,)), ((), ())), precision=highest
    )
    _, silu_back = jax.vjp(jax.nn.silu, time_hidden)
    time_hidden_grad = silu_back(act_grad)[0]
    time_first_grad = contract_exact(features, time_hidden_grad)

    def reduce(value):
        part = lax.psum_scatter(value.astype(BF16), "dp", scatter_dimension=0, tiled=True)
        return lax.psum(part, ("head", "seq")).astype(F32)

    shards = [
        reduce(value)
        for value in (
            input_grad,
            time_first_grad,
            time_second_grad,
            query_grad,
            key_grad,
            value_grad,
            output_grad,
            up_grad,
            down_grad,
        )
    ]
    mean_part = -jnp.sum(embed_grad * found.astype(F32)) / (mean_norm * mean_norm)
    scaled_grad = embed_grad / mean_norm
    table_sum = jax.ops.segment_sum(scaled_grad, tokens, num_segments=VOCAB)
    small = lax.psum(
        (first_gain_grad, first_shift_grad, second_norm[0], second_norm[1], mean_part, table_sum),
        ("dp", "head", "seq"),
    )
    table_rows = lax.dynamic_slice_in_dim(small[5], seq_index * shard_rows, shard_rows)
    table_wide = table.astype(F32)
    row_norms = jnp.sqrt(jnp.sum(table_wide * table_wide, axis=1))
    table_grad = table_rows + small[4] / VOCAB * table_wide / row_norms[:, None]
    return (
        activation,
        embed_grad,
        table_grad,
        shards[0],
        shards[1],
        shards[2],
        small[0],
        small[1],
        shards[3],
        shards[4],
        shards[5],
        shards[6],
        small[2],
        small[3],
        shards[7],
        shards[8],
    )


def solution(mesh):
    tokens = P(("dp", "head", "seq"))
    wide = P(("dp", "head", "seq"), None)
    group = P("dp", None)
    return jax.shard_map(
        body,
        mesh=mesh,
        in_specs=(tokens, tokens, group, group, P("seq", None)) + (P(),) * 13 + (wide,),
        out_specs=(wide, wide, P("seq", None), group, group, group, P(), P())
        + (group,) * 4
        + (P(), P(), group, group),
        check_vma=False,
    )
```

```python
import functools
import math

import jax
import jax.numpy as jnp
from jax import lax
from jax.experimental import pallas as pl
from jax.experimental.pallas import tpu as pltpu
from jax.sharding import PartitionSpec as P

HEADS = 12
HEAD_DIM = 64
VOCAB = 8192
EPSILON = 1e-05
MASKED = -1e30
LOG2E = math.log2(math.e)
LN2 = math.log(2.0)
KEY_BLOCK = 512
SLOTS = 32
DEAD = 25
ONES = 32
VMEM_LIMIT = 60 * 2**20
SAFE = 60.0
PIECE = 96
UNIT = (2, 2, 2, 4, PIECE, 768)
MESH = pl.DeviceIdType.MESH

(
    GREET,
    D_LOCAL,
    U_LOCAL,
    X_LOCAL,
    LOAD,
    LOADED,
    GRAD_Q,
    GRAD_K,
    GRAD_V,
    NORM,
    NORM_REST,
    D_CORE,
    D_ONE,
    D_LEFT,
    D_RIGHT,
    D_THREE,
    U_CORE,
    U_ONE,
    U_LEFT,
    U_RIGHT,
    U_THREE,
    X_CORE,
    X_ONE,
    X_LEFT,
    X_RIGHT,
    X_THREE,
    H_CORE,
    H_ONE,
    H_LEFT,
    H_RIGHT,
    H_THREE,
    D_SEND,
    D_SUM,
    D_PASS_X,
    D_PASS_Y,
    D_SHARE,
    D_END,
    U_SEND,
    U_SUM,
    U_PASS_X,
    U_PASS_Y,
    U_SHARE,
    U_END,
    H_SEND,
    H_SUM,
    H_PASS_X,
    H_PASS_Y,
    H_SHARE,
    H_END,
    T_FIRST,
    T_PASS_X,
    T_PASS_Y,
    T_CORE,
    T_ROWS,
    T_SUM,
    T_PASS,
    T_END,
    S_FIRST,
    S_CORE,
    S_X,
    S_Y,
    S_COLLECT,
    S_END,
) = range(0, 252, 4)

BACK_ORDER = (
    (
        GREET, D_CORE, D_CORE + 3, D_CORE + 2, D_CORE + 1,
    ),
    (
        D_LOCAL, D_ONE + 2, U_CORE, U_CORE + 3, U_CORE + 2, U_CORE + 1, D_ONE + 1, D_ONE + 3,
    ),
    (
        U_LOCAL, D_LEFT + 2, D_RIGHT + 2, D_RIGHT + 1, D_LEFT + 1, D_ONE,
    ),
    (
        D_THREE + 1, D_SEND + 1, U_ONE + 1, D_LEFT + 3, D_RIGHT + 3, U_ONE, D_THREE + 2, D_SEND + 2,
    ),
    (
        D_LEFT, D_RIGHT, U_ONE + 3, D_THREE + 3, D_SEND + 3, U_ONE + 2,
    ),
    (
        D_THREE, D_SUM, U_LEFT + 1, U_LEFT, U_RIGHT + 1, U_RIGHT,
    ),
    (
        D_PASS_X, D_PASS_Y, U_RIGHT + 2, U_RIGHT + 3, U_THREE + 1, U_LEFT + 2, U_LEFT + 3,
    ),
    (
        U_THREE, D_SHARE,
    ),
    (
        U_THREE + 2, U_THREE + 3, D_END,
    ),
)
LATE_ORDER = (
    GREET, X_CORE + 3, X_CORE + 1, X_LOCAL, LOAD, U_SEND + 1, U_SEND + 2, U_SEND + 3, X_CORE + 2, X_ONE + 3,
    X_CORE, X_ONE + 2, X_ONE + 1, X_ONE, LOADED, GRAD_Q, GRAD_V, X_RIGHT + 2, X_LEFT + 3, X_LEFT + 2,
    X_RIGHT + 3, GRAD_K, H_CORE + 3, X_RIGHT + 1, X_LEFT + 1, X_LEFT, X_RIGHT, H_CORE + 1, X_THREE + 2,
    H_CORE + 2, X_THREE + 3, H_CORE, H_ONE + 3, X_THREE + 1, H_ONE + 2, X_THREE, NORM, H_LEFT + 3,
    H_RIGHT + 3, T_FIRST, NORM_REST, H_THREE + 3, H_SEND + 3, H_RIGHT + 2, H_LEFT + 2, S_FIRST, T_PASS_X, T_PASS_Y,
    H_ONE + 1, U_SUM, H_THREE + 2, H_SEND + 2, T_CORE, T_ROWS, H_RIGHT + 1, H_LEFT + 1, T_ROWS + 1, H_ONE,
    U_PASS_X, T_ROWS + 2, S_CORE, H_THREE + 1, H_SEND + 1, T_ROWS + 3, H_RIGHT, U_PASS_Y, H_LEFT, T_SUM,
    S_X, H_THREE, H_SUM, U_SHARE, S_Y, H_PASS_Y, T_PASS, H_PASS_X, H_SHARE, S_COLLECT, H_END,
    U_END, S_END, T_END,
)

F32 = jnp.float32
BF16 = jnp.bfloat16


def dot(left, right, left_dim=1, right_dim=0):
    return lax.dot_general(
        left, right, (((left_dim,), (right_dim,)), ((), ())), preferred_element_type=F32
    )


def contract_exact(left, right):
    return lax.dot_general(left, right, (((0,), (0,)), ((), ())), precision=lax.Precision.HIGHEST)


def whole(shape):
    return pl.BlockSpec(shape, lambda *_: (0,) * len(shape))


def params(**more):
    return pltpu.CompilerParams(vmem_limit_bytes=VMEM_LIMIT, **more)


def norm_parts(values):
    centre = values - jnp.mean(values, axis=-1, keepdims=True)
    spread = jnp.mean(centre * centre, axis=-1, keepdims=True)
    scale = lax.rsqrt(spread + EPSILON)
    return centre * scale, scale


def norm_back(incoming, gain, unit, scale):
    scaled = incoming * gain
    inner = scaled - jnp.mean(scaled, axis=-1, keepdims=True)
    return scale * (inner - unit * jnp.mean(scaled * unit, axis=-1, keepdims=True))


def place():
    seq = lax.axis_index("seq")
    return lax.axis_index("dp"), lax.axis_index("head"), lax.div(seq, 2), lax.rem(seq, 2)


def device(z, x, y, c):
    return (z, x, y * 2 + c)


def neighbours():
    z, x, y, c = place()
    planes = lax.axis_size("dp")
    near = [device(z, x, y, 1 - c), device(z, 1 - x, y, c), device(z, x, 1 - y, c)]
    return near, [device(lax.rem(z + step, planes), x, y, c) for step in range(1, planes)]


def greet(devices):
    barrier = pltpu.get_barrier_semaphore()
    for other in devices:
        pl.semaphore_signal(barrier, inc=1, device_id=other, device_id_type=MESH)
    pl.semaphore_wait(barrier, len(devices))


def send(source, target, sems, slot, other):
    return pltpu.make_async_remote_copy(
        src_ref=source,
        dst_ref=target,
        send_sem=sems[0].at[slot],
        recv_sem=sems[1].at[slot],
        device_id=other,
        device_id_type=MESH,
    )


def column_of(row):
    size = row.shape[1]
    shape = (size, size)
    same = lax.broadcasted_iota(jnp.int32, shape, 0) == lax.broadcasted_iota(jnp.int32, shape, 1)
    return jnp.sum(jnp.where(same, jnp.broadcast_to(row, shape), 0.0), axis=1, keepdims=True)


def split_three(values):
    high = values.astype(BF16)
    rest = values - high.astype(F32)
    middle = rest.astype(BF16)
    return high, middle, (rest - middle.astype(F32)).astype(BF16)


def dot_three(left, right):
    return sum(dot(part, right) for part in split_three(left))


def gather_kernel(
    table,
    tokens,
    segments,
    timesteps,
    lengths,
    input_weight,
    first_weight,
    second_weight,
    full,
    notes_all,
    mean_out,
    entry_out,
    hidden_out,
    acts_out,
    features_out,
    steps_all,
    acts,
    sums,
    local,
    *sems,
):
    z, x, y, c = place()
    seq = y * 2 + c
    own = x * 4 + seq
    near, planes = neighbours()
    others = []
    for flip in range(1, 8):
        xx, yy, cc = flip // 4, (flip // 2) % 2, flip % 2
        others.append(device(z, x + xx - 2 * xx * x, y + yy - 2 * yy * y, c + cc - 2 * cc * c))
    slot_count = timesteps.shape[1]
    notes_all[own, 0:3] = tokens[...]
    notes_all[own, 3:6] = segments[...]
    notes_all[own, 6:8] = jnp.zeros((2, 128), jnp.int32)
    notes_all[own, 6:7, 0:slot_count] = timesteps[...]
    notes_all[own, 7:8, 0:slot_count] = lengths[...]
    notes = notes_all.at[own]
    greet(others + planes)
    keep = pltpu.make_async_copy(table, full.at[seq], local.at[0])
    keep.start()
    tables = [
        send(table, full.at[seq], sems, 0, near[2]),
        send(table, full.at[seq], sems, 1, near[0]),
    ]
    for copy in tables:
        copy.start()
    copies = [send(notes, notes, sems, 3 + index, other) for index, other in enumerate(others)]
    steps = [
        send(notes, steps_all.at[z], sems, 13 + index, other) for index, other in enumerate(planes)
    ]
    for copy in copies + steps:
        copy.start()
    wide = table[...].astype(F32)
    norms = jnp.sqrt(jnp.sum(wide * wide, axis=1, keepdims=True))
    total = jnp.sum(norms, axis=0, keepdims=True)
    sums[seq] = jnp.broadcast_to(total, (8, 128))
    partials = [
        send(sums.at[seq], sums.at[seq], sems, 10 + index, other)
        for index, other in enumerate((near[0], near[2], device(z, x, 1 - y, 1 - c)))
    ]
    for copy in partials:
        copy.start()
    for copy in steps:
        copy.wait()
    steps_all[z] = notes_all[own]

    count = steps_all.shape[0]
    half = features_out.shape[0] // 2
    lanes = lax.broadcasted_iota(jnp.int32, (SLOTS, 2 * half), 1)
    slots = lax.broadcasted_iota(jnp.int32, (SLOTS, 2 * half), 0)
    freqs = jnp.exp((-math.log(10000.0)) * jnp.where(lanes < half, lanes, lanes - half).astype(F32) / half)
    parts = []
    for plane in range(count):
        angles = column_of(steps_all[plane, 6:7].astype(F32))[0:SLOTS] * freqs
        waves = jnp.where(lanes < half, jnp.cos(angles), jnp.sin(angles))
        parts.append(jnp.where(slots < slot_count, waves, 0.0))
    features = jnp.concatenate(parts, axis=0)
    features_out[...] = features.T
    hidden = dot_three(features, first_weight[...])
    hidden_out[...] = hidden
    act = hidden / (1.0 + jnp.exp(-hidden))
    acts[...] = act
    acts_out[...] = act.T
    time_rows = dot_three(acts[pl.ds(pl.multiple_of(z * SLOTS, SLOTS), SLOTS), :], second_weight[...])
    entry_out[0:128] = input_weight[...]
    for index, part in enumerate(split_three(time_rows)):
        entry_out[128 + index * SLOTS : 128 + (index + 1) * SLOTS] = part
    entry_out[128 + 3 * SLOTS : 256] = jnp.zeros((128 - 3 * SLOTS, entry_out.shape[1]), BF16)

    for copy in copies + partials:
        copy.wait()
    mean_out[...] = jnp.sum(sums[...], axis=0) * (1.0 / VOCAB)
    tables[0].wait_recv()
    away = (1 - y) * 2 + c
    forward = send(full.at[away], full.at[away], sems, 2, near[0])
    forward.start()
    keep.wait()
    tables[1].wait_recv()
    forward.wait()
    for copy in tables:
        copy.wait_send()


def gather(table, tokens, segments, timesteps, lengths, input_weight, first_weight, second_weight):
    rows, _ = table.shape
    width = input_weight.shape[1]
    planes = lax.axis_size("dp")
    vmem = pl.BlockSpec(memory_space=pltpu.VMEM)
    hbm = pl.BlockSpec(memory_space=pltpu.HBM)
    slots = 13 + planes - 1
    return pl.pallas_call(
        gather_kernel,
        in_specs=[vmem] * 8,
        out_specs=[hbm] + [vmem] * 6,
        out_shape=[
            jax.ShapeDtypeStruct((4, rows, 128), BF16),
            jax.ShapeDtypeStruct((8, 8, 128), jnp.int32),
            jax.ShapeDtypeStruct((8, 128), F32),
            jax.ShapeDtypeStruct((256, width), BF16),
            jax.ShapeDtypeStruct((planes * SLOTS, width), F32),
            jax.ShapeDtypeStruct((width, planes * SLOTS), F32),
            jax.ShapeDtypeStruct((first_weight.shape[0], planes * SLOTS), F32),
        ],
        scratch_shapes=[
            pltpu.VMEM((planes, 8, 128), jnp.int32),
            pltpu.VMEM((planes * SLOTS, width), F32),
            pltpu.VMEM((4, 8, 128), F32),
            pltpu.SemaphoreType.DMA((1,)),
            pltpu.SemaphoreType.DMA((slots,)),
            pltpu.SemaphoreType.DMA((slots,)),
        ],
        compiler_params=params(collective_id=0, has_side_effects=True),
        name="gather",
    )(table, tokens, segments, timesteps, lengths, input_weight, first_weight, second_weight)


def embed_kernel(
    own,
    tokens,
    notes,
    mean_norm,
    table_low,
    entry,
    gain,
    shift,
    query_weight,
    key_weight,
    value_weight,
    normed_out,
    key_out,
    value_out,
    mark_out,
    stream_out,
    query_out,
    low_out,
    found_out,
    picked,
    limits,
    table,
):
    step = pl.program_id(0)
    blocks = pl.num_programs(0)
    rows = picked.shape[1]
    width = stream_out.shape[1]
    block = lax.rem(own[0] + step, blocks)
    base = block * rows

    @pl.when(step == 0)
    def _():
        kinds = lax.broadcasted_iota(jnp.int32, (128, 128), 0)
        below = jnp.zeros((128, 128), F32)
        for part in range(blocks if isinstance(blocks, int) else 8):
            for line in range(3, 6):
                below = below + jnp.where(notes[part, line : line + 1, :] < kinds, 1.0, 0.0)
        starts = jnp.sum(below, axis=1, keepdims=True)
        shape = (128, 128)
        same = lax.broadcasted_iota(jnp.int32, shape, 0) == lax.broadcasted_iota(jnp.int32, shape, 1)
        starts = jnp.sum(jnp.where(same, jnp.broadcast_to(starts, shape), 0.0), axis=0, keepdims=True)
        limits[...] = starts + notes[own[0], 7:8, :].astype(F32)
        for part in range(4):
            table[part * 2048 : (part + 1) * 2048, :] = table_low[part].astype(F32)

    def pick(slot, source, row):
        line, lane = row // 128, row % 128
        picked[slot, pl.ds(row, 1), :] = table[pl.ds(tokens[source, line, lane], 1), :]

    @pl.when(step == 0)
    def _():
        def pick_some(index, carry):
            for inner in range(32):
                pick(0, block, index * 32 + inner)
            return carry

        lax.fori_loop(0, rows // 32, pick_some, 0)

    found = picked[lax.rem(step, 2)]
    low = (found / mean_norm[0:1]).astype(BF16)
    following = lax.rem(block + 1, blocks)
    for row in range(rows):
        pick(lax.rem(step + 1, 2), following, row)
    lanes = lax.broadcasted_iota(jnp.int32, (rows, 128), 1)
    slot = jnp.concatenate(
        [column_of(notes[block, line : line + 1, :].astype(F32)) for line in range(3, 6)], axis=0
    )
    same = jnp.where((lanes & (SLOTS - 1)).astype(F32) == slot, 1.0, 0.0)
    spread = jnp.where(lanes < 3 * SLOTS, same, 0.0).astype(BF16)
    stream = dot(jnp.concatenate([low, spread], axis=1), entry[...])
    unit, _ = norm_parts(stream)
    normed = (unit * gain[...].reshape(1, width) + shift[...].reshape(1, width)).astype(BF16)
    normed_out[...] = normed.T
    for weight, target in ((key_weight, key_out), (value_weight, value_out)):
        result = dot(normed, weight[...]).astype(BF16)
        for pair in range(width // 128):
            target[pair] = result[:, pair * 128 : (pair + 1) * 128]
    first = jnp.where(lanes < SLOTS, same, 0.0)
    limit = jnp.sum(first * limits[...], axis=1, keepdims=True)
    index = (base + lax.broadcasted_iota(jnp.int32, (rows, 1), 0)).astype(F32)
    dead = jnp.where(index < limit, 0.0, 1.0)
    marks = jnp.where(lanes == DEAD, dead, first)
    marks = jnp.where((lanes >= ONES) & (lanes < ONES + 2), 1.0, marks)
    mark_out[...] = marks.astype(BF16)

    @pl.when(step == 0)
    def _():
        stream_out[...] = stream
        low_out[...] = low
        found_out[...] = found.astype(BF16)
        query = dot(query_weight[...], normed, 0, 1) * (LOG2E / math.sqrt(HEAD_DIM))
        query_out[...] = query.astype(BF16)


def embed(own, notes, mean_norm, table, entry, gain, shift, wq, wk, wv, rows, blocks):
    group = rows * blocks
    width = wq.shape[0]
    turn = lambda step, own: (lax.rem(own[0] + step, blocks), 0)
    return pl.pallas_call(
        embed_kernel,
        grid_spec=pltpu.PrefetchScalarGridSpec(
            num_scalar_prefetch=1,
            grid=(blocks,),
            in_specs=[
                pl.BlockSpec(memory_space=pltpu.SMEM),
                whole(notes.shape),
                whole((8, 128)),
                whole(table.shape),
                whole(entry.shape),
                whole((width,)),
                whole((width,)),
                whole((width, width)),
                whole((width, width)),
                whole((width, width)),
            ],
            out_specs=[
                pl.BlockSpec((width, rows), lambda *args: turn(*args)[::-1]),
                pl.BlockSpec((width // 128, rows, 128), lambda *args: (0, *turn(*args))),
                pl.BlockSpec((width // 128, rows, 128), lambda *args: (0, *turn(*args))),
                pl.BlockSpec((rows, 128), turn),
                whole((rows, width)),
                whole((width, rows)),
                whole((rows, 128)),
                whole((rows, 128)),
            ],
            scratch_shapes=[
                pltpu.VMEM((2, rows, 128), F32),
                pltpu.VMEM((1, 128), F32),
                pltpu.VMEM((VOCAB, 128), F32),
            ],
        ),
        out_shape=[
            jax.ShapeDtypeStruct((width, group), BF16),
            jax.ShapeDtypeStruct((width // 128, group, 128), BF16),
            jax.ShapeDtypeStruct((width // 128, group, 128), BF16),
            jax.ShapeDtypeStruct((group, 128), BF16),
            jax.ShapeDtypeStruct((rows, width), F32),
            jax.ShapeDtypeStruct((width, rows), BF16),
            jax.ShapeDtypeStruct((rows, 128), BF16),
            jax.ShapeDtypeStruct((rows, 128), BF16),
        ],
        compiler_params=params(),
        name="embed",
    )(own, notes, notes, mean_norm, table, entry, gain, shift, wq, wk, wv)


def pair_columns(target, pair, rows):
    target[0:HEAD_DIM, 0:rows] = pair[0:HEAD_DIM]
    target[0:HEAD_DIM, rows : 2 * rows] = jnp.zeros((HEAD_DIM, rows), BF16)
    target[HEAD_DIM : 2 * HEAD_DIM, 0:rows] = jnp.zeros((HEAD_DIM, rows), BF16)
    target[HEAD_DIM : 2 * HEAD_DIM, rows : 2 * rows] = pair[HEAD_DIM : 2 * HEAD_DIM]


def forward_kernel(query, keys, values, marks, slots, probs_out, mixed_out, inverse_out, right, scores):
    rows = query.shape[1]
    group = keys.shape[0]
    blocks = group // KEY_BLOCK
    pair_columns(right, query, rows)
    kinds = lax.broadcasted_iota(jnp.int32, (128, rows), 0)
    slot = jnp.concatenate([slots[line : line + 1, :] for line in range(rows // 128)], axis=1)
    away = jnp.where((kinds < DEAD) & (kinds != slot), MASKED, 0.0)
    away = jnp.where(kinds == DEAD, MASKED, away).astype(BF16)
    right[128:256, 0:rows] = away
    right[128:256, rows : 2 * rows] = away

    ones = jnp.ones((16, KEY_BLOCK), BF16)

    def left_of(part):
        return jnp.concatenate([keys[part, :], marks[part, :]], axis=1)

    def weigh(part, probs, total):
        probs_out[part, :] = probs
        return total + dot(jnp.concatenate([values[part, :].T, ones], axis=0), probs)

    def store(total):
        inverse = 1.0 / total[128:129]
        mixed_out[0:HEAD_DIM] = total[0:HEAD_DIM, 0:rows] * inverse[:, 0:rows]
        mixed_out[HEAD_DIM:128] = total[HEAD_DIM:128, rows : 2 * rows] * inverse[:, rows : 2 * rows]
        inverse_out[0, 0:1] = inverse[:, 0:rows]
        inverse_out[0, 1:2] = inverse[:, rows : 2 * rows]

    highest = jnp.max(jnp.abs(keys[...]).astype(F32), axis=0, keepdims=True)
    spans = jnp.abs(query[...].astype(F32)) * column_of(highest)
    first = jnp.max(jnp.sum(spans[0:HEAD_DIM], axis=0, keepdims=True))
    second = jnp.max(jnp.sum(spans[HEAD_DIM : 2 * HEAD_DIM], axis=0, keepdims=True))
    bounded = jnp.maximum(first, second) < SAFE

    @pl.when(bounded)
    def _():
        total = jnp.zeros((144, 2 * rows), F32)
        for index in range(blocks):
            part = slice(index * KEY_BLOCK, (index + 1) * KEY_BLOCK)
            probs = jnp.exp2(dot(left_of(part), right[...])).astype(BF16)
            total = weigh(part, probs, total)
        store(total)

    @pl.when(jnp.logical_not(bounded))
    def _():
        def part_of(index):
            return pl.ds(pl.multiple_of(index * KEY_BLOCK, KEY_BLOCK), KEY_BLOCK)

        def score(index, top):
            part = part_of(index)
            current = dot(left_of(part), right[...])
            scores[part, :] = current
            return jnp.maximum(top, jnp.max(current.reshape(KEY_BLOCK // 8, 8, 2 * rows), axis=0))

        top = lax.fori_loop(0, blocks, score, jnp.full((8, 2 * rows), MASKED, F32))
        top = jnp.max(top, axis=0, keepdims=True)

        def shifted(index, total):
            part = part_of(index)
            return weigh(part, jnp.exp2(scores[part, :] - top).astype(BF16), total)

        store(lax.fori_loop(0, blocks, shifted, jnp.zeros((144, 2 * rows), F32)))


def attend(query, keys, values, marks, slots):
    width, rows = query.shape
    group = keys.shape[1]
    pairs = width // 128
    column = pl.BlockSpec((None, group, 128), lambda pair: (pair, 0, 0))
    return pl.pallas_call(
        forward_kernel,
        grid=(pairs,),
        in_specs=[
            pl.BlockSpec((128, rows), lambda pair: (pair, 0)),
            column,
            column,
            whole((group, 128)),
            whole((rows // 128, 128)),
        ],
        out_specs=[
            pl.BlockSpec((None, group, 2 * rows), lambda pair: (pair, 0, 0)),
            pl.BlockSpec((128, rows), lambda pair: (pair, 0)),
            pl.BlockSpec((1, 2, rows), lambda pair: (pair, 0, 0)),
        ],
        out_shape=[
            jax.ShapeDtypeStruct((pairs, group, 2 * rows), BF16),
            jax.ShapeDtypeStruct((width, rows), F32),
            jax.ShapeDtypeStruct((pairs, 2, rows), F32),
        ],
        scratch_shapes=[pltpu.VMEM((256, 2 * rows), BF16), pltpu.VMEM((group, 2 * rows), F32)],
        compiler_params=params(),
        name="attend",
    )(query, keys, values, marks, slots)


def feed_kernel(
    mixed_wide,
    inverse,
    stream,
    upstream,
    gain,
    shift,
    output_hbm,
    up_hbm,
    down_hbm,
    activation_out,
    middle_grad_out,
    norm_out,
    mixed_grad_out,
    row_out,
    output_grad_hbm,
    up_grad_hbm,
    down_grad_hbm,
    output_weight,
    up_weight,
    down_weight,
    output_grad,
    up_grad,
    down_grad,
    activation_sum,
    normed_sum,
    loads,
    stores,
):
    rows, width = stream.shape
    hidden_width = up_weight.shape[1]
    chunk = width
    chunks = hidden_width // chunk
    load_output = pltpu.make_async_copy(output_hbm, output_weight, loads.at[0])
    load_output.start()

    def load_parts(index):
        part = pl.ds(pl.multiple_of(index * chunk, 128), chunk)
        return (
            pltpu.make_async_copy(up_hbm.at[:, part], up_weight.at[:, part], loads.at[1 + 2 * index]),
            pltpu.make_async_copy(down_hbm.at[part], down_weight.at[part], loads.at[2 + 2 * index]),
        )

    def store_parts(index):
        y, c = lax.rem(index, 2), lax.div(index, 2)
        return (
            pltpu.make_async_copy(
                down_grad.at[:, :, :, index], down_grad_hbm.at[:, :, :, index], stores.at[1 + 2 * index]
            ),
            pltpu.make_async_copy(up_grad.at[c, y], up_grad_hbm.at[c, y], stores.at[2 + 2 * index]),
        )

    for index in range(chunks):
        for copy in load_parts(index):
            copy.start()
    mixed = mixed_wide[...].astype(BF16)
    load_output.wait()
    middle = stream[...] + dot(mixed, output_weight[...], 0, 0)
    unit, scale = norm_parts(middle)
    wide_gain = gain[...].reshape(1, width)
    normed = (unit * wide_gain + shift[...].reshape(1, width)).astype(BF16)
    normed_t = normed.T
    incoming = upstream[...]
    activation_sum[...] = middle
    normed_sum[...] = jnp.zeros((rows, width), F32)

    def step(index, carry):
        part = pl.ds(pl.multiple_of(index * chunk, 128), chunk)
        for copy in load_parts(index):
            copy.wait()
        pre = dot(normed, up_weight[:, part])
        cdf = 0.5 * (1.0 + lax.erf(pre * math.sqrt(0.5)))
        slope = cdf + pre * jnp.exp(-0.5 * pre * pre) * (1.0 / math.sqrt(2.0 * math.pi))
        hidden = (pre * cdf).astype(BF16)
        back = dot(incoming, down_weight[part, :], 1, 1)
        pre_grad = (back * slope).astype(BF16)
        activation_sum[...] += dot(hidden, down_weight[part, :])
        down_part = dot(hidden, incoming, 0, 0).astype(BF16).reshape(8, PIECE, width)
        for piece in range(8):
            down_grad[piece // 4, piece // 2 % 2, piece % 2, index] = down_part[piece]
        up_part = dot(normed_t, pre_grad).astype(BF16).reshape(4, 2, PIECE, width)
        for half in range(2):
            up_grad[lax.div(index, 2), lax.rem(index, 2), half] = up_part[:, half]
        for copy in store_parts(index):
            copy.start()
        normed_sum[...] += dot(pre_grad, up_weight[:, part], 1, 1)
        return carry

    lax.fori_loop(0, chunks, step, 0)
    activation = activation_sum[...]
    normed_grad = normed_sum[...]
    activation_out[...] = activation.astype(BF16)
    norm_out[0:1] = jnp.sum(normed_grad * unit, axis=0, keepdims=True)
    norm_out[1:2] = jnp.sum(normed_grad, axis=0, keepdims=True)
    middle_grad = incoming.astype(F32) + norm_back(normed_grad, wide_gain, unit, scale)
    middle_grad_out[...] = middle_grad
    middle_low = middle_grad.astype(BF16)
    output_part = dot(mixed, middle_low).astype(BF16).reshape(4, 2, PIECE, width)
    for half in range(2):
        output_grad[half] = output_part[:, half]
    store_output = pltpu.make_async_copy(output_grad, output_grad_hbm, stores.at[0])
    store_output.start()
    mixed_grad = dot(output_weight[...], middle_low, 1, 1).astype(BF16).astype(F32)
    for head in range(HEADS):
        part = slice(head * HEAD_DIM, (head + 1) * HEAD_DIM)
        factor = inverse[head // 2, head % 2 : head % 2 + 1]
        mixed_grad_out[part, :] = (mixed_grad[part] * factor).astype(BF16)
        row_out[head // 2, head % 2 : head % 2 + 1] = factor * jnp.sum(
            mixed_grad[part] * mixed_wide[part, :], axis=0, keepdims=True
        )
    store_output.wait()
    for index in range(chunks):
        for copy in store_parts(index):
            copy.wait()


def feed(mixed, inverse, stream, upstream, gain, shift, output_weight, up_weight, down_weight):
    rows, width = stream.shape
    hidden_width = up_weight.shape[1]
    vmem = pl.BlockSpec(memory_space=pltpu.VMEM)
    hbm = pl.BlockSpec(memory_space=pltpu.HBM)
    return pl.pallas_call(
        feed_kernel,
        in_specs=[vmem] * 6 + [hbm] * 3,
        out_specs=[vmem] * 5 + [hbm] * 3,
        out_shape=[
            jax.ShapeDtypeStruct((rows, width), BF16),
            jax.ShapeDtypeStruct((rows, width), F32),
            jax.ShapeDtypeStruct((2, width), F32),
            jax.ShapeDtypeStruct((width, rows), BF16),
            jax.ShapeDtypeStruct((HEADS // 2, 2, rows), F32),
            jax.ShapeDtypeStruct((2, 4, PIECE, width), BF16),
            jax.ShapeDtypeStruct(UNIT, BF16),
            jax.ShapeDtypeStruct(UNIT, BF16),
        ],
        scratch_shapes=[
            pltpu.VMEM((width, width), BF16),
            pltpu.VMEM((width, hidden_width), BF16),
            pltpu.VMEM((hidden_width, width), BF16),
            pltpu.VMEM((2, 4, PIECE, width), BF16),
            pltpu.VMEM(UNIT, BF16),
            pltpu.VMEM(UNIT, BF16),
            pltpu.VMEM((rows, width), F32),
            pltpu.VMEM((rows, width), F32),
            pltpu.SemaphoreType.DMA((9,)),
            pltpu.SemaphoreType.DMA((9,)),
        ],
        compiler_params=params(),
        name="feed",
    )(mixed, inverse, stream, upstream, gain, shift, output_weight, up_weight, down_weight)


class Plane:
    def __init__(self, unit, local, scratch):
        self.unit, self.local = unit, local
        self.one, self.two_a, self.two_b, self.three, self.sems = *scratch[:4], scratch[4:6]
        self.z, self.x, self.y, self.c = place()
        (self.core, self.across, self.along), _ = neighbours()
        self.half = self.three.shape[-1] // 2

    def chunk(self, step):
        return lax.rem(self.z + step, 4)

    def copy(self, slot, step):
        x, y, z, half = self.x, self.y, self.chunk(step), self.half
        left, right = pl.ds(0, half), pl.ds(half, half)
        sem = slot * 4 + step
        if slot == 0:
            source, target = self.unit.at[1 - self.c, :, :, z], self.one.at[:, :, z]
            return send(source, target, self.sems, sem, self.core)
        if slot == 1:
            source, target = self.one.at[:, 1 - x, z, :, left], self.two_a.at[:, z]
            return send(source, target, self.sems, sem, self.across)
        if slot == 2:
            source, target = self.one.at[1 - y, :, z, :, right], self.two_b.at[:, z]
            return send(source, target, self.sems, sem, self.along)
        if slot == 3:
            source, target = self.two_a.at[1 - y, z], self.three.at[z, :, left]
            return send(source, target, self.sems, sem, self.along)
        source, target = self.two_b.at[1 - x, z], self.three.at[z, :, right]
        return send(source, target, self.sems, sem, self.across)

    def begin(self, step):
        self.copy(0, step).start()

    def add_one(self, step):
        z = self.chunk(step)
        self.copy(0, step).wait_recv()
        for y in range(2):
            for x in range(2):
                self.one[y, x, z] = self.one[y, x, z] + self.local(y, x, z)
        self.copy(1, step).start()
        self.copy(2, step).start()

    def add_two_a(self, step):
        z = self.chunk(step)
        self.copy(1, step).wait_recv()
        for y in range(2):
            self.two_a[y, z] = self.two_a[y, z] + self.one[y, self.x, z, :, 0 : self.half]
        self.copy(3, step).start()

    def add_two_b(self, step):
        z = self.chunk(step)
        self.copy(2, step).wait_recv()
        for x in range(2):
            self.two_b[x, z] = self.two_b[x, z] + self.one[self.y, x, z, :, self.half : 2 * self.half]
        self.copy(4, step).start()

    def add_three(self, step):
        z, half = self.chunk(step), self.half
        self.copy(3, step).wait_recv()
        self.copy(4, step).wait_recv()
        self.three[z, :, 0:half] = self.three[z, :, 0:half] + self.two_a[self.y, z]
        right = slice(half, 2 * half)
        self.three[z, :, right] = self.three[z, :, right] + self.two_b[self.x, z]

    def finish(self):
        for slot in range(5):
            for step in range(4):
                self.copy(slot, step).wait_send()

    def actions(self, first):
        kinds = (self.begin, self.add_one, self.add_two_a, self.add_two_b, self.add_three)
        return {
            first + 4 * index + step: functools.partial(kind, step)
            for index, kind in enumerate(kinds)
            for step in range(4)
        }


def plane_buffers():
    _, _, _, zs, piece, width = UNIT
    return [
        pltpu.VMEM((2, 2, zs, piece, width), BF16),
        pltpu.VMEM((2, zs, piece, width // 2), BF16),
        pltpu.VMEM((2, zs, piece, width // 2), BF16),
        pltpu.VMEM((zs, piece, width), BF16),
        pltpu.SemaphoreType.DMA((20,)),
        pltpu.SemaphoreType.DMA((20,)),
    ]


class Line:
    def __init__(self, three, scratch, out):
        self.three, self.four, self.sems, self.out = three, scratch[0], scratch[1:3], out
        self.z, self.x, self.y, self.c = place()
        (self.core, self.across, self.along), self.planes = neighbours()
        self.half = three.shape[-1] // 2

    def copy(self, slot):
        x, y, c = self.x, self.y, self.c
        left, right = pl.ds(0, self.half), pl.ds(self.half, self.half)
        if slot < 3:
            target = lax.rem(self.z + slot + 1, 4)
            return send(self.three.at[target], self.four.at[slot], self.sems, slot, self.planes[slot])
        mine = self.out.at[c, y, x]
        if slot == 3:
            return send(mine, mine, self.sems, 3, self.across)
        if slot == 4:
            return send(mine, mine, self.sems, 4, self.along)
        if slot == 5:
            other = self.out.at[c, y, 1 - x, :, left]
            return send(other, other, self.sems, 5, self.along)
        if slot == 6:
            other = self.out.at[c, 1 - y, x, :, right]
            return send(other, other, self.sems, 6, self.across)
        return send(self.out.at[c], self.out.at[c], self.sems, 7, self.core)

    def begin(self, step):
        if step:
            self.copy(step - 1).start()

    def add(self):
        total = self.three[self.z].astype(F32)
        for slot in range(3):
            self.copy(slot).wait_recv()
            total = total + self.four[slot].astype(F32)
        self.out[self.c, self.y, self.x] = total.astype(BF16)
        self.copy(3).start()
        self.copy(4).start()

    def forward(self, slot):
        self.copy(slot).wait_recv()
        self.copy(slot + 2).start()

    def share(self):
        self.copy(5).wait_recv()
        self.copy(6).wait_recv()
        self.copy(7).start()

    def end(self):
        self.copy(7).wait_recv()

    def finish(self):
        for slot in range(8):
            self.copy(slot).wait_send()

    def actions(self, first):
        steps = {first + step: functools.partial(self.begin, step) for step in range(4)}
        forward_x, forward_y = (functools.partial(self.forward, slot) for slot in (3, 4))
        rest = (self.add, forward_x, forward_y, self.share, self.end)
        steps.update({first + 4 + 4 * index: step for index, step in enumerate(rest)})
        return steps


def line_buffers():
    _, _, _, _, piece, width = UNIT
    return [
        pltpu.VMEM((3, piece, width), BF16),
        pltpu.SemaphoreType.DMA((8,)),
        pltpu.SemaphoreType.DMA((8,)),
    ]


def back_kernel(
    linked,
    query,
    keys,
    values,
    marks,
    probs,
    mixed_grad,
    row_sums,
    query_hbm,
    key_hbm,
    value_hbm,
    down_unit,
    up_unit,
    query_back_hbm,
    key_back_hbm,
    value_back_hbm,
    normed_unit,
    down_out,
    up_out,
    left,
    right,
    query_back,
    key_back,
    value_back,
    query_weight,
    key_weight,
    value_weight,
    staged,
    loads,
    stores,
    pair_sems,
    *scratch,
):
    pair = pl.program_id(0)
    pairs = pl.num_programs(0) - 1
    width, rows = query_back.shape
    group = keys.shape[0]
    blocks = group // KEY_BLOCK
    owners = group // rows
    copies = [
        pltpu.make_async_copy(source, target, loads.at[index])
        for index, (source, target) in enumerate(
            ((query_hbm, query_weight), (key_hbm, key_weight), (value_hbm, value_weight))
        )
    ]
    steps = {}
    if linked:
        down_local, up_local = scratch[0:2]
        down = Plane(down_unit, lambda y, x, z: down_local[y, x, z], scratch[2:8])
        up = Plane(up_unit, lambda y, x, z: up_local[y, x, z], scratch[8:14])
        line = Line(down.three, scratch[14:17], scratch[17])
        seat = lax.rem(lax.axis_index("seq"), 2)
        locals_ = [
            pltpu.make_async_copy(down_unit.at[seat], down_local, loads.at[3]),
            pltpu.make_async_copy(up_unit.at[seat], up_local, loads.at[4]),
        ]
        down_store = pltpu.make_async_copy(scratch[17], down_out, stores.at[5])
        up_store = pltpu.make_async_copy(up.three, up_out, stores.at[6])

        steps = {
            GREET: lambda: greet(neighbours()[0] + neighbours()[1]),
            D_LOCAL: locals_[0].wait,
            U_LOCAL: locals_[1].wait,
        }
        steps.update(down.actions(D_CORE))
        steps.update(up.actions(U_CORE))
        steps.update(line.actions(D_SEND))

    def pair_stores(pair):
        column = pl.ds(pl.multiple_of(pair * 128, 128), 128)
        return [
            pltpu.make_async_copy(source.at[:, column], target.at[:, column], pair_sems.at[index, pair])
            for index, (source, target) in enumerate(
                ((key_back, key_back_hbm), (value_back, value_back_hbm))
            )
        ]

    def run(spot):
        if linked:
            for key in BACK_ORDER[spot]:
                steps[key]()

    @pl.when(pair == 0)
    def _():
        if linked:
            locals_[0].start()
        run(0)

    @pl.when(pair == 1)
    def _():
        if linked:
            locals_[1].start()

    @pl.when(pair == 3)
    def _():
        for copy in copies:
            copy.start()

    @pl.when(pair < pairs)
    def _():
        pair_columns(left, query, rows)
        pair_columns(right, mixed_grad, rows)
        kinds = lax.broadcasted_iota(jnp.int32, (128, rows), 0)
        shape = (128, rows)
        for half in range(2):
            total = -row_sums[0, half : half + 1]
            high = total.astype(BF16).astype(F32)
            fill = jnp.where(kinds == ONES, jnp.broadcast_to(high, shape), 0.0)
            fill = jnp.where(kinds == ONES + 1, jnp.broadcast_to(total - high, shape), fill)
            right[128:256, half * rows : (half + 1) * rows] = fill.astype(BF16)

        column = pl.ds(pl.multiple_of(pair * 128, 128), 128)

        def block(index, total):
            part = pl.ds(pl.multiple_of(index * KEY_BLOCK, KEY_BLOCK), KEY_BLOCK)
            weights = probs[part, :]
            inner = dot(jnp.concatenate([values[part, :], marks[part, :]], axis=1), right[...])
            score_grad = (weights.astype(F32) * inner).astype(BF16)
            key_back[part, column] = (dot(score_grad, left[...], 1, 1) * LN2).astype(BF16)
            value_back[part, column] = dot(weights, right[0:128, :], 1, 1).astype(BF16)
            return total + dot(keys[part, :].T, score_grad)

        total = lax.fori_loop(0, blocks, block, jnp.zeros((128, 2 * rows), F32), unroll=3)
        scale = HEAD_DIM**-0.5
        base = pl.multiple_of(pair * 128, 128)
        query_back[pl.ds(base, HEAD_DIM), :] = (total[0:HEAD_DIM, 0:rows] * scale).astype(BF16)
        base = pl.multiple_of(pair * 128 + HEAD_DIM, HEAD_DIM)
        query_back[pl.ds(base, HEAD_DIM), :] = (total[HEAD_DIM:128, rows : 2 * rows] * scale).astype(BF16)

        for copy in pair_stores(pair):
            copy.start()
        for spot in range(1, 7):
            if linked and BACK_ORDER[spot]:
                pl.when(pair == spot - 1)(functools.partial(run, spot))

    @pl.when(pair == pairs)
    def _():
        query_store = pltpu.make_async_copy(query_back, query_back_hbm, stores.at[2])
        query_store.start()
        for copy in copies:
            copy.wait()
        own = lax.axis_index("head") * lax.axis_size("seq") + lax.axis_index("seq")

        def owner_store(owner):
            x, y, c = lax.div(owner, 4), lax.rem(lax.div(owner, 2), 2), lax.rem(owner, 2)
            slot = lax.rem(owner, 2)
            return pltpu.make_async_copy(staged.at[slot], normed_unit.at[c, y, x], stores.at[slot])

        def owner_step(owner, carry):
            part = pl.ds(pl.multiple_of(owner * rows, 128), rows)
            slot = lax.rem(owner, 2)
            total = dot(key_back[part, :], key_weight[...], 1, 1)
            total = total + dot(value_back[part, :], value_weight[...], 1, 1)

            @pl.when(owner >= 2)
            def _():
                owner_store(owner).wait()

            staged[slot] = total.astype(BF16).reshape(4, PIECE, width)

            @pl.when(own == owner)
            def _():
                extra = dot(query_back[...], query_weight[...], 0, 1)
                staged[slot] = (total + extra).astype(BF16).reshape(4, PIECE, width)

            owner_store(owner).start()
            return carry

        lax.fori_loop(0, owners // 2, owner_step, 0)
        run(7)
        lax.fori_loop(owners // 2, owners, owner_step, 0)
        run(8)
        for slot in range(2):
            owner_store(slot).wait()
        if linked:
            up_store.start()
            up_store.wait()
            down_store.start()
            down_store.wait()
            down.finish()
            up.finish()
            line.finish()
        query_store.wait()
        for done in range(6):
            for copy in pair_stores(done):
                copy.wait()


def attend_back(linked, query, keys, values, marks, probs, mixed_grad, row_sums, wq, wk, wv, down_unit, up_unit):
    width, rows = query.shape
    group = keys.shape[1]
    pairs = width // 128
    held = lambda pair: jnp.minimum(pair, pairs - 1)
    column = pl.BlockSpec((None, group, 128), lambda pair: (held(pair), 0, 0))
    row = pl.BlockSpec((128, rows), lambda pair: (held(pair), 0))
    hbm = pl.BlockSpec(memory_space=pltpu.HBM)
    third = jax.ShapeDtypeStruct(UNIT[3:], BF16)
    more = dict(collective_id=1, has_side_effects=True) if linked else {}
    scratch = []
    if linked:
        scratch = [pltpu.VMEM(UNIT[1:], BF16)] * 2 + plane_buffers() * 2 + line_buffers()
        scratch += [pltpu.VMEM(UNIT[:3] + UNIT[4:], BF16)]
    return pl.pallas_call(
        functools.partial(back_kernel, linked),
        grid=(pairs + 1,),
        in_specs=[
            row,
            column,
            column,
            pl.BlockSpec((group, 128), lambda pair: (0, 0), pipeline_mode=pl.Buffered(1)),
            pl.BlockSpec((None, group, 2 * rows), lambda pair: (held(pair), 0, 0)),
            row,
            pl.BlockSpec((1, 2, rows), lambda pair: (held(pair), 0, 0)),
        ]
        + [hbm] * 5,
        out_specs=[hbm] * 6,
        out_shape=[
            jax.ShapeDtypeStruct((width, rows), BF16),
            jax.ShapeDtypeStruct((group, width), BF16),
            jax.ShapeDtypeStruct((group, width), BF16),
            jax.ShapeDtypeStruct(UNIT, BF16),
            jax.ShapeDtypeStruct(UNIT[:3] + UNIT[4:], BF16),
            third,
        ],
        scratch_shapes=[
            pltpu.VMEM((128, 2 * rows), BF16),
            pltpu.VMEM((256, 2 * rows), BF16),
            pltpu.VMEM((width, rows), BF16),
            pltpu.VMEM((group, width), BF16),
            pltpu.VMEM((group, width), BF16),
            pltpu.VMEM((width, width), BF16),
            pltpu.VMEM((width, width), BF16),
            pltpu.VMEM((width, width), BF16),
            pltpu.VMEM((2, 4, PIECE, width), BF16),
            pltpu.SemaphoreType.DMA((5,)),
            pltpu.SemaphoreType.DMA((7,)),
            pltpu.SemaphoreType.DMA((2, 6)),
        ]
        + scratch,
        compiler_params=params(**more),
        name="attend_back",
    )(query, keys, values, marks, probs, mixed_grad, row_sums, wq, wk, wv, down_unit, up_unit)


class Rows:
    def __init__(self, given, part, landed, out, sems):
        self.given, self.part, self.landed, self.out, self.sems = given, part, landed, out, sems
        self.z, self.x, self.y, self.c = place()
        (self.core, self.across, self.along), self.planes = neighbours()

    def index(self, x, y, c):
        return x * 4 + y * 2 + c

    def copy(self, slot):
        x, y, c = self.x, self.y, self.c
        size = self.given.shape[1] // 2
        mine = self.given.at[self.index(x, y, c)]
        if slot < 3:
            return send(mine, mine, self.sems, slot, (self.core, self.across, self.along)[slot])
        if slot == 3:
            other = self.given.at[self.index(1 - x, y, c), pl.ds(0, size)]
            return send(other, other, self.sems, 3, self.along)
        if slot == 4:
            other = self.given.at[self.index(x, 1 - y, c), pl.ds(size, size)]
            return send(other, other, self.sems, 4, self.across)
        if slot < 8:
            flip_x, flip_y = ((1, 0), (0, 1), (1, 1))[slot - 5]
            other = self.given.at[
                self.index(x + flip_x - 2 * flip_x * x, y + flip_y - 2 * flip_y * y, c)
            ]
            return send(other, other, self.sems, slot, self.core)
        if slot < 11:
            step = slot - 8
            return send(
                self.part.at[step + 1], self.landed.at[step], self.sems, slot, self.planes[step]
            )
        if slot < 14:
            mine = self.out.at[x, self.z]
            return send(mine, mine, self.sems, slot, self.planes[slot - 11])
        other = self.out.at[x, lax.rem(self.z + 18 - slot, 4)]
        return send(other, other, self.sems, slot, self.across)

    def start(self, *slots):
        for slot in slots:
            self.copy(slot).start()

    def landed_all(self, *slots):
        for slot in slots:
            self.copy(slot).wait_recv()

    def finish(self):
        for slot in range(18):
            self.copy(slot).wait_send()


class Small:
    def __init__(self, rows, entry, half_rows, half_entry, landings, out, entry_out, sems):
        self.rows, self.entry, self.half_rows, self.half_entry = rows, entry, half_rows, half_entry
        self.landings, self.out, self.entry_out, self.sems = landings, out, entry_out, sems
        self.z, self.x, self.y, self.c = place()
        (self.core, self.across, self.along), self.planes = neighbours()
        half = rows.shape[-1] // 2
        self.mine = pl.ds(pl.multiple_of(self.c * half, 128), half)
        self.away = pl.ds(pl.multiple_of((1 - self.c) * half, 128), half)

    def copy(self, slot):
        rows_land, entry_land, last = self.landings
        stage, kind = slot // 2, slot % 2
        if stage == 0:
            source = (self.rows.at[:, self.away], self.entry.at[:, :, self.away])[kind]
        else:
            source = (self.half_rows, self.half_entry)[kind]
        if stage < 3:
            target = (rows_land, entry_land)[kind].at[stage]
            return send(source, target, self.sems, slot, (self.core, self.across, self.along)[stage])
        if stage < 6:
            step = stage - 3
            if kind == 0:
                target = self.out.at[self.z, :, self.mine]
            else:
                source = self.half_entry.at[lax.rem(self.z + step + 1, 4)]
                target = last.at[step]
            return send(source, target, self.sems, slot, self.planes[step])
        part = (self.out.at[:, :, self.mine], self.entry_out.at[:, self.mine])[kind]
        return send(part, part, self.sems, slot, self.core)

    def start(self, stage):
        self.copy(2 * stage).start()
        self.copy(2 * stage + 1).start()

    def landed(self, stage):
        self.copy(2 * stage).wait_recv()
        self.copy(2 * stage + 1).wait_recv()

    def add(self, stage):
        rows_land, entry_land, _ = self.landings
        self.landed(stage)
        if stage == 0:
            self.half_rows[...] = self.rows[:, self.mine] + rows_land[0]
            self.half_entry[...] = self.entry[:, :, self.mine] + entry_land[0]
        else:
            self.sent(stage)
            self.half_rows[...] = self.half_rows[...] + rows_land[stage]
            self.half_entry[...] = self.half_entry[...] + entry_land[stage]
        if stage < 2:
            self.start(stage + 1)
        else:
            for step in (3, 4, 5):
                self.start(step)

    def sent(self, stage):
        self.copy(2 * stage).wait_send()
        self.copy(2 * stage + 1).wait_send()

    def collect(self):
        last = self.landings[2]
        self.out[self.z, :, self.mine] = self.half_rows[...]
        total = self.half_entry[self.z].astype(F32)
        for step in range(3):
            self.landed(3 + step)
            total = total + last[step].astype(F32)
        self.entry_out[:, self.mine] = total.astype(BF16)
        self.start(6)


def late_kernel(
    slots,
    tokens,
    stream,
    middle_grad,
    gain,
    embed_low,
    found,
    input_weight,
    second_norm,
    query_back,
    up_three,
    normed_hbm,
    key_back_hbm,
    value_back_hbm,
    output_hbm,
    normed_unit,
    embed_grad_out,
    table_out,
    small_out,
    entry_out,
    up_out,
    heads_out,
    normed,
    key_back,
    value_back,
    heads_unit,
    normed_local,
    given,
    part,
    part_landed,
    rows_own,
    entry_own,
    half_rows,
    half_entry,
    rows_land,
    entry_land,
    entry_last,
    loads,
    *scratch,
):
    z, x, y, c = place()
    own = x * 4 + y * 2 + c
    width = stream.shape[1]
    rows = stream.shape[0]
    near, planes = neighbours()
    normed_plane = Plane(normed_unit, lambda yy, xx, zz: normed_local[yy, xx, zz], scratch[0:6])
    heads_plane = Plane(heads_unit, lambda yy, xx, zz: heads_unit[c, yy, xx, zz], scratch[6:12])
    up = Line(up_three, scratch[12:15], up_out)
    heads = Line(heads_plane.three, scratch[15:18], heads_out)
    table = Rows(given, part, part_landed, table_out, scratch[18:20])
    small = Small(
        rows_own,
        entry_own,
        half_rows,
        half_entry,
        (rows_land, entry_land, entry_last),
        small_out,
        entry_out,
        scratch[20:22],
    )
    local = pltpu.make_async_copy(normed_unit.at[c], normed_local, loads.at[0])
    copies = [
        pltpu.make_async_copy(source, target, loads.at[1 + index])
        for index, (source, target) in enumerate(
            (
                (normed_hbm, normed),
                (key_back_hbm, key_back),
                (value_back_hbm, value_back),
                (output_hbm, heads_unit.at[0, 0]),
            )
        )
    ]
    kept = {}

    def load():
        for copy in copies:
            copy.start()

    def loaded():
        for index in (0, 1, 3):
            copies[index].wait()

    def keep(kind):
        if kind == 1:
            mine = pl.ds(pl.multiple_of(own * rows, 128), rows)
            value = dot(normed[:, mine], query_back[...], 1, 1)
        else:
            if kind == 3:
                copies[2].wait()
            value = dot(normed[...], (key_back, value_back)[kind - 2][...])
        value = value.astype(BF16).reshape(4, 2, PIECE, width)
        for half in range(2):
            heads_unit[kind // 2, kind % 2, half] = value[:, half]

    def norm():
        unit, scale = norm_parts(stream[...])
        incoming = normed_plane.three[...].reshape(rows, width).astype(F32)
        stream_grad = middle_grad[...] + norm_back(incoming, gain[...].reshape(1, width), unit, scale)
        embed_grad = dot(stream_grad.astype(BF16), input_weight[...], 1, 1)
        given[own] = embed_grad.astype(BF16)
        embed_grad_out[...] = embed_grad
        kept["unit"], kept["incoming"], kept["stream_grad"] = unit, incoming, stream_grad
        kept["embed_grad"] = embed_grad

    def norm_rest():
        unit, incoming, stream_grad = kept["unit"], kept["incoming"], kept["stream_grad"]
        stream_low = stream_grad.astype(BF16)
        entry_own[...] = dot(embed_low[...], stream_low, 0, 0).astype(BF16).reshape(4, 32, width)
        kinds = lax.broadcasted_iota(jnp.int32, (SLOTS, rows), 0)
        slot = jnp.concatenate([slots[line : line + 1, :] for line in range(rows // 128)], axis=1)
        picker = jnp.where(kinds == slot, 1.0, 0.0).astype(BF16)
        rest = (stream_grad - stream_low.astype(F32)).astype(BF16)
        rows_own[...] = dot(picker, stream_low) + dot(picker, rest)
        rows_own[DEAD : DEAD + 1] = jnp.sum(incoming * unit, axis=0, keepdims=True)
        rows_own[DEAD + 1 : DEAD + 2] = jnp.sum(incoming, axis=0, keepdims=True)
        rows_own[DEAD + 2 : DEAD + 4] = second_norm[...]
        inner = jnp.sum(kept["embed_grad"] * found[...].astype(F32), axis=0, keepdims=True)
        inner = jnp.sum(inner, axis=1, keepdims=True)
        rows_own[DEAD + 4 : DEAD + 5] = jnp.broadcast_to(inner, (1, width))

    def hot(step):
        size = part.shape[1]
        seq = y * 2 + c
        base = seq * (8 * size) + x * (4 * size) + lax.rem(z + step, 4) * size
        ids = lax.broadcasted_iota(jnp.int32, (size, 128), 0) + base
        hits = [
            jnp.where(ids == tokens[owner, line : line + 1, :], 1.0, 0.0).astype(BF16)
            for owner in range(8)
            for line in range(rows // 128)
        ]
        hits = jnp.concatenate(hits, axis=1)
        part[step] = dot(hits, given[...].reshape(8 * rows, 128)).astype(BF16)
        if step:
            table.start(7 + step)

    def table_add():
        total = part[0].astype(F32)
        for slot in (8, 9, 10):
            table.landed_all(slot)
            total = total + part_landed[slot - 8].astype(F32)
        table_out[x, z] = total.astype(BF16)
        table.start(11, 12, 13, 14)

    def table_forward(*slots):
        for slot in slots:
            table.landed_all(slot)
            table.start(slot + 4)

    def after(wait, *starts):
        table.landed_all(*wait)
        table.start(*starts)

    def hot_first():
        table.landed_all(0, 5, 6, 7)
        hot(1)

    steps = {
        GREET: lambda: greet(near + planes),
        X_LOCAL: local.wait,
        LOAD: load,
        LOADED: loaded,
        GRAD_Q: lambda: keep(1),
        GRAD_K: lambda: keep(2),
        GRAD_V: lambda: keep(3),
        NORM: norm,
        NORM_REST: norm_rest,
        T_FIRST: lambda: table.start(0, 1, 2),
        T_PASS_X: lambda: after((1,), 3),
        T_PASS_Y: lambda: after((2,), 4),
        T_CORE: lambda: after((3, 4), 5, 6, 7),
        T_ROWS: hot_first,
        T_ROWS + 1: lambda: hot(2),
        T_ROWS + 2: lambda: hot(3),
        T_ROWS + 3: lambda: hot(0),
        T_SUM: table_add,
        T_PASS: lambda: table_forward(11, 12, 13),
        T_END: lambda: table.landed_all(14, 15, 16, 17),
        S_FIRST: lambda: small.start(0),
        S_CORE: lambda: small.add(0),
        S_X: lambda: small.add(1),
        S_Y: lambda: small.add(2),
        S_COLLECT: small.collect,
        S_END: lambda: small.landed(6),
    }
    steps.update(normed_plane.actions(X_CORE))
    steps.update(heads_plane.actions(H_CORE))
    steps.update(up.actions(U_SEND))
    steps.update(heads.actions(H_SEND))
    local.start()
    for key in LATE_ORDER:
        steps[key]()
    small.sent(0)
    for stage in (3, 4, 5, 6):
        small.sent(stage)
    table.finish()
    normed_plane.finish()
    heads_plane.finish()
    up.finish()
    heads.finish()


def late(
    slots,
    tokens,
    stream,
    middle_grad,
    gain,
    embed_low,
    found,
    input_weight,
    second_norm,
    query_back,
    up_three,
    normed,
    key_back,
    value_back,
    output_part,
    normed_unit,
):
    rows, width = stream.shape
    group = key_back.shape[0]
    quarter = VOCAB // 4 // 8
    vmem = pl.BlockSpec(memory_space=pltpu.VMEM)
    hbm = pl.BlockSpec(memory_space=pltpu.HBM)
    done = jax.ShapeDtypeStruct((2, 2, 2, PIECE, width), BF16)
    pair = lambda count: [pltpu.SemaphoreType.DMA((count,)), pltpu.SemaphoreType.DMA((count,))]
    return pl.pallas_call(
        late_kernel,
        in_specs=[vmem] * 11 + [hbm] * 5,
        out_specs=[vmem] * 6,
        out_shape=[
            jax.ShapeDtypeStruct((rows, 128), F32),
            jax.ShapeDtypeStruct((2, 4, quarter, 128), BF16),
            jax.ShapeDtypeStruct((4, 32, width), F32),
            jax.ShapeDtypeStruct((32, width), BF16),
            done,
            done,
        ],
        scratch_shapes=[
            pltpu.VMEM((width, group), BF16),
            pltpu.VMEM((group, width), BF16),
            pltpu.VMEM((group, width), BF16),
            pltpu.VMEM(UNIT, BF16),
            pltpu.VMEM(UNIT[1:], BF16),
            pltpu.VMEM((8, rows, 128), BF16),
            pltpu.VMEM((4, quarter, 128), BF16),
            pltpu.VMEM((3, quarter, 128), BF16),
            pltpu.VMEM((32, width), F32),
            pltpu.VMEM((4, 32, width), BF16),
            pltpu.VMEM((32, width // 2), F32),
            pltpu.VMEM((4, 32, width // 2), BF16),
            pltpu.VMEM((3, 32, width // 2), F32),
            pltpu.VMEM((3, 4, 32, width // 2), BF16),
            pltpu.VMEM((3, 32, width // 2), BF16),
            pltpu.SemaphoreType.DMA((5,)),
        ]
        + plane_buffers() * 2
        + line_buffers() * 2
        + pair(18)
        + pair(14),
        compiler_params=params(collective_id=2, has_side_effects=True),
        name="late",
    )(
        slots,
        tokens,
        stream,
        middle_grad,
        gain,
        embed_low,
        found,
        input_weight,
        second_norm,
        query_back,
        up_three,
        normed,
        key_back,
        value_back,
        output_part,
        normed_unit,
    )


def finish_kernel(
    embed_grad,
    table_sum,
    small,
    entry,
    down,
    up,
    heads,
    table,
    mean_norm,
    hidden,
    acts,
    features,
    second_weight,
    embed_out,
    table_out,
    entry_out,
    first_out,
    second_out,
    gain_one,
    shift_one,
    query_out,
    key_out,
    value_out,
    output_out,
    gain_two,
    shift_two,
    up_out,
    down_out,
):
    width = second_weight.shape[0]
    embed_out[...] = embed_grad[...]
    entry_out[...] = entry[...].astype(F32)
    for piece in range(8):
        c, y, x = piece // 4, (piece // 2) % 2, piece % 2
        down_out[piece * PIECE : (piece + 1) * PIECE, :] = down[c, y, x].astype(F32)
        quarter = piece // 2
        up_out[x * PIECE : (x + 1) * PIECE, quarter * width : (quarter + 1) * width] = up[c, y, x].astype(F32)
        target = (output_out, query_out, key_out, value_out)[quarter]
        target[x * PIECE : (x + 1) * PIECE, :] = heads[c, y, x].astype(F32)
    totals = small[0, DEAD : DEAD + 5]
    for plane in range(1, small.shape[0]):
        totals = totals + small[plane, DEAD : DEAD + 5]
    gain_one[...] = totals[0:1].reshape(width)
    shift_one[...] = totals[1:2].reshape(width)
    gain_two[...] = totals[2:3].reshape(width)
    shift_two[...] = totals[3:4].reshape(width)
    mean = mean_norm[0:1]
    inverse = 1.0 / mean
    mean_grad = -totals[4:5, 0:128] * inverse * inverse * (1.0 / VOCAB)
    wide = table[...].astype(F32)
    norms = jnp.sqrt(jnp.sum(wide * wide, axis=1, keepdims=True))
    sums = table_sum[...].reshape(table.shape).astype(F32)
    table_out[...] = sums * inverse + mean_grad * (wide / norms)
    tog = jnp.concatenate([small[plane, 0:SLOTS] for plane in range(small.shape[0])], axis=0)
    plane = lax.axis_index("dp")

    def rows_of(array, count):
        return array[pl.ds(pl.multiple_of(plane * count, 8), count), :]

    second_out[...] = lax.dot_general(
        rows_of(acts, second_out.shape[0]),
        tog,
        (((1,), (0,)), ((), ())),
        precision=lax.Precision.HIGHEST,
        preferred_element_type=F32,
    )
    high = tog.astype(BF16)
    rest = (tog - high.astype(F32)).astype(BF16)
    act_grad = dot(high, second_weight[...], 1, 1) + dot(rest, second_weight[...], 1, 1)
    value = hidden[...]
    gate = 1.0 / (1.0 + jnp.exp(-value))
    hidden_grad = act_grad * (gate * (1.0 + value * (1.0 - gate)))
    first_out[...] = lax.dot_general(
        rows_of(features, first_out.shape[0]),
        hidden_grad,
        (((1,), (0,)), ((), ())),
        precision=lax.Precision.HIGHEST,
        preferred_element_type=F32,
    )


def finish(embed_grad, table_sum, small, entry, down, up, heads, table, mean_norm, hidden, acts, features, second_weight):
    rows = embed_grad.shape[0]
    width = second_weight.shape[0]
    wide = lambda *shape: jax.ShapeDtypeStruct(shape, F32)
    shard = width // 4
    return pl.pallas_call(
        finish_kernel,
        out_shape=[
            wide(rows, 128),
            wide(*table.shape),
            wide(32, width),
            wide(features.shape[0] // 4, width),
            wide(acts.shape[0] // 4, width),
            wide(width),
            wide(width),
            wide(shard, width),
            wide(shard, width),
            wide(shard, width),
            wide(shard, width),
            wide(width),
            wide(width),
            wide(shard, 4 * width),
            wide(width, width),
        ],
        compiler_params=params(),
        name="finish",
    )(embed_grad, table_sum, small, entry, down, up, heads, table, mean_norm, hidden, acts, features, second_weight)


def body(
    tokens,
    segments,
    live_lengths,
    timesteps,
    table,
    input_weight,
    time_first,
    time_second,
    first_gain,
    first_shift,
    query_weight,
    key_weight,
    value_weight,
    output_weight,
    second_gain,
    second_shift,
    up_weight,
    down_weight,
    upstream,
):
    blocks = lax.axis_size("head") * lax.axis_size("seq")
    planes = lax.axis_size("dp")
    rows = tokens.shape[0]
    width = query_weight.shape[0]
    shard_rows = table.shape[0]
    slot_count = live_lengths.shape[1]
    highest = lax.Precision.HIGHEST
    plane = lax.axis_index("dp")
    seq_index = lax.axis_index("seq")
    own = lax.axis_index("head") * lax.axis_size("seq") + seq_index
    linked = planes == 4

    slot_rows = segments.reshape(rows // 128, 128)
    full_table, notes_all, mean_norm, entry, time_hidden, acts, features = gather(
        table,
        tokens.reshape(rows // 128, 128),
        slot_rows,
        timesteps,
        live_lengths,
        input_weight,
        time_first,
        time_second,
    )
    normed, keys, values, marks, stream, query, embed_low, found = embed(
        own[None],
        notes_all,
        mean_norm,
        full_table,
        entry,
        first_gain,
        first_shift,
        query_weight,
        key_weight,
        value_weight,
        rows,
        blocks,
    )
    probs, mixed, inverse = attend(query, keys, values, marks, slot_rows)
    activation, middle_grad, second_norm, mixed_grad, row_sums, output_part, up_unit, down_unit = feed(
        mixed,
        inverse,
        stream,
        upstream,
        second_gain,
        second_shift,
        output_weight,
        up_weight,
        down_weight,
    )
    query_back, key_back, value_back, normed_unit, down_sum, up_three = attend_back(
        linked,
        query,
        keys,
        values,
        marks,
        probs,
        mixed_grad,
        row_sums,
        query_weight,
        key_weight,
        value_weight,
        down_unit,
        up_unit,
    )
    if linked:
        embed_grad, table_sum, small, entry_sum, up_sum, heads_sum = late(
            slot_rows,
            notes_all,
            stream,
            middle_grad,
            first_gain,
            embed_low,
            found,
            input_weight,
            second_norm,
            query_back,
            up_three,
            normed,
            key_back,
            value_back,
            output_part,
            normed_unit,
        )
        outs = finish(
            embed_grad,
            table_sum,
            small,
            entry_sum,
            down_sum,
            up_sum,
            heads_sum,
            table,
            mean_norm,
            time_hidden,
            acts,
            features,
            time_second,
        )
        return (activation, *outs)

    output_grad = output_part.transpose(1, 0, 2, 3).reshape(width, width)
    query_grad = dot(lax.dynamic_slice_in_dim(normed, own * rows, rows, axis=1), query_back, 1, 1)
    key_grad = dot(normed, key_back)
    value_grad = dot(normed, value_back)
    down_grad = down_unit.transpose(3, 0, 1, 2, 4, 5).reshape(-1, width)
    up_grad = up_unit.transpose(3, 2, 4, 0, 1, 5).reshape(width, -1)
    normed_grad = lax.psum_scatter(
        normed_unit.transpose(2, 1, 0, 3, 4, 5).reshape(-1, width),
        ("head", "seq"),
        scatter_dimension=0,
        tiled=True,
    ).astype(F32)
    mean_norm = mean_norm[0, 0]
    features = lax.dynamic_slice_in_dim(features.T, plane * SLOTS, slot_count)
    time_hidden = lax.dynamic_slice_in_dim(time_hidden, plane * SLOTS, slot_count)
    time_act = lax.dynamic_slice_in_dim(acts.T, plane * SLOTS, slot_count)
    second_wide = time_second.astype(F32)

    def one_norm(values, gain, shift):
        unit, _ = norm_parts(values)
        return unit * gain + shift

    _, first_back = jax.vjp(one_norm, stream, first_gain, first_shift)
    stream_part, first_gain_grad, first_shift_grad = first_back(normed_grad)
    stream_grad = middle_grad + stream_part
    stream_low = stream_grad.astype(BF16)
    input_grad = dot(embed_low, stream_low, 0, 0)
    embed_grad = dot(stream_low, input_weight, 1, 1)
    picker = (segments[:, None] == jnp.arange(slot_count, dtype=jnp.int32)[None, :]).astype(F32)
    time_out_grad = contract_exact(picker, stream_grad)
    time_second_grad = contract_exact(time_act, time_out_grad)
    act_grad = lax.dot_general(
        time_out_grad, second_wide, (((1,), (1,)), ((), ())), precision=highest
    )
    _, silu_back = jax.vjp(jax.nn.silu, time_hidden)
    time_hidden_grad = silu_back(act_grad)[0]
    time_first_grad = contract_exact(features, time_hidden_grad)

    def reduce(value):
        part = lax.psum_scatter(value.astype(BF16), "dp", scatter_dimension=0, tiled=True)
        return lax.psum(part, ("head", "seq")).astype(F32)

    shards = [
        reduce(value)
        for value in (
            input_grad,
            time_first_grad,
            time_second_grad,
            query_grad,
            key_grad,
            value_grad,
            output_grad,
            up_grad,
            down_grad,
        )
    ]
    mean_part = -jnp.sum(embed_grad * found.astype(F32)) / (mean_norm * mean_norm)
    scaled_grad = embed_grad / mean_norm
    table_sum = jax.ops.segment_sum(scaled_grad, tokens, num_segments=VOCAB)
    small = lax.psum(
        (first_gain_grad, first_shift_grad, second_norm[0], second_norm[1], mean_part, table_sum),
        ("dp", "head", "seq"),
    )
    table_rows = lax.dynamic_slice_in_dim(small[5], seq_index * shard_rows, shard_rows)
    table_wide = table.astype(F32)
    row_norms = jnp.sqrt(jnp.sum(table_wide * table_wide, axis=1))
    table_grad = table_rows + small[4] / VOCAB * table_wide / row_norms[:, None]
    return (
        activation,
        embed_grad,
        table_grad,
        shards[0],
        shards[1],
        shards[2],
        small[0],
        small[1],
        shards[3],
        shards[4],
        shards[5],
        shards[6],
        small[2],
        small[3],
        shards[7],
        shards[8],
    )


def solution(mesh):
    tokens = P(("dp", "head", "seq"))
    wide = P(("dp", "head", "seq"), None)
    group = P("dp", None)
    return jax.shard_map(
        body,
        mesh=mesh,
        in_specs=(tokens, tokens, group, group, P("seq", None)) + (P(),) * 13 + (wide,),
        out_specs=(wide, wide, P("seq", None), group, group, group, P(), P())
        + (group,) * 4
        + (P(), P(), group, group),
        check_vma=False,
    )
```

```python
import functools
import math

import jax
import jax.numpy as jnp
from jax import lax
from jax.experimental import pallas as pl
from jax.experimental.pallas import tpu as pltpu
from jax.sharding import PartitionSpec as P

HEADS = 12
HEAD_DIM = 64
VOCAB = 8192
EPSILON = 1e-05
MASKED = -1e30
LOG2E = math.log2(math.e)
LN2 = math.log(2.0)
KEY_BLOCK = 1024
SLOTS = 32
DEAD = 25
ONES = 32
VMEM_LIMIT = 60 * 2**20
SAFE = 60.0
PIECE = 96
UNIT = (2, 2, 2, 4, PIECE, 768)
MESH = pl.DeviceIdType.MESH

(
    GREET,
    D_LOCAL,
    U_LOCAL,
    X_LOCAL,
    LOAD,
    LOADED,
    GRAD_Q,
    GRAD_K,
    GRAD_V,
    NORM,
    NORM_REST,
    D_CORE,
    D_ONE,
    D_LEFT,
    D_RIGHT,
    D_THREE,
    U_CORE,
    U_ONE,
    U_LEFT,
    U_RIGHT,
    U_THREE,
    X_CORE,
    X_ONE,
    X_LEFT,
    X_RIGHT,
    X_THREE,
    H_CORE,
    H_ONE,
    H_LEFT,
    H_RIGHT,
    H_THREE,
    D_SEND,
    D_SUM,
    D_PASS_X,
    D_PASS_Y,
    D_SHARE,
    D_END,
    U_SEND,
    U_SUM,
    U_PASS_X,
    U_PASS_Y,
    U_SHARE,
    U_END,
    H_SEND,
    H_SUM,
    H_PASS_X,
    H_PASS_Y,
    H_SHARE,
    H_END,
    T_FIRST,
    T_PASS_X,
    T_PASS_Y,
    T_CORE,
    T_ROWS,
    T_SUM,
    T_PASS,
    T_END,
    S_FIRST,
    S_CORE,
    S_X,
    S_Y,
    S_COLLECT,
    S_END,
) = range(0, 252, 4)

BACK_ORDER = (
    (
        GREET, D_CORE + 1, D_CORE + 2, D_CORE,
    ),
    (
        D_LOCAL, D_ONE + 2, U_CORE + 2, U_CORE + 3, U_CORE + 1, D_CORE + 3, D_ONE + 1, D_ONE, U_CORE,
    ),
    (
        D_LEFT + 2, U_LOCAL, D_ONE + 3, D_RIGHT + 2, D_RIGHT + 1, D_LEFT + 1, U_ONE + 1,
    ),
    (
        D_LEFT, D_RIGHT, D_LEFT + 3, D_THREE + 2, D_SEND + 2, D_RIGHT + 3, U_ONE + 2, U_ONE + 3, U_ONE,
        D_THREE + 1, D_SEND + 1,
    ),
    (
        U_LEFT + 1, D_THREE + 3, D_SEND + 3, D_THREE, U_RIGHT + 1,
    ),
    (
        D_SUM, U_LEFT + 3, U_RIGHT + 3,
    ),
    (
        D_PASS_X, D_PASS_Y, U_THREE + 1, U_LEFT + 2, U_LEFT, U_RIGHT + 2, U_RIGHT,
    ),
    (
        U_THREE + 3, D_SHARE,
    ),
    (
        U_THREE + 2, U_THREE, D_END,
    ),
)
LATE_ORDER = (
    GREET, X_CORE, X_CORE + 1, X_CORE + 2, X_CORE + 3, LOAD, X_LOCAL, X_ONE, X_ONE + 1,
    U_SEND + 1, U_SEND + 2, U_SEND + 3, X_ONE + 2, LOADED, GRAD_K, X_LEFT, X_RIGHT, X_ONE + 3, GRAD_V,
    X_RIGHT + 1, X_LEFT + 1, GRAD_Q, X_THREE, H_CORE, X_RIGHT + 2, X_LEFT + 2, H_CORE + 2, X_LEFT + 3,
    X_RIGHT + 3, H_CORE + 1, X_THREE + 1, H_ONE + 2, X_THREE + 2, X_THREE + 3, H_ONE + 1, NORM, H_CORE + 3,
    H_LEFT + 2, H_RIGHT + 2, T_FIRST, NORM_REST, H_RIGHT + 1, H_LEFT + 1, S_FIRST, H_THREE + 2, H_SEND + 2, T_PASS_X,
    T_PASS_Y, H_ONE + 3, H_ONE, H_THREE + 1, H_SEND + 1, T_CORE, T_ROWS, H_RIGHT + 3, H_LEFT + 3, T_ROWS + 1,
    T_ROWS + 2, H_LEFT, S_CORE, H_RIGHT, U_SUM, H_THREE + 3, H_SEND + 3, T_ROWS + 3, T_SUM, S_X,
    H_THREE, H_SUM, S_Y, U_PASS_X, U_PASS_Y, H_PASS_Y, T_PASS, H_PASS_X, U_SHARE, H_SHARE, S_COLLECT,
    U_END, H_END, S_END, T_END,
)

F32 = jnp.float32
BF16 = jnp.bfloat16


def dot(left, right, left_dim=1, right_dim=0):
    return lax.dot_general(
        left, right, (((left_dim,), (right_dim,)), ((), ())), preferred_element_type=F32
    )


def contract_exact(left, right):
    return lax.dot_general(left, right, (((0,), (0,)), ((), ())), precision=lax.Precision.HIGHEST)


def whole(shape):
    return pl.BlockSpec(shape, lambda *_: (0,) * len(shape))


def params(**more):
    return pltpu.CompilerParams(vmem_limit_bytes=VMEM_LIMIT, **more)


def norm_parts(values):
    centre = values - jnp.mean(values, axis=-1, keepdims=True)
    spread = jnp.mean(centre * centre, axis=-1, keepdims=True)
    scale = lax.rsqrt(spread + EPSILON)
    return centre * scale, scale


def norm_back(incoming, gain, unit, scale):
    scaled = incoming * gain
    inner = scaled - jnp.mean(scaled, axis=-1, keepdims=True)
    return scale * (inner - unit * jnp.mean(scaled * unit, axis=-1, keepdims=True))


def place():
    seq = lax.axis_index("seq")
    return lax.axis_index("dp"), lax.axis_index("head"), lax.div(seq, 2), lax.rem(seq, 2)


def device(z, x, y, c):
    return (z, x, y * 2 + c)


def neighbours():
    z, x, y, c = place()
    planes = lax.axis_size("dp")
    near = [device(z, x, y, 1 - c), device(z, 1 - x, y, c), device(z, x, 1 - y, c)]
    return near, [device(lax.rem(z + step, planes), x, y, c) for step in range(1, planes)]


def greet(devices):
    barrier = pltpu.get_barrier_semaphore()
    for other in devices:
        pl.semaphore_signal(barrier, inc=1, device_id=other, device_id_type=MESH)
    pl.semaphore_wait(barrier, len(devices))


def send(source, target, sems, slot, other):
    return pltpu.make_async_remote_copy(
        src_ref=source,
        dst_ref=target,
        send_sem=sems[0].at[slot],
        recv_sem=sems[1].at[slot],
        device_id=other,
        device_id_type=MESH,
    )


def column_of(row):
    size = row.shape[1]
    shape = (size, size)
    same = lax.broadcasted_iota(jnp.int32, shape, 0) == lax.broadcasted_iota(jnp.int32, shape, 1)
    return jnp.sum(jnp.where(same, jnp.broadcast_to(row, shape), 0.0), axis=1, keepdims=True)


def split_three(values):
    high = values.astype(BF16)
    rest = values - high.astype(F32)
    middle = rest.astype(BF16)
    return high, middle, (rest - middle.astype(F32)).astype(BF16)


def dot_three(left, right):
    return sum(dot(part, right) for part in split_three(left))


def gather_kernel(
    table,
    tokens,
    segments,
    timesteps,
    lengths,
    input_weight,
    first_weight,
    second_weight,
    full,
    notes_all,
    mean_out,
    entry_out,
    hidden_out,
    acts_out,
    features_out,
    steps_all,
    acts,
    sums,
    local,
    *sems,
):
    z, x, y, c = place()
    seq = y * 2 + c
    own = x * 4 + seq
    near, planes = neighbours()
    others = []
    for flip in range(1, 8):
        xx, yy, cc = flip // 4, (flip // 2) % 2, flip % 2
        others.append(device(z, x + xx - 2 * xx * x, y + yy - 2 * yy * y, c + cc - 2 * cc * c))
    slot_count = timesteps.shape[1]
    notes_all[own, 0:3] = tokens[...]
    notes_all[own, 3:6] = segments[...]
    notes_all[own, 6:8] = jnp.zeros((2, 128), jnp.int32)
    notes_all[own, 6:7, 0:slot_count] = timesteps[...]
    notes_all[own, 7:8, 0:slot_count] = lengths[...]
    notes = notes_all.at[own]
    greet(others + planes)
    keep = pltpu.make_async_copy(table, full.at[seq], local.at[0])
    keep.start()
    tables = [
        send(table, full.at[seq], sems, 0, near[2]),
        send(table, full.at[seq], sems, 1, near[0]),
    ]
    for copy in tables:
        copy.start()
    copies = [send(notes, notes, sems, 3 + index, other) for index, other in enumerate(others)]
    steps = [
        send(notes, steps_all.at[z], sems, 13 + index, other) for index, other in enumerate(planes)
    ]
    for copy in copies + steps:
        copy.start()
    wide = table[...].astype(F32)
    norms = jnp.sqrt(jnp.sum(wide * wide, axis=1, keepdims=True))
    total = jnp.sum(norms, axis=0, keepdims=True)
    sums[seq] = jnp.broadcast_to(total, (8, 128))
    partials = [
        send(sums.at[seq], sums.at[seq], sems, 10 + index, other)
        for index, other in enumerate((near[0], near[2], device(z, x, 1 - y, 1 - c)))
    ]
    for copy in partials:
        copy.start()
    for copy in steps:
        copy.wait()
    steps_all[z] = notes_all[own]

    count = steps_all.shape[0]
    half = features_out.shape[0] // 2
    lanes = lax.broadcasted_iota(jnp.int32, (SLOTS, 2 * half), 1)
    slots = lax.broadcasted_iota(jnp.int32, (SLOTS, 2 * half), 0)
    freqs = jnp.exp((-math.log(10000.0)) * jnp.where(lanes < half, lanes, lanes - half).astype(F32) / half)
    parts = []
    for plane in range(count):
        angles = column_of(steps_all[plane, 6:7].astype(F32))[0:SLOTS] * freqs
        waves = jnp.where(lanes < half, jnp.cos(angles), jnp.sin(angles))
        parts.append(jnp.where(slots < slot_count, waves, 0.0))
    features = jnp.concatenate(parts, axis=0)
    features_out[...] = features.T
    hidden = dot_three(features, first_weight[...])
    hidden_out[...] = hidden
    act = hidden / (1.0 + jnp.exp(-hidden))
    acts[...] = act
    acts_out[...] = act.T
    time_rows = dot_three(acts[pl.ds(pl.multiple_of(z * SLOTS, SLOTS), SLOTS), :], second_weight[...])
    entry_out[0:128] = input_weight[...]
    for index, part in enumerate(split_three(time_rows)):
        entry_out[128 + index * SLOTS : 128 + (index + 1) * SLOTS] = part
    entry_out[128 + 3 * SLOTS : 256] = jnp.zeros((128 - 3 * SLOTS, entry_out.shape[1]), BF16)

    for copy in copies + partials:
        copy.wait()
    mean_out[...] = jnp.sum(sums[...], axis=0) * (1.0 / VOCAB)
    tables[0].wait_recv()
    away = (1 - y) * 2 + c
    forward = send(full.at[away], full.at[away], sems, 2, near[0])
    forward.start()
    keep.wait()
    tables[1].wait_recv()
    forward.wait()
    for copy in tables:
        copy.wait_send()


def gather(table, tokens, segments, timesteps, lengths, input_weight, first_weight, second_weight):
    rows, _ = table.shape
    width = input_weight.shape[1]
    planes = lax.axis_size("dp")
    vmem = pl.BlockSpec(memory_space=pltpu.VMEM)
    hbm = pl.BlockSpec(memory_space=pltpu.HBM)
    slots = 13 + planes - 1
    return pl.pallas_call(
        gather_kernel,
        in_specs=[vmem] * 8,
        out_specs=[hbm] + [vmem] * 6,
        out_shape=[
            jax.ShapeDtypeStruct((4, rows, 128), BF16),
            jax.ShapeDtypeStruct((8, 8, 128), jnp.int32),
            jax.ShapeDtypeStruct((8, 128), F32),
            jax.ShapeDtypeStruct((256, width), BF16),
            jax.ShapeDtypeStruct((planes * SLOTS, width), F32),
            jax.ShapeDtypeStruct((width, planes * SLOTS), F32),
            jax.ShapeDtypeStruct((first_weight.shape[0], planes * SLOTS), F32),
        ],
        scratch_shapes=[
            pltpu.VMEM((planes, 8, 128), jnp.int32),
            pltpu.VMEM((planes * SLOTS, width), F32),
            pltpu.VMEM((4, 8, 128), F32),
            pltpu.SemaphoreType.DMA((1,)),
            pltpu.SemaphoreType.DMA((slots,)),
            pltpu.SemaphoreType.DMA((slots,)),
        ],
        compiler_params=params(collective_id=0, has_side_effects=True),
        name="gather",
    )(table, tokens, segments, timesteps, lengths, input_weight, first_weight, second_weight)


def embed_kernel(
    own,
    tokens,
    notes,
    mean_norm,
    table_low,
    entry,
    gain,
    shift,
    query_weight,
    key_weight,
    value_weight,
    normed_out,
    key_out,
    value_out,
    mark_out,
    stream_out,
    query_out,
    low_out,
    found_out,
    picked,
    limits,
    table,
):
    step = pl.program_id(0)
    blocks = pl.num_programs(0)
    rows = picked.shape[1]
    width = stream_out.shape[1]
    block = lax.rem(own[0] + step, blocks)
    base = block * rows

    @pl.when(step == 0)
    def _():
        kinds = lax.broadcasted_iota(jnp.int32, (128, 128), 0)
        below = jnp.zeros((128, 128), F32)
        for part in range(blocks if isinstance(blocks, int) else 8):
            for line in range(3, 6):
                below = below + jnp.where(notes[part, line : line + 1, :] < kinds, 1.0, 0.0)
        starts = jnp.sum(below, axis=1, keepdims=True)
        shape = (128, 128)
        same = lax.broadcasted_iota(jnp.int32, shape, 0) == lax.broadcasted_iota(jnp.int32, shape, 1)
        starts = jnp.sum(jnp.where(same, jnp.broadcast_to(starts, shape), 0.0), axis=0, keepdims=True)
        limits[...] = starts + notes[own[0], 7:8, :].astype(F32)
        for part in range(4):
            table[part * 2048 : (part + 1) * 2048, :] = table_low[part].astype(F32)

    def pick(slot, source, row):
        line, lane = row // 128, row % 128
        picked[slot, pl.ds(row, 1), :] = table[pl.ds(tokens[source, line, lane], 1), :]

    @pl.when(step == 0)
    def _():
        def pick_some(index, carry):
            for inner in range(32):
                pick(0, block, index * 32 + inner)
            return carry

        lax.fori_loop(0, rows // 32, pick_some, 0)

    found = picked[lax.rem(step, 2)]
    low = (found / mean_norm[0:1]).astype(BF16)
    following = lax.rem(block + 1, blocks)
    for row in range(rows):
        pick(lax.rem(step + 1, 2), following, row)
    lanes = lax.broadcasted_iota(jnp.int32, (rows, 128), 1)
    slot = jnp.concatenate(
        [column_of(notes[block, line : line + 1, :].astype(F32)) for line in range(3, 6)], axis=0
    )
    same = jnp.where((lanes & (SLOTS - 1)).astype(F32) == slot, 1.0, 0.0)
    spread = jnp.where(lanes < 3 * SLOTS, same, 0.0).astype(BF16)
    stream = dot(jnp.concatenate([low, spread], axis=1), entry[...])
    unit, _ = norm_parts(stream)
    normed = (unit * gain[...].reshape(1, width) + shift[...].reshape(1, width)).astype(BF16)
    normed_out[...] = normed.T
    for weight, target in ((key_weight, key_out), (value_weight, value_out)):
        result = dot(normed, weight[...]).astype(BF16)
        for pair in range(width // 128):
            target[pair] = result[:, pair * 128 : (pair + 1) * 128]
    first = jnp.where(lanes < SLOTS, same, 0.0)
    limit = jnp.sum(first * limits[...], axis=1, keepdims=True)
    index = (base + lax.broadcasted_iota(jnp.int32, (rows, 1), 0)).astype(F32)
    dead = jnp.where(index < limit, 0.0, 1.0)
    marks = jnp.where(lanes == DEAD, dead, first)
    marks = jnp.where((lanes >= ONES) & (lanes < ONES + 2), 1.0, marks)
    mark_out[...] = marks.astype(BF16)

    @pl.when(step == 0)
    def _():
        stream_out[...] = stream
        low_out[...] = low
        found_out[...] = found.astype(BF16)
        query = dot(query_weight[...], normed, 0, 1) * (LOG2E / math.sqrt(HEAD_DIM))
        query_out[...] = query.astype(BF16)


def embed(own, notes, mean_norm, table, entry, gain, shift, wq, wk, wv, rows, blocks):
    group = rows * blocks
    width = wq.shape[0]
    turn = lambda step, own: (lax.rem(own[0] + step, blocks), 0)
    return pl.pallas_call(
        embed_kernel,
        grid_spec=pltpu.PrefetchScalarGridSpec(
            num_scalar_prefetch=1,
            grid=(blocks,),
            in_specs=[
                pl.BlockSpec(memory_space=pltpu.SMEM),
                whole(notes.shape),
                whole((8, 128)),
                whole(table.shape),
                whole(entry.shape),
                whole((width,)),
                whole((width,)),
                whole((width, width)),
                whole((width, width)),
                whole((width, width)),
            ],
            out_specs=[
                pl.BlockSpec((width, rows), lambda *args: turn(*args)[::-1]),
                pl.BlockSpec((width // 128, rows, 128), lambda *args: (0, *turn(*args))),
                pl.BlockSpec((width // 128, rows, 128), lambda *args: (0, *turn(*args))),
                pl.BlockSpec((rows, 128), turn),
                whole((rows, width)),
                whole((width, rows)),
                whole((rows, 128)),
                whole((rows, 128)),
            ],
            scratch_shapes=[
                pltpu.VMEM((2, rows, 128), F32),
                pltpu.VMEM((1, 128), F32),
                pltpu.VMEM((VOCAB, 128), F32),
            ],
        ),
        out_shape=[
            jax.ShapeDtypeStruct((width, group), BF16),
            jax.ShapeDtypeStruct((width // 128, group, 128), BF16),
            jax.ShapeDtypeStruct((width // 128, group, 128), BF16),
            jax.ShapeDtypeStruct((group, 128), BF16),
            jax.ShapeDtypeStruct((rows, width), F32),
            jax.ShapeDtypeStruct((width, rows), BF16),
            jax.ShapeDtypeStruct((rows, 128), BF16),
            jax.ShapeDtypeStruct((rows, 128), BF16),
        ],
        compiler_params=params(),
        name="embed",
    )(own, notes, notes, mean_norm, table, entry, gain, shift, wq, wk, wv)


def pair_columns(target, pair, rows):
    target[0:HEAD_DIM, 0:rows] = pair[0:HEAD_DIM]
    target[0:HEAD_DIM, rows : 2 * rows] = jnp.zeros((HEAD_DIM, rows), BF16)
    target[HEAD_DIM : 2 * HEAD_DIM, 0:rows] = jnp.zeros((HEAD_DIM, rows), BF16)
    target[HEAD_DIM : 2 * HEAD_DIM, rows : 2 * rows] = pair[HEAD_DIM : 2 * HEAD_DIM]


def forward_kernel(query, keys, values, marks, slots, probs_out, mixed_out, inverse_out, right, scores):
    rows = query.shape[1]
    group = keys.shape[0]
    blocks = group // KEY_BLOCK
    pair_columns(right, query, rows)
    kinds = lax.broadcasted_iota(jnp.int32, (128, rows), 0)
    slot = jnp.concatenate([slots[line : line + 1, :] for line in range(rows // 128)], axis=1)
    away = jnp.where((kinds < DEAD) & (kinds != slot), MASKED, 0.0)
    away = jnp.where(kinds == DEAD, MASKED, away).astype(BF16)
    right[128:256, 0:rows] = away
    right[128:256, rows : 2 * rows] = away

    ones = jnp.ones((16, KEY_BLOCK), BF16)

    def left_of(part):
        return jnp.concatenate([keys[part, :], marks[part, :]], axis=1)

    def weigh(part, probs, total):
        probs_out[part, :] = probs
        return total + dot(jnp.concatenate([values[part, :].T, ones], axis=0), probs)

    def store(total):
        inverse = 1.0 / total[128:129]
        mixed_out[0:HEAD_DIM] = total[0:HEAD_DIM, 0:rows] * inverse[:, 0:rows]
        mixed_out[HEAD_DIM:128] = total[HEAD_DIM:128, rows : 2 * rows] * inverse[:, rows : 2 * rows]
        inverse_out[0, 0:1] = inverse[:, 0:rows]
        inverse_out[0, 1:2] = inverse[:, rows : 2 * rows]

    highest = jnp.max(jnp.abs(keys[...]).astype(F32), axis=0, keepdims=True)
    spans = jnp.abs(query[...].astype(F32)) * column_of(highest)
    first = jnp.max(jnp.sum(spans[0:HEAD_DIM], axis=0, keepdims=True))
    second = jnp.max(jnp.sum(spans[HEAD_DIM : 2 * HEAD_DIM], axis=0, keepdims=True))
    bounded = jnp.maximum(first, second) < SAFE

    @pl.when(bounded)
    def _():
        total = jnp.zeros((144, 2 * rows), F32)
        for index in range(blocks):
            part = slice(index * KEY_BLOCK, (index + 1) * KEY_BLOCK)
            probs = jnp.exp2(dot(left_of(part), right[...])).astype(BF16)
            total = weigh(part, probs, total)
        store(total)

    @pl.when(jnp.logical_not(bounded))
    def _():
        def part_of(index):
            return pl.ds(pl.multiple_of(index * KEY_BLOCK, KEY_BLOCK), KEY_BLOCK)

        def score(index, top):
            part = part_of(index)
            current = dot(left_of(part), right[...])
            scores[part, :] = current
            return jnp.maximum(top, jnp.max(current.reshape(KEY_BLOCK // 8, 8, 2 * rows), axis=0))

        top = lax.fori_loop(0, blocks, score, jnp.full((8, 2 * rows), MASKED, F32))
        top = jnp.max(top, axis=0, keepdims=True)

        def shifted(index, total):
            part = part_of(index)
            return weigh(part, jnp.exp2(scores[part, :] - top).astype(BF16), total)

        store(lax.fori_loop(0, blocks, shifted, jnp.zeros((144, 2 * rows), F32)))


def attend(query, keys, values, marks, slots):
    width, rows = query.shape
    group = keys.shape[1]
    pairs = width // 128
    column = pl.BlockSpec((None, group, 128), lambda pair: (pair, 0, 0))
    return pl.pallas_call(
        forward_kernel,
        grid=(pairs,),
        in_specs=[
            pl.BlockSpec((128, rows), lambda pair: (pair, 0)),
            column,
            column,
            whole((group, 128)),
            whole((rows // 128, 128)),
        ],
        out_specs=[
            pl.BlockSpec((None, group, 2 * rows), lambda pair: (pair, 0, 0)),
            pl.BlockSpec((128, rows), lambda pair: (pair, 0)),
            pl.BlockSpec((1, 2, rows), lambda pair: (pair, 0, 0)),
        ],
        out_shape=[
            jax.ShapeDtypeStruct((pairs, group, 2 * rows), BF16),
            jax.ShapeDtypeStruct((width, rows), F32),
            jax.ShapeDtypeStruct((pairs, 2, rows), F32),
        ],
        scratch_shapes=[pltpu.VMEM((256, 2 * rows), BF16), pltpu.VMEM((group, 2 * rows), F32)],
        compiler_params=params(),
        name="attend",
    )(query, keys, values, marks, slots)


def feed_kernel(
    mixed_wide,
    inverse,
    stream,
    upstream,
    gain,
    shift,
    output_hbm,
    up_hbm,
    down_hbm,
    activation_out,
    middle_grad_out,
    norm_out,
    mixed_grad_out,
    row_out,
    output_grad_hbm,
    up_grad_hbm,
    down_grad_hbm,
    output_weight,
    up_weight,
    down_weight,
    output_grad,
    up_grad,
    down_grad,
    activation_sum,
    normed_sum,
    loads,
    stores,
):
    rows, width = stream.shape
    hidden_width = up_weight.shape[1]
    chunk = width
    chunks = hidden_width // chunk
    load_output = pltpu.make_async_copy(output_hbm, output_weight, loads.at[0])
    load_output.start()

    def load_parts(index):
        part = pl.ds(pl.multiple_of(index * chunk, 128), chunk)
        return (
            pltpu.make_async_copy(up_hbm.at[:, part], up_weight.at[:, part], loads.at[1 + 2 * index]),
            pltpu.make_async_copy(down_hbm.at[part], down_weight.at[part], loads.at[2 + 2 * index]),
        )

    def store_parts(index):
        y, c = lax.rem(index, 2), lax.div(index, 2)
        return (
            pltpu.make_async_copy(
                down_grad.at[:, :, :, index], down_grad_hbm.at[:, :, :, index], stores.at[1 + 2 * index]
            ),
            pltpu.make_async_copy(up_grad.at[c, y], up_grad_hbm.at[c, y], stores.at[2 + 2 * index]),
        )

    for index in range(chunks):
        for copy in load_parts(index):
            copy.start()
    mixed = mixed_wide[...].astype(BF16)
    load_output.wait()
    middle = stream[...] + dot(mixed, output_weight[...], 0, 0)
    unit, scale = norm_parts(middle)
    wide_gain = gain[...].reshape(1, width)
    normed = (unit * wide_gain + shift[...].reshape(1, width)).astype(BF16)
    normed_t = normed.T
    incoming = upstream[...]
    activation_sum[...] = middle
    normed_sum[...] = jnp.zeros((rows, width), F32)

    def step(index, carry):
        part = pl.ds(pl.multiple_of(index * chunk, 128), chunk)
        for copy in load_parts(index):
            copy.wait()
        pre = dot(normed, up_weight[:, part])
        cdf = 0.5 * (1.0 + lax.erf(pre * math.sqrt(0.5)))
        slope = cdf + pre * jnp.exp(-0.5 * pre * pre) * (1.0 / math.sqrt(2.0 * math.pi))
        hidden = (pre * cdf).astype(BF16)
        back = dot(incoming, down_weight[part, :], 1, 1)
        pre_grad = (back * slope).astype(BF16)
        activation_sum[...] += dot(hidden, down_weight[part, :])
        down_part = dot(hidden, incoming, 0, 0).astype(BF16).reshape(8, PIECE, width)
        for piece in range(8):
            down_grad[piece // 4, piece // 2 % 2, piece % 2, index] = down_part[piece]
        up_part = dot(normed_t, pre_grad).astype(BF16).reshape(4, 2, PIECE, width)
        for half in range(2):
            up_grad[lax.div(index, 2), lax.rem(index, 2), half] = up_part[:, half]
        for copy in store_parts(index):
            copy.start()
        normed_sum[...] += dot(pre_grad, up_weight[:, part], 1, 1)
        return carry

    lax.fori_loop(0, chunks, step, 0)
    activation = activation_sum[...]
    normed_grad = normed_sum[...]
    activation_out[...] = activation.astype(BF16)
    norm_out[0:1] = jnp.sum(normed_grad * unit, axis=0, keepdims=True)
    norm_out[1:2] = jnp.sum(normed_grad, axis=0, keepdims=True)
    middle_grad = incoming.astype(F32) + norm_back(normed_grad, wide_gain, unit, scale)
    middle_grad_out[...] = middle_grad
    middle_low = middle_grad.astype(BF16)
    output_part = dot(mixed, middle_low).astype(BF16).reshape(4, 2, PIECE, width)
    for half in range(2):
        output_grad[half] = output_part[:, half]
    store_output = pltpu.make_async_copy(output_grad, output_grad_hbm, stores.at[0])
    store_output.start()
    mixed_grad = dot(output_weight[...], middle_low, 1, 1).astype(BF16).astype(F32)
    for head in range(HEADS):
        part = slice(head * HEAD_DIM, (head + 1) * HEAD_DIM)
        factor = inverse[head // 2, head % 2 : head % 2 + 1]
        mixed_grad_out[part, :] = (mixed_grad[part] * factor).astype(BF16)
        row_out[head // 2, head % 2 : head % 2 + 1] = factor * jnp.sum(
            mixed_grad[part] * mixed_wide[part, :], axis=0, keepdims=True
        )
    store_output.wait()
    for index in range(chunks):
        for copy in store_parts(index):
            copy.wait()


def feed(mixed, inverse, stream, upstream, gain, shift, output_weight, up_weight, down_weight):
    rows, width = stream.shape
    hidden_width = up_weight.shape[1]
    vmem = pl.BlockSpec(memory_space=pltpu.VMEM)
    hbm = pl.BlockSpec(memory_space=pltpu.HBM)
    return pl.pallas_call(
        feed_kernel,
        in_specs=[vmem] * 6 + [hbm] * 3,
        out_specs=[vmem] * 5 + [hbm] * 3,
        out_shape=[
            jax.ShapeDtypeStruct((rows, width), BF16),
            jax.ShapeDtypeStruct((rows, width), F32),
            jax.ShapeDtypeStruct((2, width), F32),
            jax.ShapeDtypeStruct((width, rows), BF16),
            jax.ShapeDtypeStruct((HEADS // 2, 2, rows), F32),
            jax.ShapeDtypeStruct((2, 4, PIECE, width), BF16),
            jax.ShapeDtypeStruct(UNIT, BF16),
            jax.ShapeDtypeStruct(UNIT, BF16),
        ],
        scratch_shapes=[
            pltpu.VMEM((width, width), BF16),
            pltpu.VMEM((width, hidden_width), BF16),
            pltpu.VMEM((hidden_width, width), BF16),
            pltpu.VMEM((2, 4, PIECE, width), BF16),
            pltpu.VMEM(UNIT, BF16),
            pltpu.VMEM(UNIT, BF16),
            pltpu.VMEM((rows, width), F32),
            pltpu.VMEM((rows, width), F32),
            pltpu.SemaphoreType.DMA((9,)),
            pltpu.SemaphoreType.DMA((9,)),
        ],
        compiler_params=params(),
        name="feed",
    )(mixed, inverse, stream, upstream, gain, shift, output_weight, up_weight, down_weight)


class Plane:
    def __init__(self, unit, local, scratch):
        self.unit, self.local = unit, local
        self.one, self.two_a, self.two_b, self.three, self.sems = *scratch[:4], scratch[4:6]
        self.z, self.x, self.y, self.c = place()
        (self.core, self.across, self.along), _ = neighbours()
        self.half = self.three.shape[-1] // 2

    def chunk(self, step):
        return lax.rem(self.z + step, 4)

    def copy(self, slot, step):
        x, y, z, half = self.x, self.y, self.chunk(step), self.half
        left, right = pl.ds(0, half), pl.ds(half, half)
        sem = slot * 4 + step
        if slot == 0:
            source, target = self.unit.at[1 - self.c, :, :, z], self.one.at[:, :, z]
            return send(source, target, self.sems, sem, self.core)
        if slot == 1:
            source, target = self.one.at[:, 1 - x, z, :, left], self.two_a.at[:, z]
            return send(source, target, self.sems, sem, self.across)
        if slot == 2:
            source, target = self.one.at[1 - y, :, z, :, right], self.two_b.at[:, z]
            return send(source, target, self.sems, sem, self.along)
        if slot == 3:
            source, target = self.two_a.at[1 - y, z], self.three.at[z, :, left]
            return send(source, target, self.sems, sem, self.along)
        source, target = self.two_b.at[1 - x, z], self.three.at[z, :, right]
        return send(source, target, self.sems, sem, self.across)

    def begin(self, step):
        self.copy(0, step).start()

    def add_one(self, step):
        z = self.chunk(step)
        self.copy(0, step).wait_recv()
        for y in range(2):
            for x in range(2):
                self.one[y, x, z] = self.one[y, x, z] + self.local(y, x, z)
        self.copy(1, step).start()
        self.copy(2, step).start()

    def add_two_a(self, step):
        z = self.chunk(step)
        self.copy(1, step).wait_recv()
        for y in range(2):
            self.two_a[y, z] = self.two_a[y, z] + self.one[y, self.x, z, :, 0 : self.half]
        self.copy(3, step).start()

    def add_two_b(self, step):
        z = self.chunk(step)
        self.copy(2, step).wait_recv()
        for x in range(2):
            self.two_b[x, z] = self.two_b[x, z] + self.one[self.y, x, z, :, self.half : 2 * self.half]
        self.copy(4, step).start()

    def add_three(self, step):
        z, half = self.chunk(step), self.half
        self.copy(3, step).wait_recv()
        self.copy(4, step).wait_recv()
        self.three[z, :, 0:half] = self.three[z, :, 0:half] + self.two_a[self.y, z]
        right = slice(half, 2 * half)
        self.three[z, :, right] = self.three[z, :, right] + self.two_b[self.x, z]

    def finish(self):
        for slot in range(5):
            for step in range(4):
                self.copy(slot, step).wait_send()

    def actions(self, first):
        kinds = (self.begin, self.add_one, self.add_two_a, self.add_two_b, self.add_three)
        return {
            first + 4 * index + step: functools.partial(kind, step)
            for index, kind in enumerate(kinds)
            for step in range(4)
        }


def plane_buffers():
    _, _, _, zs, piece, width = UNIT
    return [
        pltpu.VMEM((2, 2, zs, piece, width), BF16),
        pltpu.VMEM((2, zs, piece, width // 2), BF16),
        pltpu.VMEM((2, zs, piece, width // 2), BF16),
        pltpu.VMEM((zs, piece, width), BF16),
        pltpu.SemaphoreType.DMA((20,)),
        pltpu.SemaphoreType.DMA((20,)),
    ]


class Line:
    def __init__(self, three, scratch, out):
        self.three, self.four, self.sems, self.out = three, scratch[0], scratch[1:3], out
        self.z, self.x, self.y, self.c = place()
        (self.core, self.across, self.along), self.planes = neighbours()
        self.half = three.shape[-1] // 2

    def copy(self, slot):
        x, y, c = self.x, self.y, self.c
        left, right = pl.ds(0, self.half), pl.ds(self.half, self.half)
        if slot < 3:
            target = lax.rem(self.z + slot + 1, 4)
            return send(self.three.at[target], self.four.at[slot], self.sems, slot, self.planes[slot])
        mine = self.out.at[c, y, x]
        if slot == 3:
            return send(mine, mine, self.sems, 3, self.across)
        if slot == 4:
            return send(mine, mine, self.sems, 4, self.along)
        if slot == 5:
            other = self.out.at[c, y, 1 - x, :, left]
            return send(other, other, self.sems, 5, self.along)
        if slot == 6:
            other = self.out.at[c, 1 - y, x, :, right]
            return send(other, other, self.sems, 6, self.across)
        return send(self.out.at[c], self.out.at[c], self.sems, 7, self.core)

    def begin(self, step):
        if step:
            self.copy(step - 1).start()

    def add(self):
        total = self.three[self.z].astype(F32)
        for slot in range(3):
            self.copy(slot).wait_recv()
            total = total + self.four[slot].astype(F32)
        self.out[self.c, self.y, self.x] = total.astype(BF16)
        self.copy(3).start()
        self.copy(4).start()

    def forward(self, slot):
        self.copy(slot).wait_recv()
        self.copy(slot + 2).start()

    def share(self):
        self.copy(5).wait_recv()
        self.copy(6).wait_recv()
        self.copy(7).start()

    def end(self):
        self.copy(7).wait_recv()

    def finish(self):
        for slot in range(8):
            self.copy(slot).wait_send()

    def actions(self, first):
        steps = {first + step: functools.partial(self.begin, step) for step in range(4)}
        forward_x, forward_y = (functools.partial(self.forward, slot) for slot in (3, 4))
        rest = (self.add, forward_x, forward_y, self.share, self.end)
        steps.update({first + 4 + 4 * index: step for index, step in enumerate(rest)})
        return steps


def line_buffers():
    _, _, _, _, piece, width = UNIT
    return [
        pltpu.VMEM((3, piece, width), BF16),
        pltpu.SemaphoreType.DMA((8,)),
        pltpu.SemaphoreType.DMA((8,)),
    ]


def back_kernel(
    linked,
    query,
    keys,
    values,
    marks,
    probs,
    mixed_grad,
    row_sums,
    query_hbm,
    key_hbm,
    value_hbm,
    down_unit,
    up_unit,
    query_back_hbm,
    key_back_hbm,
    value_back_hbm,
    normed_unit,
    down_out,
    up_out,
    left,
    right,
    query_back,
    key_back,
    value_back,
    query_weight,
    key_weight,
    value_weight,
    staged,
    loads,
    stores,
    pair_sems,
    *scratch,
):
    pair = pl.program_id(0)
    pairs = pl.num_programs(0) - 1
    width, rows = query_back.shape
    group = keys.shape[0]
    blocks = group // KEY_BLOCK
    owners = group // rows
    copies = [
        pltpu.make_async_copy(source, target, loads.at[index])
        for index, (source, target) in enumerate(
            ((query_hbm, query_weight), (key_hbm, key_weight), (value_hbm, value_weight))
        )
    ]
    steps = {}
    if linked:
        down_local, up_local = scratch[0:2]
        down = Plane(down_unit, lambda y, x, z: down_local[y, x, z], scratch[2:8])
        up = Plane(up_unit, lambda y, x, z: up_local[y, x, z], scratch[8:14])
        line = Line(down.three, scratch[14:17], scratch[17])
        seat = lax.rem(lax.axis_index("seq"), 2)
        locals_ = [
            pltpu.make_async_copy(down_unit.at[seat], down_local, loads.at[3]),
            pltpu.make_async_copy(up_unit.at[seat], up_local, loads.at[4]),
        ]
        down_store = pltpu.make_async_copy(scratch[17], down_out, stores.at[5])
        up_store = pltpu.make_async_copy(up.three, up_out, stores.at[6])

        steps = {
            GREET: lambda: greet(neighbours()[0] + neighbours()[1]),
            D_LOCAL: locals_[0].wait,
            U_LOCAL: locals_[1].wait,
        }
        steps.update(down.actions(D_CORE))
        steps.update(up.actions(U_CORE))
        steps.update(line.actions(D_SEND))

    def pair_stores(pair):
        column = pl.ds(pl.multiple_of(pair * 128, 128), 128)
        return [
            pltpu.make_async_copy(source.at[:, column], target.at[:, column], pair_sems.at[index, pair])
            for index, (source, target) in enumerate(
                ((key_back, key_back_hbm), (value_back, value_back_hbm))
            )
        ]

    def run(spot):
        if linked:
            for key in BACK_ORDER[spot]:
                steps[key]()

    @pl.when(pair == 0)
    def _():
        if linked:
            locals_[0].start()
        run(0)

    @pl.when(pair == 1)
    def _():
        if linked:
            locals_[1].start()

    @pl.when(pair == 3)
    def _():
        for copy in copies:
            copy.start()

    @pl.when(pair < pairs)
    def _():
        pair_columns(left, query, rows)
        pair_columns(right, mixed_grad, rows)
        kinds = lax.broadcasted_iota(jnp.int32, (128, rows), 0)
        shape = (128, rows)
        for half in range(2):
            total = -row_sums[0, half : half + 1]
            high = total.astype(BF16).astype(F32)
            fill = jnp.where(kinds == ONES, jnp.broadcast_to(high, shape), 0.0)
            fill = jnp.where(kinds == ONES + 1, jnp.broadcast_to(total - high, shape), fill)
            right[128:256, half * rows : (half + 1) * rows] = fill.astype(BF16)

        column = pl.ds(pl.multiple_of(pair * 128, 128), 128)

        def block(index, total):
            part = pl.ds(pl.multiple_of(index * KEY_BLOCK, KEY_BLOCK), KEY_BLOCK)
            weights = probs[part, :]
            inner = dot(jnp.concatenate([values[part, :], marks[part, :]], axis=1), right[...])
            score_grad = (weights.astype(F32) * inner).astype(BF16)
            key_back[part, column] = (dot(score_grad, left[...], 1, 1) * LN2).astype(BF16)
            value_back[part, column] = dot(weights, right[0:128, :], 1, 1).astype(BF16)
            return total + dot(keys[part, :].T, score_grad)

        total = lax.fori_loop(0, blocks, block, jnp.zeros((128, 2 * rows), F32), unroll=3)
        scale = HEAD_DIM**-0.5
        base = pl.multiple_of(pair * 128, 128)
        query_back[pl.ds(base, HEAD_DIM), :] = (total[0:HEAD_DIM, 0:rows] * scale).astype(BF16)
        base = pl.multiple_of(pair * 128 + HEAD_DIM, HEAD_DIM)
        query_back[pl.ds(base, HEAD_DIM), :] = (total[HEAD_DIM:128, rows : 2 * rows] * scale).astype(BF16)

        for copy in pair_stores(pair):
            copy.start()
        for spot in range(1, 7):
            if linked and BACK_ORDER[spot]:
                pl.when(pair == spot - 1)(functools.partial(run, spot))

    @pl.when(pair == pairs)
    def _():
        query_store = pltpu.make_async_copy(query_back, query_back_hbm, stores.at[2])
        query_store.start()
        for copy in copies:
            copy.wait()
        own = lax.axis_index("head") * lax.axis_size("seq") + lax.axis_index("seq")

        def owner_store(owner):
            x, y, c = lax.div(owner, 4), lax.rem(lax.div(owner, 2), 2), lax.rem(owner, 2)
            slot = lax.rem(owner, 2)
            return pltpu.make_async_copy(staged.at[slot], normed_unit.at[c, y, x], stores.at[slot])

        def owner_step(owner, carry):
            part = pl.ds(pl.multiple_of(owner * rows, 128), rows)
            slot = lax.rem(owner, 2)
            total = dot(key_back[part, :], key_weight[...], 1, 1)
            total = total + dot(value_back[part, :], value_weight[...], 1, 1)

            @pl.when(owner >= 2)
            def _():
                owner_store(owner).wait()

            staged[slot] = total.astype(BF16).reshape(4, PIECE, width)

            @pl.when(own == owner)
            def _():
                extra = dot(query_back[...], query_weight[...], 0, 1)
                staged[slot] = (total + extra).astype(BF16).reshape(4, PIECE, width)

            owner_store(owner).start()
            return carry

        lax.fori_loop(0, owners // 2, owner_step, 0)
        run(7)
        lax.fori_loop(owners // 2, owners, owner_step, 0)
        run(8)
        for slot in range(2):
            owner_store(slot).wait()
        if linked:
            up_store.start()
            up_store.wait()
            down_store.start()
            down_store.wait()
            down.finish()
            up.finish()
            line.finish()
        query_store.wait()
        for done in range(6):
            for copy in pair_stores(done):
                copy.wait()


def attend_back(linked, query, keys, values, marks, probs, mixed_grad, row_sums, wq, wk, wv, down_unit, up_unit):
    width, rows = query.shape
    group = keys.shape[1]
    pairs = width // 128
    held = lambda pair: jnp.minimum(pair, pairs - 1)
    column = pl.BlockSpec((None, group, 128), lambda pair: (held(pair), 0, 0))
    row = pl.BlockSpec((128, rows), lambda pair: (held(pair), 0))
    hbm = pl.BlockSpec(memory_space=pltpu.HBM)
    third = jax.ShapeDtypeStruct(UNIT[3:], BF16)
    more = dict(collective_id=1, has_side_effects=True) if linked else {}
    scratch = []
    if linked:
        scratch = [pltpu.VMEM(UNIT[1:], BF16)] * 2 + plane_buffers() * 2 + line_buffers()
        scratch += [pltpu.VMEM(UNIT[:3] + UNIT[4:], BF16)]
    return pl.pallas_call(
        functools.partial(back_kernel, linked),
        grid=(pairs + 1,),
        in_specs=[
            row,
            column,
            column,
            pl.BlockSpec((group, 128), lambda pair: (0, 0), pipeline_mode=pl.Buffered(1)),
            pl.BlockSpec((None, group, 2 * rows), lambda pair: (held(pair), 0, 0)),
            row,
            pl.BlockSpec((1, 2, rows), lambda pair: (held(pair), 0, 0)),
        ]
        + [hbm] * 5,
        out_specs=[hbm] * 6,
        out_shape=[
            jax.ShapeDtypeStruct((width, rows), BF16),
            jax.ShapeDtypeStruct((group, width), BF16),
            jax.ShapeDtypeStruct((group, width), BF16),
            jax.ShapeDtypeStruct(UNIT, BF16),
            jax.ShapeDtypeStruct(UNIT[:3] + UNIT[4:], BF16),
            third,
        ],
        scratch_shapes=[
            pltpu.VMEM((128, 2 * rows), BF16),
            pltpu.VMEM((256, 2 * rows), BF16),
            pltpu.VMEM((width, rows), BF16),
            pltpu.VMEM((group, width), BF16),
            pltpu.VMEM((group, width), BF16),
            pltpu.VMEM((width, width), BF16),
            pltpu.VMEM((width, width), BF16),
            pltpu.VMEM((width, width), BF16),
            pltpu.VMEM((2, 4, PIECE, width), BF16),
            pltpu.SemaphoreType.DMA((5,)),
            pltpu.SemaphoreType.DMA((7,)),
            pltpu.SemaphoreType.DMA((2, 6)),
        ]
        + scratch,
        compiler_params=params(**more),
        name="attend_back",
    )(query, keys, values, marks, probs, mixed_grad, row_sums, wq, wk, wv, down_unit, up_unit)


class Rows:
    def __init__(self, given, part, landed, out, sems):
        self.given, self.part, self.landed, self.out, self.sems = given, part, landed, out, sems
        self.z, self.x, self.y, self.c = place()
        (self.core, self.across, self.along), self.planes = neighbours()

    def index(self, x, y, c):
        return x * 4 + y * 2 + c

    def copy(self, slot):
        x, y, c = self.x, self.y, self.c
        size = self.given.shape[1] // 2
        mine = self.given.at[self.index(x, y, c)]
        if slot < 3:
            return send(mine, mine, self.sems, slot, (self.core, self.across, self.along)[slot])
        if slot == 3:
            other = self.given.at[self.index(1 - x, y, c), pl.ds(0, size)]
            return send(other, other, self.sems, 3, self.along)
        if slot == 4:
            other = self.given.at[self.index(x, 1 - y, c), pl.ds(size, size)]
            return send(other, other, self.sems, 4, self.across)
        if slot < 8:
            flip_x, flip_y = ((1, 0), (0, 1), (1, 1))[slot - 5]
            other = self.given.at[
                self.index(x + flip_x - 2 * flip_x * x, y + flip_y - 2 * flip_y * y, c)
            ]
            return send(other, other, self.sems, slot, self.core)
        if slot < 11:
            step = slot - 8
            return send(
                self.part.at[step + 1], self.landed.at[step], self.sems, slot, self.planes[step]
            )
        if slot < 14:
            mine = self.out.at[x, self.z]
            return send(mine, mine, self.sems, slot, self.planes[slot - 11])
        other = self.out.at[x, lax.rem(self.z + 18 - slot, 4)]
        return send(other, other, self.sems, slot, self.across)

    def start(self, *slots):
        for slot in slots:
            self.copy(slot).start()

    def landed_all(self, *slots):
        for slot in slots:
            self.copy(slot).wait_recv()

    def finish(self):
        for slot in range(18):
            self.copy(slot).wait_send()


class Small:
    def __init__(self, rows, entry, half_rows, half_entry, landings, out, entry_out, sems):
        self.rows, self.entry, self.half_rows, self.half_entry = rows, entry, half_rows, half_entry
        self.landings, self.out, self.entry_out, self.sems = landings, out, entry_out, sems
        self.z, self.x, self.y, self.c = place()
        (self.core, self.across, self.along), self.planes = neighbours()
        half = rows.shape[-1] // 2
        self.mine = pl.ds(pl.multiple_of(self.c * half, 128), half)
        self.away = pl.ds(pl.multiple_of((1 - self.c) * half, 128), half)

    def copy(self, slot):
        rows_land, entry_land, last = self.landings
        stage, kind = slot // 2, slot % 2
        if stage == 0:
            source = (self.rows.at[:, self.away], self.entry.at[:, :, self.away])[kind]
        else:
            source = (self.half_rows, self.half_entry)[kind]
        if stage < 3:
            target = (rows_land, entry_land)[kind].at[stage]
            return send(source, target, self.sems, slot, (self.core, self.across, self.along)[stage])
        if stage < 6:
            step = stage - 3
            if kind == 0:
                target = self.out.at[self.z, :, self.mine]
            else:
                source = self.half_entry.at[lax.rem(self.z + step + 1, 4)]
                target = last.at[step]
            return send(source, target, self.sems, slot, self.planes[step])
        part = (self.out.at[:, :, self.mine], self.entry_out.at[:, self.mine])[kind]
        return send(part, part, self.sems, slot, self.core)

    def start(self, stage):
        self.copy(2 * stage).start()
        self.copy(2 * stage + 1).start()

    def landed(self, stage):
        self.copy(2 * stage).wait_recv()
        self.copy(2 * stage + 1).wait_recv()

    def add(self, stage):
        rows_land, entry_land, _ = self.landings
        self.landed(stage)
        if stage == 0:
            self.half_rows[...] = self.rows[:, self.mine] + rows_land[0]
            self.half_entry[...] = self.entry[:, :, self.mine] + entry_land[0]
        else:
            self.sent(stage)
            self.half_rows[...] = self.half_rows[...] + rows_land[stage]
            self.half_entry[...] = self.half_entry[...] + entry_land[stage]
        if stage < 2:
            self.start(stage + 1)
        else:
            for step in (3, 4, 5):
                self.start(step)

    def sent(self, stage):
        self.copy(2 * stage).wait_send()
        self.copy(2 * stage + 1).wait_send()

    def collect(self):
        last = self.landings[2]
        self.out[self.z, :, self.mine] = self.half_rows[...]
        total = self.half_entry[self.z].astype(F32)
        for step in range(3):
            self.landed(3 + step)
            total = total + last[step].astype(F32)
        self.entry_out[:, self.mine] = total.astype(BF16)
        self.start(6)


def late_kernel(
    slots,
    tokens,
    stream,
    middle_grad,
    gain,
    embed_low,
    found,
    input_weight,
    second_norm,
    query_back,
    up_three,
    normed_hbm,
    key_back_hbm,
    value_back_hbm,
    output_hbm,
    normed_unit,
    embed_grad_out,
    table_out,
    small_out,
    entry_out,
    up_out,
    heads_out,
    normed,
    key_back,
    value_back,
    heads_unit,
    normed_local,
    given,
    part,
    part_landed,
    rows_own,
    entry_own,
    half_rows,
    half_entry,
    rows_land,
    entry_land,
    entry_last,
    loads,
    *scratch,
):
    z, x, y, c = place()
    own = x * 4 + y * 2 + c
    width = stream.shape[1]
    rows = stream.shape[0]
    near, planes = neighbours()
    normed_plane = Plane(normed_unit, lambda yy, xx, zz: normed_local[yy, xx, zz], scratch[0:6])
    heads_plane = Plane(heads_unit, lambda yy, xx, zz: heads_unit[c, yy, xx, zz], scratch[6:12])
    up = Line(up_three, scratch[12:15], up_out)
    heads = Line(heads_plane.three, scratch[15:18], heads_out)
    table = Rows(given, part, part_landed, table_out, scratch[18:20])
    small = Small(
        rows_own,
        entry_own,
        half_rows,
        half_entry,
        (rows_land, entry_land, entry_last),
        small_out,
        entry_out,
        scratch[20:22],
    )
    local = pltpu.make_async_copy(normed_unit.at[c], normed_local, loads.at[0])
    copies = [
        pltpu.make_async_copy(source, target, loads.at[1 + index])
        for index, (source, target) in enumerate(
            (
                (normed_hbm, normed),
                (key_back_hbm, key_back),
                (value_back_hbm, value_back),
                (output_hbm, heads_unit.at[0, 0]),
            )
        )
    ]
    kept = {}

    def load():
        for copy in copies:
            copy.start()

    def loaded():
        for index in (0, 1, 3):
            copies[index].wait()

    def keep(kind):
        if kind == 1:
            mine = pl.ds(pl.multiple_of(own * rows, 128), rows)
            value = dot(normed[:, mine], query_back[...], 1, 1)
        else:
            if kind == 3:
                copies[2].wait()
            value = dot(normed[...], (key_back, value_back)[kind - 2][...])
        value = value.astype(BF16).reshape(4, 2, PIECE, width)
        for half in range(2):
            heads_unit[kind // 2, kind % 2, half] = value[:, half]

    def norm():
        unit, scale = norm_parts(stream[...])
        incoming = normed_plane.three[...].reshape(rows, width).astype(F32)
        stream_grad = middle_grad[...] + norm_back(incoming, gain[...].reshape(1, width), unit, scale)
        embed_grad = dot(stream_grad.astype(BF16), input_weight[...], 1, 1)
        given[own] = embed_grad.astype(BF16)
        embed_grad_out[...] = embed_grad
        kept["unit"], kept["incoming"], kept["stream_grad"] = unit, incoming, stream_grad
        kept["embed_grad"] = embed_grad

    def norm_rest():
        unit, incoming, stream_grad = kept["unit"], kept["incoming"], kept["stream_grad"]
        stream_low = stream_grad.astype(BF16)
        entry_own[...] = dot(embed_low[...], stream_low, 0, 0).astype(BF16).reshape(4, 32, width)
        kinds = lax.broadcasted_iota(jnp.int32, (SLOTS, rows), 0)
        slot = jnp.concatenate([slots[line : line + 1, :] for line in range(rows // 128)], axis=1)
        picker = jnp.where(kinds == slot, 1.0, 0.0).astype(BF16)
        rest = (stream_grad - stream_low.astype(F32)).astype(BF16)
        rows_own[...] = dot(picker, stream_low) + dot(picker, rest)
        rows_own[DEAD : DEAD + 1] = jnp.sum(incoming * unit, axis=0, keepdims=True)
        rows_own[DEAD + 1 : DEAD + 2] = jnp.sum(incoming, axis=0, keepdims=True)
        rows_own[DEAD + 2 : DEAD + 4] = second_norm[...]
        inner = jnp.sum(kept["embed_grad"] * found[...].astype(F32), axis=0, keepdims=True)
        inner = jnp.sum(inner, axis=1, keepdims=True)
        rows_own[DEAD + 4 : DEAD + 5] = jnp.broadcast_to(inner, (1, width))

    def hot(step):
        size = part.shape[1]
        seq = y * 2 + c
        base = seq * (8 * size) + x * (4 * size) + lax.rem(z + step, 4) * size
        ids = lax.broadcasted_iota(jnp.int32, (size, 128), 0) + base
        hits = [
            jnp.where(ids == tokens[owner, line : line + 1, :], 1.0, 0.0).astype(BF16)
            for owner in range(8)
            for line in range(rows // 128)
        ]
        hits = jnp.concatenate(hits, axis=1)
        part[step] = dot(hits, given[...].reshape(8 * rows, 128)).astype(BF16)
        if step:
            table.start(7 + step)

    def table_add():
        total = part[0].astype(F32)
        for slot in (8, 9, 10):
            table.landed_all(slot)
            total = total + part_landed[slot - 8].astype(F32)
        table_out[x, z] = total.astype(BF16)
        table.start(11, 12, 13, 14)

    def table_forward(*slots):
        for slot in slots:
            table.landed_all(slot)
            table.start(slot + 4)

    def after(wait, *starts):
        table.landed_all(*wait)
        table.start(*starts)

    def hot_first():
        table.landed_all(0, 5, 6, 7)
        hot(1)

    steps = {
        GREET: lambda: greet(near + planes),
        X_LOCAL: local.wait,
        LOAD: load,
        LOADED: loaded,
        GRAD_Q: lambda: keep(1),
        GRAD_K: lambda: keep(2),
        GRAD_V: lambda: keep(3),
        NORM: norm,
        NORM_REST: norm_rest,
        T_FIRST: lambda: table.start(0, 1, 2),
        T_PASS_X: lambda: after((1,), 3),
        T_PASS_Y: lambda: after((2,), 4),
        T_CORE: lambda: after((3, 4), 5, 6, 7),
        T_ROWS: hot_first,
        T_ROWS + 1: lambda: hot(2),
        T_ROWS + 2: lambda: hot(3),
        T_ROWS + 3: lambda: hot(0),
        T_SUM: table_add,
        T_PASS: lambda: table_forward(11, 12, 13),
        T_END: lambda: table.landed_all(14, 15, 16, 17),
        S_FIRST: lambda: small.start(0),
        S_CORE: lambda: small.add(0),
        S_X: lambda: small.add(1),
        S_Y: lambda: small.add(2),
        S_COLLECT: small.collect,
        S_END: lambda: small.landed(6),
    }
    steps.update(normed_plane.actions(X_CORE))
    steps.update(heads_plane.actions(H_CORE))
    steps.update(up.actions(U_SEND))
    steps.update(heads.actions(H_SEND))
    local.start()
    for key in LATE_ORDER:
        steps[key]()
    small.sent(0)
    for stage in (3, 4, 5, 6):
        small.sent(stage)
    table.finish()
    normed_plane.finish()
    heads_plane.finish()
    up.finish()
    heads.finish()


def late(
    slots,
    tokens,
    stream,
    middle_grad,
    gain,
    embed_low,
    found,
    input_weight,
    second_norm,
    query_back,
    up_three,
    normed,
    key_back,
    value_back,
    output_part,
    normed_unit,
):
    rows, width = stream.shape
    group = key_back.shape[0]
    quarter = VOCAB // 4 // 8
    vmem = pl.BlockSpec(memory_space=pltpu.VMEM)
    hbm = pl.BlockSpec(memory_space=pltpu.HBM)
    done = jax.ShapeDtypeStruct((2, 2, 2, PIECE, width), BF16)
    pair = lambda count: [pltpu.SemaphoreType.DMA((count,)), pltpu.SemaphoreType.DMA((count,))]
    return pl.pallas_call(
        late_kernel,
        in_specs=[vmem] * 11 + [hbm] * 5,
        out_specs=[vmem] * 6,
        out_shape=[
            jax.ShapeDtypeStruct((rows, 128), F32),
            jax.ShapeDtypeStruct((2, 4, quarter, 128), BF16),
            jax.ShapeDtypeStruct((4, 32, width), F32),
            jax.ShapeDtypeStruct((32, width), BF16),
            done,
            done,
        ],
        scratch_shapes=[
            pltpu.VMEM((width, group), BF16),
            pltpu.VMEM((group, width), BF16),
            pltpu.VMEM((group, width), BF16),
            pltpu.VMEM(UNIT, BF16),
            pltpu.VMEM(UNIT[1:], BF16),
            pltpu.VMEM((8, rows, 128), BF16),
            pltpu.VMEM((4, quarter, 128), BF16),
            pltpu.VMEM((3, quarter, 128), BF16),
            pltpu.VMEM((32, width), F32),
            pltpu.VMEM((4, 32, width), BF16),
            pltpu.VMEM((32, width // 2), F32),
            pltpu.VMEM((4, 32, width // 2), BF16),
            pltpu.VMEM((3, 32, width // 2), F32),
            pltpu.VMEM((3, 4, 32, width // 2), BF16),
            pltpu.VMEM((3, 32, width // 2), BF16),
            pltpu.SemaphoreType.DMA((5,)),
        ]
        + plane_buffers() * 2
        + line_buffers() * 2
        + pair(18)
        + pair(14),
        compiler_params=params(collective_id=2, has_side_effects=True),
        name="late",
    )(
        slots,
        tokens,
        stream,
        middle_grad,
        gain,
        embed_low,
        found,
        input_weight,
        second_norm,
        query_back,
        up_three,
        normed,
        key_back,
        value_back,
        output_part,
        normed_unit,
    )


def finish_kernel(
    embed_grad,
    table_sum,
    small,
    entry,
    down,
    up,
    heads,
    table,
    mean_norm,
    hidden,
    acts,
    features,
    second_weight,
    embed_out,
    table_out,
    entry_out,
    first_out,
    second_out,
    gain_one,
    shift_one,
    query_out,
    key_out,
    value_out,
    output_out,
    gain_two,
    shift_two,
    up_out,
    down_out,
):
    width = second_weight.shape[0]
    embed_out[...] = embed_grad[...]
    entry_out[...] = entry[...].astype(F32)
    for piece in range(8):
        c, y, x = piece // 4, (piece // 2) % 2, piece % 2
        down_out[piece * PIECE : (piece + 1) * PIECE, :] = down[c, y, x].astype(F32)
        quarter = piece // 2
        up_out[x * PIECE : (x + 1) * PIECE, quarter * width : (quarter + 1) * width] = up[c, y, x].astype(F32)
        target = (output_out, query_out, key_out, value_out)[quarter]
        target[x * PIECE : (x + 1) * PIECE, :] = heads[c, y, x].astype(F32)
    totals = small[0, DEAD : DEAD + 5]
    for plane in range(1, small.shape[0]):
        totals = totals + small[plane, DEAD : DEAD + 5]
    gain_one[...] = totals[0:1].reshape(width)
    shift_one[...] = totals[1:2].reshape(width)
    gain_two[...] = totals[2:3].reshape(width)
    shift_two[...] = totals[3:4].reshape(width)
    mean = mean_norm[0:1]
    inverse = 1.0 / mean
    mean_grad = -totals[4:5, 0:128] * inverse * inverse * (1.0 / VOCAB)
    wide = table[...].astype(F32)
    norms = jnp.sqrt(jnp.sum(wide * wide, axis=1, keepdims=True))
    sums = table_sum[...].reshape(table.shape).astype(F32)
    table_out[...] = sums * inverse + mean_grad * (wide / norms)
    tog = jnp.concatenate([small[plane, 0:SLOTS] for plane in range(small.shape[0])], axis=0)
    plane = lax.axis_index("dp")

    def rows_of(array, count):
        return array[pl.ds(pl.multiple_of(plane * count, 8), count), :]

    second_out[...] = lax.dot_general(
        rows_of(acts, second_out.shape[0]),
        tog,
        (((1,), (0,)), ((), ())),
        precision=lax.Precision.HIGHEST,
        preferred_element_type=F32,
    )
    high = tog.astype(BF16)
    rest = (tog - high.astype(F32)).astype(BF16)
    act_grad = dot(high, second_weight[...], 1, 1) + dot(rest, second_weight[...], 1, 1)
    value = hidden[...]
    gate = 1.0 / (1.0 + jnp.exp(-value))
    hidden_grad = act_grad * (gate * (1.0 + value * (1.0 - gate)))
    first_out[...] = lax.dot_general(
        rows_of(features, first_out.shape[0]),
        hidden_grad,
        (((1,), (0,)), ((), ())),
        precision=lax.Precision.HIGHEST,
        preferred_element_type=F32,
    )


def finish(embed_grad, table_sum, small, entry, down, up, heads, table, mean_norm, hidden, acts, features, second_weight):
    rows = embed_grad.shape[0]
    width = second_weight.shape[0]
    wide = lambda *shape: jax.ShapeDtypeStruct(shape, F32)
    shard = width // 4
    return pl.pallas_call(
        finish_kernel,
        out_shape=[
            wide(rows, 128),
            wide(*table.shape),
            wide(32, width),
            wide(features.shape[0] // 4, width),
            wide(acts.shape[0] // 4, width),
            wide(width),
            wide(width),
            wide(shard, width),
            wide(shard, width),
            wide(shard, width),
            wide(shard, width),
            wide(width),
            wide(width),
            wide(shard, 4 * width),
            wide(width, width),
        ],
        compiler_params=params(),
        name="finish",
    )(embed_grad, table_sum, small, entry, down, up, heads, table, mean_norm, hidden, acts, features, second_weight)


def body(
    tokens,
    segments,
    live_lengths,
    timesteps,
    table,
    input_weight,
    time_first,
    time_second,
    first_gain,
    first_shift,
    query_weight,
    key_weight,
    value_weight,
    output_weight,
    second_gain,
    second_shift,
    up_weight,
    down_weight,
    upstream,
):
    blocks = lax.axis_size("head") * lax.axis_size("seq")
    planes = lax.axis_size("dp")
    rows = tokens.shape[0]
    width = query_weight.shape[0]
    shard_rows = table.shape[0]
    slot_count = live_lengths.shape[1]
    highest = lax.Precision.HIGHEST
    plane = lax.axis_index("dp")
    seq_index = lax.axis_index("seq")
    own = lax.axis_index("head") * lax.axis_size("seq") + seq_index
    linked = planes == 4

    slot_rows = segments.reshape(rows // 128, 128)
    full_table, notes_all, mean_norm, entry, time_hidden, acts, features = gather(
        table,
        tokens.reshape(rows // 128, 128),
        slot_rows,
        timesteps,
        live_lengths,
        input_weight,
        time_first,
        time_second,
    )
    normed, keys, values, marks, stream, query, embed_low, found = embed(
        own[None],
        notes_all,
        mean_norm,
        full_table,
        entry,
        first_gain,
        first_shift,
        query_weight,
        key_weight,
        value_weight,
        rows,
        blocks,
    )
    probs, mixed, inverse = attend(query, keys, values, marks, slot_rows)
    activation, middle_grad, second_norm, mixed_grad, row_sums, output_part, up_unit, down_unit = feed(
        mixed,
        inverse,
        stream,
        upstream,
        second_gain,
        second_shift,
        output_weight,
        up_weight,
        down_weight,
    )
    query_back, key_back, value_back, normed_unit, down_sum, up_three = attend_back(
        linked,
        query,
        keys,
        values,
        marks,
        probs,
        mixed_grad,
        row_sums,
        query_weight,
        key_weight,
        value_weight,
        down_unit,
        up_unit,
    )
    if linked:
        embed_grad, table_sum, small, entry_sum, up_sum, heads_sum = late(
            slot_rows,
            notes_all,
            stream,
            middle_grad,
            first_gain,
            embed_low,
            found,
            input_weight,
            second_norm,
            query_back,
            up_three,
            normed,
            key_back,
            value_back,
            output_part,
            normed_unit,
        )
        outs = finish(
            embed_grad,
            table_sum,
            small,
            entry_sum,
            down_sum,
            up_sum,
            heads_sum,
            table,
            mean_norm,
            time_hidden,
            acts,
            features,
            time_second,
        )
        return (activation, *outs)

    output_grad = output_part.transpose(1, 0, 2, 3).reshape(width, width)
    query_grad = dot(lax.dynamic_slice_in_dim(normed, own * rows, rows, axis=1), query_back, 1, 1)
    key_grad = dot(normed, key_back)
    value_grad = dot(normed, value_back)
    down_grad = down_unit.transpose(3, 0, 1, 2, 4, 5).reshape(-1, width)
    up_grad = up_unit.transpose(3, 2, 4, 0, 1, 5).reshape(width, -1)
    normed_grad = lax.psum_scatter(
        normed_unit.transpose(2, 1, 0, 3, 4, 5).reshape(-1, width),
        ("head", "seq"),
        scatter_dimension=0,
        tiled=True,
    ).astype(F32)
    mean_norm = mean_norm[0, 0]
    features = lax.dynamic_slice_in_dim(features.T, plane * SLOTS, slot_count)
    time_hidden = lax.dynamic_slice_in_dim(time_hidden, plane * SLOTS, slot_count)
    time_act = lax.dynamic_slice_in_dim(acts.T, plane * SLOTS, slot_count)
    second_wide = time_second.astype(F32)

    def one_norm(values, gain, shift):
        unit, _ = norm_parts(values)
        return unit * gain + shift

    _, first_back = jax.vjp(one_norm, stream, first_gain, first_shift)
    stream_part, first_gain_grad, first_shift_grad = first_back(normed_grad)
    stream_grad = middle_grad + stream_part
    stream_low = stream_grad.astype(BF16)
    input_grad = dot(embed_low, stream_low, 0, 0)
    embed_grad = dot(stream_low, input_weight, 1, 1)
    picker = (segments[:, None] == jnp.arange(slot_count, dtype=jnp.int32)[None, :]).astype(F32)
    time_out_grad = contract_exact(picker, stream_grad)
    time_second_grad = contract_exact(time_act, time_out_grad)
    act_grad = lax.dot_general(
        time_out_grad, second_wide, (((1,), (1,)), ((), ())), precision=highest
    )
    _, silu_back = jax.vjp(jax.nn.silu, time_hidden)
    time_hidden_grad = silu_back(act_grad)[0]
    time_first_grad = contract_exact(features, time_hidden_grad)

    def reduce(value):
        part = lax.psum_scatter(value.astype(BF16), "dp", scatter_dimension=0, tiled=True)
        return lax.psum(part, ("head", "seq")).astype(F32)

    shards = [
        reduce(value)
        for value in (
            input_grad,
            time_first_grad,
            time_second_grad,
            query_grad,
            key_grad,
            value_grad,
            output_grad,
            up_grad,
            down_grad,
        )
    ]
    mean_part = -jnp.sum(embed_grad * found.astype(F32)) / (mean_norm * mean_norm)
    scaled_grad = embed_grad / mean_norm
    table_sum = jax.ops.segment_sum(scaled_grad, tokens, num_segments=VOCAB)
    small = lax.psum(
        (first_gain_grad, first_shift_grad, second_norm[0], second_norm[1], mean_part, table_sum),
        ("dp", "head", "seq"),
    )
    table_rows = lax.dynamic_slice_in_dim(small[5], seq_index * shard_rows, shard_rows)
    table_wide = table.astype(F32)
    row_norms = jnp.sqrt(jnp.sum(table_wide * table_wide, axis=1))
    table_grad = table_rows + small[4] / VOCAB * table_wide / row_norms[:, None]
    return (
        activation,
        embed_grad,
        table_grad,
        shards[0],
        shards[1],
        shards[2],
        small[0],
        small[1],
        shards[3],
        shards[4],
        shards[5],
        shards[6],
        small[2],
        small[3],
        shards[7],
        shards[8],
    )


def solution(mesh):
    tokens = P(("dp", "head", "seq"))
    wide = P(("dp", "head", "seq"), None)
    group = P("dp", None)
    return jax.shard_map(
        body,
        mesh=mesh,
        in_specs=(tokens, tokens, group, group, P("seq", None)) + (P(),) * 13 + (wide,),
        out_specs=(wide, wide, P("seq", None), group, group, group, P(), P())
        + (group,) * 4
        + (P(), P(), group, group),
        check_vma=False,
    )
```
